32 devices in a mesh: dp: 8 (over z, y), seq: 4 (over x, core).
Axes of the slice: x: 2, y: 2, z: 4, core: 2. Of those that a mesh axis runs over, the one named last changes fastest.
Arguments:
- tokens: bfloat16 [64, 512, 768], P('dp', 'seq'), may hold values from -8 to 8
- cotangent: bfloat16 [64, 512, 768], P('dp', 'seq'), may hold values from -6 to 6
- token_weight: float32 [64, 512], P('dp', 'seq'), may hold values from 0.25 to 2
- lengths: int32 [64], P('dp'), may hold values from 1 to 512, as said below
- qkv_master: float32 [768, 2304], P(('dp', 'seq')), may hold values from -1 to 1
- out_master: float32 [768, 768], P(('dp', 'seq')), may hold values from -0.625 to 0.625
- up_master: float32 [768, 3072], P(('dp', 'seq')), may hold values from -1 to 1
- down_master: float32 [3072, 768], P(('dp', 'seq')), may hold values from -0.109375 to 0.109375
- vec_master: float32 [9216], P(('dp', 'seq')), may hold values from -3 to 3
- qkv_first: float32 [768, 2304], P(('dp', 'seq')), may hold values from -0.00024414062 to 0.00024414062
- out_first: float32 [768, 768], P(('dp', 'seq')), may hold values from -0.00024414062 to 0.00024414062
- up_first: float32 [768, 3072], P(('dp', 'seq')), may hold values from -0.00024414062 to 0.00024414062
- down_first: float32 [3072, 768], P(('dp', 'seq')), may hold values from -0.00024414062 to 0.00024414062
- vec_first: float32 [9216], P(('dp', 'seq')), may hold values from -0.0007324219 to 0.0007324219
- qkv_second: float32 [768, 2304], P(('dp', 'seq')), may hold values from 7.0550676e-11 to 1.1288108e-09
- out_second: float32 [768, 768], P(('dp', 'seq')), may hold values from 7.0550676e-11 to 1.1288108e-09
- up_second: float32 [768, 3072], P(('dp', 'seq')), may hold values from 7.0550676e-11 to 1.1288108e-09
- down_second: float32 [3072, 768], P(('dp', 'seq')), may hold values from 7.0550676e-11 to 1.1288108e-09
- vec_second: float32 [9216], P(('dp', 'seq')), may hold values from 6.349561e-10 to 1.0159297e-08
Outputs:
- block_out: bfloat16 [64, 512, 768], P('dp', 'seq')
- input_grad: bfloat16 [64, 512, 768], P('dp', 'seq')
- grad_norm: float32 [], replicated
- qkv_new: float32 [768, 2304], P(('dp', 'seq'))
- qkv_first_new: float32 [768, 2304], P(('dp', 'seq'))
- qkv_second_new: float32 [768, 2304], P(('dp', 'seq'))
- qkv_copy: bfloat16 [768, 2304], P(('dp', 'seq'))
- out_new: float32 [768, 768], P(('dp', 'seq'))
- out_first_new: float32 [768, 768], P(('dp', 'seq'))
- out_second_new: float32 [768, 768], P(('dp', 'seq'))
- out_copy: bfloat16 [768, 768], P(('dp', 'seq'))
- up_new: float32 [768, 3072], P(('dp', 'seq'))
- up_first_new: float32 [768, 3072], P(('dp', 'seq'))
- up_second_new: float32 [768, 3072], P(('dp', 'seq'))
- up_copy: bfloat16 [768, 3072], P(('dp', 'seq'))
- down_new: float32 [3072, 768], P(('dp', 'seq'))
- down_first_new: float32 [3072, 768], P(('dp', 'seq'))
- down_second_new: float32 [3072, 768], P(('dp', 'seq'))
- down_copy: bfloat16 [3072, 768], P(('dp', 'seq'))
- vec_new: float32 [9216], P(('dp', 'seq'))
- vec_first_new: float32 [9216], P(('dp', 'seq'))
- vec_second_new: float32 [9216], P(('dp', 'seq'))
- vec_copy: bfloat16 [9216], P(('dp', 'seq'))
The draws below stay inside these ranges and needn't reach their ends.
Inputs may be any that keep to these rules, and one draw needn't show every extreme that they name: Each index of dp holds 8 rows, and one of them, chosen at random, has length 512; the other lengths are mostly short.
All inputs are finite; a program needn't handle non-finite values.
Results may differ from the reference program's by a relative error of at most 0.012.
Values may be sent and summed in bfloat16 or wider, within the bound.
A program may use at most 192 MiB of HBM per device.

```python
import math
from functools import partial
import jax
import jax.numpy as jnp
from jax import lax

D = 768
HEADS = 12
HEAD_DIM = 64
FF = 3072
SEQ_LEN = 512
ROWS_DEV = 8
STEP_COUNT = 10
ROWS = 64
VEC_LEN = 9216
PARAMS = 7087104


def ramp_scale(count, low_end, ratio):
    return low_end * ratio ** (jnp.arange(count, dtype=jnp.float32) / (count - 1))


def clipped_normal(key, shape):
    return jnp.clip(jax.random.normal(key, shape, jnp.float32), -4.0, 4.0)


def draw_tokens(key, part):
    key = jax.random.fold_in(key, 3)
    shape = (ROWS, SEQ_LEN, D)
    base = clipped_normal(key, shape)
    column_scale = ramp_scale(D, 0.6, 3.0)
    return (base * column_scale).astype(jnp.bfloat16)


def draw_lengths(key, part):
    key = jax.random.fold_in(key, 5)
    key_one, key_two, key_pick = jax.random.split(key, 3)
    first_draw = jax.random.randint(key_one, (ROWS,), 1, SEQ_LEN + 1)
    second_draw = jax.random.randint(key_two, (ROWS,), 1, SEQ_LEN + 1)
    shorter = jnp.minimum(first_draw, second_draw)
    chosen = jax.random.randint(key_pick, (ROWS // ROWS_DEV,), 0, ROWS_DEV)
    full_row = jnp.arange(ROWS) % ROWS_DEV == jnp.repeat(chosen, ROWS_DEV)
    return jnp.where(full_row, SEQ_LEN, shorter).astype(jnp.int32)


def draw_qkv_master(key, part):
    key = jax.random.fold_in(key, 7)
    shape = (D, 3 * D)
    base = clipped_normal(key, shape)
    value_scale = ramp_scale(D, 0.6, 3.0)
    column_scale = jnp.concatenate([jnp.ones((2 * D,), jnp.float32), value_scale])
    return base * column_scale / jnp.sqrt(jnp.float32(D))


def draw_up_master(key, part):
    key = jax.random.fold_in(key, 9)
    shape = (D, FF)
    base = clipped_normal(key, shape)
    column_scale = ramp_scale(FF, 0.5, 3.0)
    return base * column_scale / jnp.sqrt(jnp.float32(D))


def draw_vec_master(key, part):
    key = jax.random.fold_in(key, 11)
    key_bias, key_one, key_two = jax.random.split(key, 3)
    total = 8 * D + FF
    biases = 0.3 * clipped_normal(key_bias, (total,))
    gain_one = ramp_scale(D, 0.6, 3.0) * jax.random.uniform(key_one, (D,), jnp.float32, 0.85, 1.15)
    gain_two = jax.random.uniform(key_two, (D,), jnp.float32, 0.7, 1.3)
    return jnp.concatenate([biases[:3 * D], gain_one, biases[4 * D:6 * D + FF], gain_two, biases[7 * D + FF:]])


def shard_levels(own_key, dims, shards, low, top_value):
    def one(axis_at, blocks):
        steps = jax.random.uniform(jax.random.fold_in(jax.random.fold_in(own_key, 6), axis_at), (blocks,), jnp.float32, low / len(shards), top_value / len(shards))
        return jnp.repeat(jnp.exp(steps), dims[axis_at] // blocks).reshape((-1,) + (1,) * (len(dims) - axis_at - 1))

    factor_of = one(*shards[0])
    for cut in shards[1:]:
        factor_of = factor_of * one(*cut)
    return factor_of


def normal_values(rng, shape, deviation, bound, cuts=(), kind=jnp.bfloat16):
    factor_of = shard_levels(rng, shape, cuts, -0.22, 0.18) if cuts else 1.0
    entries = jax.random.normal(rng, shape, jnp.float32) * deviation * factor_of
    return jnp.minimum(jnp.maximum(entries, -bound), bound).astype(kind)


def setup_inputs(seed: int = 0) -> dict:
    key_list = jax.random.split(jax.random.key(seed), 20)
    tokens = draw_tokens(jax.random.fold_in(key_list[19], 71), 0)
    cotangent = normal_values(key_list[1], (ROWS, SEQ_LEN, D), 1.0, 6.0, ((0, 8), (1, 4)))
    token_weight = jnp.clip(0.25 + 1.75 * jax.random.uniform(key_list[2], (ROWS, SEQ_LEN), jnp.float32) ** shard_levels(key_list[2], (ROWS, SEQ_LEN), ((0, 8), (1, 4)), -0.2, 0.2), 0.25, 2.0)
    lengths = draw_lengths(jax.random.fold_in(key_list[19], 71), 0)
    qkv_master = draw_qkv_master(jax.random.fold_in(key_list[19], 71), 0)
    out_master = normal_values(key_list[5], (D, D), (D // 8) ** -0.5, 0.625, ((0, 32),), jnp.float32)
    up_master = draw_up_master(jax.random.fold_in(key_list[19], 71), 0)
    down_master = normal_values(key_list[7], (FF, D), FF ** -0.5, 0.109375, ((0, 32),), jnp.float32)
    vec_master = draw_vec_master(jax.random.fold_in(key_list[19], 71), 0)
    qkv_first = normal_values(key_list[9], (D, 3 * D), (0.11 / PARAMS ** 0.5), 0.00024414062, ((0, 32),), jnp.float32)
    out_first = normal_values(key_list[10], (D, D), (0.11 / PARAMS ** 0.5), 0.00024414062, ((0, 32),), jnp.float32)
    up_first = normal_values(key_list[11], (D, FF), (0.11 / PARAMS ** 0.5), 0.00024414062, ((0, 32),), jnp.float32)
    down_first = normal_values(key_list[12], (FF, D), (0.11 / PARAMS ** 0.5), 0.00024414062, ((0, 32),), jnp.float32)
    vec_first = normal_values(key_list[13], (VEC_LEN,), (0.33 / PARAMS ** 0.5), 0.0007324219, ((0, 32),), jnp.float32)
    qkv_second = jnp.clip(jnp.exp(math.log(1.1288108225926408e-09) - 2.7725887 * jax.random.uniform(key_list[14], (D, 3 * D), jnp.float32) ** shard_levels(key_list[14], (D, 3 * D), ((0, 32),), -0.2, 0.2)), 7.055067641204005e-11, 1.1288108225926408e-09)
    out_second = jnp.clip(jnp.exp(math.log(1.1288108225926408e-09) - 2.7725887 * jax.random.uniform(key_list[15], (D, D), jnp.float32) ** shard_levels(key_list[15], (D, D), ((0, 32),), -0.2, 0.2)), 7.055067641204005e-11, 1.1288108225926408e-09)
    up_second = jnp.clip(jnp.exp(math.log(1.1288108225926408e-09) - 2.7725887 * jax.random.uniform(key_list[16], (D, FF), jnp.float32) ** shard_levels(key_list[16], (D, FF), ((0, 32),), -0.2, 0.2)), 7.055067641204005e-11, 1.1288108225926408e-09)
    down_second = jnp.clip(jnp.exp(math.log(1.1288108225926408e-09) - 2.7725887 * jax.random.uniform(key_list[17], (FF, D), jnp.float32) ** shard_levels(key_list[17], (FF, D), ((0, 32),), -0.2, 0.2)), 7.055067641204005e-11, 1.1288108225926408e-09)
    vec_second = jnp.clip(jnp.exp(math.log(1.0159297403333767e-08) - 2.7725887 * jax.random.uniform(key_list[18], (VEC_LEN,), jnp.float32) ** shard_levels(key_list[18], (VEC_LEN,), ((0, 32),), -0.2, 0.2)), 6.349560877083604e-10, 1.0159297403333767e-08)
    return {"tokens": tokens, "cotangent": cotangent, "token_weight": token_weight, "lengths": lengths, "qkv_master": qkv_master, "out_master": out_master, "up_master": up_master, "down_master": down_master, "vec_master": vec_master, "qkv_first": qkv_first, "out_first": out_first, "up_first": up_first, "down_first": down_first, "vec_first": vec_first, "qkv_second": qkv_second, "out_second": out_second, "up_second": up_second, "down_second": down_second, "vec_second": vec_second}


@jax.custom_vjp
def low(v):
    return lax.optimization_barrier(v.astype(jnp.bfloat16)).astype(jnp.float32)

@jax.custom_vjp
def low_back(v):
    return v

def low_keep(v):
    return (low(v), None)

def low_pass(kept, grad):
    return (grad,)

def back_keep(v):
    return (v, None)

def back_low(kept, grad):
    return (low(grad),)
low.defvjp(low_keep, low_pass)
low_back.defvjp(back_keep, back_low)
CLIP_NORM = 1.0
BETA_ONE = 0.9
BETA_TWO = 0.999
LEARN_RATE = 0.05
VEC_RATE = 0.3
WEIGHT_DECAY = 0.01
ADAM_EPS = 1e-08
NORM_EPS = 1e-05
MASK_FILL = -1e+30
PRECISE = lax.Precision.HIGHEST

def unpack(vector):
    return (vector[:D], vector[D:2 * D], vector[2 * D:3 * D], vector[3 * D:4 * D], vector[4 * D:5 * D], vector[5 * D:5 * D + FF], vector[5 * D + FF:6 * D + FF], vector[6 * D + FF:7 * D + FF], vector[7 * D + FF:8 * D + FF])

def normalize(hidden, gain_vec, shift_vec):
    centre = hidden - lax.optimization_barrier(jnp.mean(hidden, axis=-1, keepdims=True))
    inverse = lax.rsqrt(lax.optimization_barrier(jnp.mean(centre * centre, axis=-1, keepdims=True)) + NORM_EPS)
    return centre * inverse * gain_vec + shift_vec

def attend(packed):
    queries, key_rows, value_rows, row_length = packed
    scale = 1.0 / math.sqrt(HEAD_DIM)
    scores = low_back(scale * jnp.einsum('qhd,khd->hqk', queries, key_rows, precision=PRECISE))
    key_mask = jnp.arange(SEQ_LEN, dtype=jnp.int32) < row_length
    scores = jnp.where(key_mask[None, None, :], scores, MASK_FILL)
    row_peak = lax.optimization_barrier(jnp.max(scores, axis=-1, keepdims=True))
    row_exp = jnp.exp(scores - row_peak)
    attn_probs = row_exp / lax.optimization_barrier(jnp.sum(row_exp, axis=-1, keepdims=True))
    mixed_rows = jnp.einsum('hqk,khd->qhd', low(attn_probs), value_rows, precision=PRECISE)
    return low_back(low(mixed_rows))

def forward(tokens_f, qkv_m, out_m, up_m, down_m, vec_m, lengths):
    qkv_w = low(qkv_m)
    out_w = low(out_m)
    up_w = low(up_m)
    down_w = low(down_m)
    bias_q, bias_v, bias_o, gain_one, shift_one, bias_up, bias_down, gain_two, shift_two = unpack(low(vec_m))
    flat_tokens = tokens_f.reshape(ROWS * SEQ_LEN, D)
    merged = jnp.dot(flat_tokens, qkv_w, precision=PRECISE, preferred_element_type=jnp.float32)
    merged = merged + jnp.concatenate([bias_q, jnp.zeros((D,), jnp.float32), bias_v])
    merged = low_back(low(merged)).reshape(ROWS, SEQ_LEN, 3, HEADS, HEAD_DIM)
    mixed = lax.map(jax.checkpoint(attend), (merged[:, :, 0], merged[:, :, 1], merged[:, :, 2], lengths))
    mixed_flat = mixed.reshape(ROWS * SEQ_LEN, D)
    attn_out = low_back(jnp.dot(mixed_flat, out_w, precision=PRECISE, preferred_element_type=jnp.float32) + bias_o)
    first_out = normalize(flat_tokens + attn_out, gain_one, shift_one)
    pre_act = low_back(jnp.dot(low(first_out), up_w, precision=PRECISE, preferred_element_type=jnp.float32) + bias_up)
    act_low = low(jax.nn.gelu(pre_act, approximate=False))
    branch = low_back(jnp.dot(act_low, down_w, precision=PRECISE, preferred_element_type=jnp.float32) + bias_down)
    return normalize(first_out + branch, gain_two, shift_two)

def adam_step(master, gradient, moment_one, second, factor, decay_rate, step_rate):
    clipped = gradient * factor
    first_new = BETA_ONE * moment_one + (1.0 - BETA_ONE) * clipped
    second_new = BETA_TWO * second + (1.0 - BETA_TWO) * clipped * clipped
    first_hat = first_new / (1.0 - BETA_ONE ** STEP_COUNT)
    second_hat = second_new / (1.0 - BETA_TWO ** STEP_COUNT)
    updated = master - step_rate * (first_hat / (jnp.sqrt(second_hat) + ADAM_EPS) + decay_rate * master)
    return (updated, first_new, second_new, updated.astype(jnp.bfloat16))

def reference(tokens, cotangent, token_weight, lengths, qkv_master, out_master, up_master, down_master, vec_master, qkv_first, out_first, up_first, down_first, vec_first, qkv_second, out_second, up_second, down_second, vec_second):
    tokens_f = tokens.astype(jnp.float32)
    token_mask = (jnp.arange(SEQ_LEN, dtype=jnp.int32)[None, :] < lengths[:, None]).astype(jnp.float32)
    grad_result = cotangent.astype(jnp.float32) * (token_weight * token_mask)[:, :, None]
    result, pullback = jax.vjp(partial(forward, lengths=lengths), tokens_f, qkv_master, out_master, up_master, down_master, vec_master)
    grads = pullback(grad_result.reshape(ROWS * SEQ_LEN, D))
    squares = jnp.sum(grads[1] * grads[1]) + jnp.sum(grads[2] * grads[2]) + jnp.sum(grads[3] * grads[3])
    squares = squares + jnp.sum(grads[4] * grads[4]) + jnp.sum(grads[5] * grads[5])
    norm_value = jnp.sqrt(squares)
    factor = CLIP_NORM / jnp.maximum(norm_value, CLIP_NORM)
    qkv_up = adam_step(qkv_master, grads[1], qkv_first, qkv_second, factor, WEIGHT_DECAY, LEARN_RATE)
    out_up = adam_step(out_master, grads[2], out_first, out_second, factor, WEIGHT_DECAY, LEARN_RATE)
    ffn_up = adam_step(up_master, grads[3], up_first, up_second, factor, WEIGHT_DECAY, LEARN_RATE)
    down_up = adam_step(down_master, grads[4], down_first, down_second, factor, WEIGHT_DECAY, LEARN_RATE)
    vec_up = adam_step(vec_master, grads[5], vec_first, vec_second, factor, 0.0, VEC_RATE)
    block_out = result.astype(jnp.bfloat16).reshape(ROWS, SEQ_LEN, D)
    input_grad = grads[0].astype(jnp.bfloat16).reshape(ROWS, SEQ_LEN, D)
    return (block_out, input_grad, norm_value, qkv_up[0], qkv_up[1], qkv_up[2], qkv_up[3], out_up[0], out_up[1], out_up[2], out_up[3], ffn_up[0], ffn_up[1], ffn_up[2], ffn_up[3], down_up[0], down_up[1], down_up[2], down_up[3], vec_up[0], vec_up[1], vec_up[2], vec_up[3])
```

```python
import functools
import math

import jax
import jax.numpy as jnp
from jax import lax
from jax.experimental import pallas as pl
from jax.experimental.pallas import tpu as pltpu
from jax.sharding import PartitionSpec as P

D = 768
HEADS = 12
HEAD_DIM = 64
FF = 3072
STEP_COUNT = 10
CLIP_NORM = 1.0
BETA_ONE = 0.9
BETA_TWO = 0.999
LEARN_RATE = 0.05
VEC_RATE = 0.3
WEIGHT_DECAY = 0.01
ADAM_EPS = 1e-08
NORM_EPS = 1e-05
MASK_FILL = -1e30
MESH = pl.DeviceIdType.MESH
F32 = jnp.float32
BF16 = jnp.bfloat16
VMEM_LIMIT = 60 << 20


class Place:
    def __init__(self):
        self.ndp, self.nsq = lax.axis_size("dp"), lax.axis_size("seq")
        self.dp, self.sq = lax.axis_index("dp"), lax.axis_index("seq")
        self.z, self.y = self.dp // 2, self.dp % 2
        self.x, self.c = self.sq // 2, self.sq % 2
        self.nz = self.ndp // 2
        self.core = (self.dp, self.x * 2 + 1 - self.c)
        self.across_x = (self.dp, (1 - self.x) * 2 + self.c)
        self.across_y = (self.z * 2 + 1 - self.y, self.sq)

    def along_z(self, k):
        return (self.z + k) % self.nz

    def at_z(self, z):
        return (z * 2 + self.y, self.sq)


def greet(targets):
    barrier = pltpu.get_barrier_semaphore()
    for target in targets:
        pl.semaphore_signal(barrier, inc=1, device_id=target, device_id_type=MESH)
    pl.semaphore_wait(barrier, len(targets))


class Sems:
    def __init__(self, send, recv, local):
        self.send, self.recv, self.local = send, recv, local
        self.n = self.m = 0

    def remote(self, src, dst, target):
        i = self.n
        self.n += 1
        return pltpu.make_async_remote_copy(
            src_ref=src,
            dst_ref=dst,
            send_sem=self.send.at[i],
            recv_sem=self.recv.at[i],
            device_id=target,
            device_id_type=MESH,
        )

    def here(self, src, dst):
        i = self.m
        self.m += 1
        return pltpu.make_async_copy(src, dst, self.local.at[i])


def begin(copies):
    for copy in copies:
        copy.start()


def finish(copies):
    for copy in copies:
        copy.wait()


class Gather:
    def __init__(self, place, sems, at, own, x_first):
        p = place
        whole = slice(None)
        mine = at(p.z, p.y, p.x)
        self.stages = [
            [sems.here(own, mine)]
            + [sems.remote(own, mine, p.at_z(p.along_z(k))) for k in range(1, p.nz)]
        ]
        line = at(whole, p.y, p.x)
        if x_first:
            plane, hops = at(whole, p.y, whole), (p.across_x, p.across_y)
        else:
            plane, hops = at(whole, whole, p.x), (p.across_y, p.across_x)
        everything = at(whole, whole, whole)
        self.stages.append([sems.remote(line, line, hops[0])])
        self.stages.append([sems.remote(plane, plane, hops[1])])
        self.stages.append([sems.remote(everything, everything, p.core)])


def pipeline(items):
    depth = len(items[0].stages)

    def step(t):
        for s in reversed(range(depth)):
            i = t - s
            if 0 <= i < len(items):
                if s:
                    finish(items[i].stages[s - 1])
                begin(items[i].stages[s])
        i = t - depth
        if 0 <= i < len(items):
            finish(items[i].stages[depth - 1])

    return [functools.partial(step, t) for t in range(len(items) + depth)]


def tokens_to_rows(place, sems, src, dst, here):
    p = place
    part, length = dst.shape[0], src.shape[1]
    spot = dst.at[:, pl.ds(p.sq * length, length)]
    copies = [sems.here(src.at[pl.ds(p.sq * part, part)], spot)]
    for k in range(1, p.nsq):
        to = (p.sq + k) % p.nsq
        copies.append(sems.remote(src.at[pl.ds(to * part, part)], spot, (p.dp, to)))
    return copies


def rows_to_tokens(place, sems, src, dst):
    p = place
    part, length = src.shape[0], dst.shape[1]
    spot = dst.at[pl.ds(p.sq * part, part)]
    copies = [sems.here(src.at[:, pl.ds(p.sq * length, length)], spot)]
    for k in range(1, p.nsq):
        to = (p.sq + k) % p.nsq
        copies.append(sems.remote(src.at[:, pl.ds(to * length, length)], spot, (p.dp, to)))
    return copies


PIECES = {
    "qkv": ((0, 640, True), (640, 512, False)),
    "out": ((0, 384, True),),
    "up": ((0, 768, True), (768, 768, False)),
}


def gather_kernel(
    tokens, cotangent, weight, qkv_m, out_m, up_m, down_m, vec_m,
    x_rows, cot_rows, weight_all, qkv_w, out_w, up_w, down_w, vec_w,
    qkv_f, out_f, up_f, down_f, qkv_b, out_b, up_b, down_b, send, recv, local,
):
    p = Place()
    greet([p.core, p.across_x, p.across_y, (p.dp, 3 - p.sq)] + [p.at_z(p.along_z(k)) for k in range(1, p.nz)])
    sems = Sems(send, recv, local)
    move_tokens = tokens_to_rows(p, sems, tokens, x_rows, True)
    move_cot = tokens_to_rows(p, sems, cotangent, cot_rows, True)
    spot = weight_all.at[p.sq]
    move_weight = [sems.here(weight, spot)] + [
        sems.remote(weight, spot, (p.dp, (p.sq + k) % p.nsq)) for k in range(1, p.nsq)
    ]
    masters = {"qkv": (qkv_m, qkv_f, qkv_b, qkv_w), "out": (out_m, out_f, out_b, out_w), "up": (up_m, up_f, up_b, up_w)}
    rows = qkv_m.shape[0]
    mine = pl.ds(p.c * rows, rows)
    halves = {}
    for name, (master, wide, _, _) in masters.items():
        half = wide.shape[1]
        halves[name] = [
            sems.here(master.at[:, pl.ds(p.c * half, half)], wide.at[mine]),
            sems.remote(master.at[:, pl.ds((1 - p.c) * half, half)], wide.at[mine], p.core),
        ]
    load_down = [sems.here(down_m, down_f)]
    items = {}
    for name, (_, wide, low, whole) in masters.items():
        half = wide.shape[1]
        for offset, width, x_first in PIECES[name]:

            def at(z, y, x, whole=whole, half=half, offset=offset, width=width):
                return whole.at[z, y, x, :, pl.ds(p.c * half + offset, width)]

            items[name, offset] = Gather(p, sems, at, low.at[:, pl.ds(offset, width)], x_first)
    items["vec"] = Gather(p, sems, lambda z, y, x: vec_w.at[z, y, x, p.c], vec_m, False)
    items["down"] = Gather(p, sems, lambda z, y, x: down_w.at[z, y, x, p.c], down_b, True)

    begin(halves["qkv"])
    begin(move_tokens)
    begin(halves["out"])
    begin(halves["up"])
    begin(load_down)
    begin(move_weight)
    for name, (_, wide, low, _) in masters.items():
        finish(halves[name])
        low[...] = wide[...].astype(BF16)
    finish(load_down)
    down_b[...] = down_f[...].astype(BF16)
    order = [("qkv", 0), ("qkv", 640), "vec", ("out", 0), ("up", 0), ("up", 768), "down"]
    steps = pipeline([items[key] for key in order])
    for t, step in enumerate(steps):
        step()
        if t == 4:
            begin(move_cot)
    finish(move_tokens + move_cot + move_weight)


def gather_weights(tokens, cotangent, weight, qkv_m, out_m, up_m, down_m, vec_m):
    ndp, nsq = lax.axis_size("dp"), lax.axis_size("seq")
    rows, length, width = tokens.shape
    part, full = rows // nsq, length * nsq
    chip, low = 2 * qkv_m.shape[0], down_m.shape[0]
    grid = (ndp // 2, 2, nsq // 2)
    any_space = pl.BlockSpec(memory_space=pl.ANY)
    shapes = [
        jax.ShapeDtypeStruct((part, full, width), BF16),
        jax.ShapeDtypeStruct((part, full, width), BF16),
        jax.ShapeDtypeStruct((nsq,) + weight.shape, F32),
    ]
    shapes += [jax.ShapeDtypeStruct(grid + (chip, m.shape[1]), BF16) for m in (qkv_m, out_m, up_m)]
    shapes += [
        jax.ShapeDtypeStruct(grid + (2, low, down_m.shape[1]), BF16),
        jax.ShapeDtypeStruct(grid + (2,) + vec_m.shape, F32),
    ]
    half = [m.shape[1] // 2 for m in (qkv_m, out_m, up_m)]
    return pl.pallas_call(
        gather_kernel,
        out_shape=shapes,
        in_specs=[any_space] * 8,
        out_specs=[any_space] * 8,
        scratch_shapes=[pltpu.VMEM((chip, h), F32) for h in half]
        + [pltpu.VMEM(down_m.shape, F32)]
        + [pltpu.VMEM((chip, h), BF16) for h in half]
        + [pltpu.VMEM(down_m.shape, BF16)]
        + [pltpu.SemaphoreType.DMA((64,)), pltpu.SemaphoreType.DMA((64,)), pltpu.SemaphoreType.DMA((24,))],
        compiler_params=pltpu.CompilerParams(
            collective_id=1, has_side_effects=True, vmem_limit_bytes=VMEM_LIMIT
        ),
    )(tokens, cotangent, weight, qkv_m, out_m, up_m, down_m, vec_m)


def add_into(total, extra, lead):
    count = math.prod(lead)

    def one(i, carry):
        spot = []
        for size in reversed(lead):
            spot.insert(0, i % size)
            i = i // size
        spot = tuple(spot)
        total[spot] = (total[spot].astype(F32) + extra[spot].astype(F32)).astype(total.dtype)
        return carry

    lax.fori_loop(0, count, one, 0)


class Scatter:
    def __init__(self, place, sems, at, bufs, x_first):
        p = place
        total, near, first, second, along, final = bufs
        nz = p.nz
        self.stages = [
            [
                sems.here(at(p.c), total),
                sems.remote(at(1 - p.c), near, p.core),
            ]
        ]
        if x_first:
            self.stages.append([sems.remote(total.at[:, :, 1 - p.x], first, p.across_x)])
            kept = total.at[:, :, p.x]
            self.stages.append([sems.remote(total.at[:, 1 - p.y, p.x], second, p.across_y)])
        else:
            self.stages.append([sems.remote(total.at[:, 1 - p.y], first, p.across_y)])
            kept = total.at[:, p.y]
            self.stages.append([sems.remote(total.at[:, p.y, 1 - p.x], second, p.across_x)])
        line = total.at[:, p.y, p.x]
        self.stages.append(
            [
                sems.remote(total.at[p.along_z(k), p.y, p.x], along.at[k - 1], p.at_z(p.along_z(k)))
                for k in range(1, nz)
            ]
        )

        def close():
            value = total[p.z, p.y, p.x].astype(F32)
            for k in range(1, nz):
                value = value + along[k - 1].astype(F32)
            final[...] = value

        self.after = [
            lambda: add_into(total, near, (nz, 2, 2)),
            lambda: add_into(kept, first, (nz, 2)),
            lambda: add_into(line, second, (nz,)),
            close,
        ]


def scatter_pipeline(items):
    depth = 4

    def step(t):
        for s in reversed(range(depth + 1)):
            i = t - s
            if 0 <= i < len(items):
                if s:
                    finish(items[i].stages[s - 1])
                    items[i].after[s - 1]()
                if s < depth:
                    begin(items[i].stages[s])

    return [functools.partial(step, t) for t in range(len(items) + depth)]


def scatter_scratch(block, nz, dtype):
    return [
        pltpu.VMEM((nz, 2, 2) + block, dtype),
        pltpu.VMEM((nz, 2, 2) + block, dtype),
        pltpu.VMEM((nz, 2) + block, dtype),
        pltpu.VMEM((nz,) + block, dtype),
        pltpu.VMEM((nz - 1,) + block, dtype),
        pltpu.VMEM(block, F32),
    ]


def scatter_kernel(
    block_rows, grad_rows, qkv_g, out_g, up_g, down_g, vec_g,
    block_out, input_grad, qkv_s, out_s, up_s, down_s, vec_s, norm,
    *scratch,
):
    send, recv, local, near_sum, far_sum = scratch[-5:]
    p = Place()
    greet(
        [(p.dp, (p.sq + k) % p.nsq) for k in range(1, p.nsq)]
        + [((p.dp + k) % p.ndp, p.sq) for k in range(1, p.ndp)]
    )
    sems = Sems(send, recv, local)
    move_out = rows_to_tokens(p, sems, block_rows, block_out)
    move_grad = rows_to_tokens(p, sems, grad_rows, input_grad)
    arrays = {"qkv": (qkv_g, qkv_s), "out": (out_g, out_s), "up": (up_g, up_s)}
    items, last, finals = {}, [], []
    pool = list(scratch[:-5])
    for name, (grad, shard) in arrays.items():
        half = grad.shape[-1] // 2
        for offset, width, x_first in PIECES[name]:
            bufs, pool = pool[:6], pool[6:]

            def at(core, grad=grad, half=half, offset=offset, width=width):
                return grad.at[:, :, :, :, pl.ds(core * half + offset, width)]

            items[name, offset] = Scatter(p, sems, at, bufs, not x_first)
            final = bufs[5]
            rows = final.shape[0] // 2
            spot = shard.at[:, pl.ds(p.c * half + offset, width)]
            last += [
                sems.here(final.at[pl.ds(p.c * rows, rows)], spot),
                sems.remote(final.at[pl.ds((1 - p.c) * rows, rows)], spot, p.core),
            ]
            finals.append(final)
    for name, grad, shard in (("vec", vec_g, vec_s), ("down", down_g, down_s)):
        bufs, pool = pool[:6], pool[6:]
        items[name] = Scatter(p, sems, lambda core, grad=grad: grad.at[:, :, :, core], bufs, name == "vec")
        last.append(sems.here(bufs[5], shard))
        finals.append(bufs[5])
    order = ["down", ("up", 0), ("up", 768), ("out", 0), ("qkv", 0), ("qkv", 640), "vec"]
    for t, step in enumerate(scatter_pipeline([items[key] for key in order])):
        step()
        if t == 0:
            begin(move_out)
        if t == 2:
            begin(move_grad)
    begin(last)
    part = jnp.zeros((1, 1), F32)
    for final in finals:
        value = final[...]
        part = part + jnp.sum(jnp.sum(value * value, axis=0, keepdims=True), axis=1, keepdims=True)
    near_sum[p.sq] = jnp.broadcast_to(part, near_sum.shape[1:])
    spread = [
        sems.remote(near_sum.at[p.sq], near_sum.at[p.sq], (p.dp, (p.sq + k) % p.nsq)) for k in range(1, p.nsq)
    ]
    begin(spread)
    finish(spread)
    part = near_sum[0]
    for k in range(1, p.nsq):
        part = part + near_sum[k]
    far_sum[p.dp] = part
    spread = [
        sems.remote(far_sum.at[p.dp], far_sum.at[p.dp], ((p.dp + k) % p.ndp, p.sq)) for k in range(1, p.ndp)
    ]
    begin(spread)
    finish(spread)
    part = far_sum[0]
    for k in range(1, p.ndp):
        part = part + far_sum[k]
    norm[...] = jnp.sqrt(part)
    finish(last + move_out + move_grad)


def scatter_grads(block_rows, grad_rows, qkv_g, out_g, up_g, down_g, vec_g):
    ndp, nsq = lax.axis_size("dp"), lax.axis_size("seq")
    nz = ndp // 2
    part, full, width = block_rows.shape
    token_shape = (part * nsq, full // nsq, width)
    any_space = pl.BlockSpec(memory_space=pl.ANY)
    grid = (nz, 2, nsq // 2)
    rows = D // (ndp * nsq)
    low = FF // (ndp * nsq)
    vec_block = vec_g.shape[-2:]
    shapes = [jax.ShapeDtypeStruct(token_shape, BF16)] * 2
    shapes += [jax.ShapeDtypeStruct((rows, g.shape[1]), F32) for g in (qkv_g, out_g, up_g)]
    shapes += [
        jax.ShapeDtypeStruct((low, D), F32),
        jax.ShapeDtypeStruct(vec_block, F32),
        jax.ShapeDtypeStruct((8, 128), F32),
    ]
    scratch = []
    for name in ("qkv", "out", "up"):
        for _, piece, _ in PIECES[name]:
            scratch += scatter_scratch((2 * rows, piece), nz, BF16)
    scratch += scatter_scratch(vec_block, nz, F32)
    scratch += scatter_scratch((low, D), nz, BF16)
    scratch += [pltpu.SemaphoreType.DMA((80,)), pltpu.SemaphoreType.DMA((80,)), pltpu.SemaphoreType.DMA((24,))]
    scratch += [pltpu.VMEM((nsq, 8, 128), F32), pltpu.VMEM((ndp, 8, 128), F32)]
    return pl.pallas_call(
        scatter_kernel,
        out_shape=shapes,
        in_specs=[any_space] * 7,
        out_specs=[any_space] * 7 + [pl.BlockSpec(memory_space=pltpu.VMEM)],
        scratch_shapes=scratch,
        compiler_params=pltpu.CompilerParams(
            collective_id=2, has_side_effects=True, vmem_limit_bytes=VMEM_LIMIT
        ),
    )(
        block_rows,
        grad_rows,
        qkv_g.reshape(grid + (2 * rows, qkv_g.shape[1])),
        out_g.reshape(grid + (2 * rows, out_g.shape[1])),
        up_g.reshape(grid + (2 * rows, up_g.shape[1])),
        down_g.reshape(grid + (2, low, D)),
        vec_g.reshape(grid + (2,) + vec_block),
    )


def pad_vec(vector, count):
    size = vector.shape[0] // count
    wide = 96 if size % 96 == 0 else size
    parts = vector.astype(F32).reshape(count, size // wide, wide)
    return jnp.pad(parts, ((0, 0), (0, 8 - size // wide), (0, 128 - wide)))


def unpad_vec(parts, size):
    wide = 96 if size % 96 == 0 else size
    return parts[:, : size // wide, :wide].reshape(-1)


def unpack(vector):
    return (
        vector[:D],
        vector[D : 2 * D],
        vector[2 * D : 3 * D],
        vector[3 * D : 4 * D],
        vector[4 * D : 5 * D],
        vector[5 * D : 5 * D + FF],
        vector[5 * D + FF : 6 * D + FF],
        vector[6 * D + FF : 7 * D + FF],
        vector[7 * D + FF : 8 * D + FF],
    )


def normalize(hidden, gain_vec, shift_vec):
    centre = hidden - jnp.mean(hidden, axis=-1, keepdims=True)
    inverse = lax.rsqrt(jnp.mean(centre * centre, axis=-1, keepdims=True) + NORM_EPS)
    normed = centre * inverse
    return (normed * gain_vec + shift_vec, normed, inverse)


def normalize_back(grad_out, normed, inverse, gain_vec):
    scaled = grad_out * gain_vec
    centred = scaled - jnp.mean(scaled, axis=-1, keepdims=True)
    return inverse * (centred - normed * jnp.mean(scaled * normed, axis=-1, keepdims=True))


def gelu_exact(values):
    return jax.nn.gelu(values, approximate=False)


def split_parts(packed_rows):
    full_len = packed_rows.shape[0]
    group_count = packed_rows.shape[-1] // (3 * HEAD_DIM)
    parts = packed_rows.reshape(full_len, 3, group_count, HEAD_DIM)
    return (parts[:, 0], parts[:, 1], parts[:, 2])


def row_probs(queries, key_rows, key_mask):
    scale = 1.0 / math.sqrt(HEAD_DIM)
    scores = jnp.einsum("qhd,khd->hqk", queries, key_rows, preferred_element_type=F32) * scale
    scores = jnp.where(key_mask[None, None, :], scores, MASK_FILL)
    row_peak = jnp.max(scores, axis=-1, keepdims=True)
    row_exp = jnp.exp(scores - row_peak)
    return row_exp / jnp.sum(row_exp, axis=-1, keepdims=True)


def attend_row(packed):
    packed_rows, key_mask = packed
    queries, key_rows, value_rows = split_parts(packed_rows)
    attn_probs = row_probs(queries, key_rows, key_mask)
    mixed_rows = jnp.einsum("hqk,khd->qhd", attn_probs.astype(BF16), value_rows, preferred_element_type=F32)
    return mixed_rows.astype(BF16).reshape(packed_rows.shape[0], D)


def attend_back(packed):
    packed_rows, grad_rows, key_mask = packed
    full_len = packed_rows.shape[0]
    queries, key_rows, value_rows = split_parts(packed_rows)
    grad_mixed = grad_rows.reshape(full_len, HEADS, HEAD_DIM)
    attn_probs = row_probs(queries, key_rows, key_mask)
    grad_probs = jnp.einsum("qhd,khd->hqk", grad_mixed, value_rows, preferred_element_type=F32)
    row_delta = jnp.sum(attn_probs * grad_probs, axis=-1, keepdims=True)
    grad_scores = (attn_probs * (grad_probs - row_delta)).astype(BF16)
    scale = 1.0 / math.sqrt(HEAD_DIM)
    grad_query = jnp.einsum("hqk,khd->qhd", grad_scores, key_rows, preferred_element_type=F32) * scale
    grad_key = jnp.einsum("hqk,qhd->khd", grad_scores, queries, preferred_element_type=F32) * scale
    grad_value = jnp.einsum("hqk,qhd->khd", attn_probs.astype(BF16), grad_mixed, preferred_element_type=F32)
    stacked = jnp.stack([grad_query, grad_key, grad_value], axis=1).astype(BF16)
    return stacked.reshape(full_len, 3 * D)


def adam_step(master, gradient, moment_one, second, factor, decay_rate, step_rate):
    clipped = gradient * factor
    first_new = BETA_ONE * moment_one + (1.0 - BETA_ONE) * clipped
    second_new = BETA_TWO * second + (1.0 - BETA_TWO) * clipped * clipped
    first_hat = first_new / (1.0 - BETA_ONE**STEP_COUNT)
    second_hat = second_new / (1.0 - BETA_TWO**STEP_COUNT)
    updated = master - step_rate * (first_hat / (jnp.sqrt(second_hat) + ADAM_EPS) + decay_rate * master)
    return (updated, first_new, second_new, updated.astype(BF16))


def layer(rows_in, cot_in, token_weight, lengths, qkv_w, out_w, up_w, down_w, vec_w):
    row_count, full_len, width_d = rows_in.shape
    token_count = row_count * full_len
    bias_q, bias_v, bias_o, gain_one, shift_one, bias_up, bias_down, gain_two, shift_two = unpack(vec_w)
    key_mask = jnp.arange(full_len, dtype=jnp.int32)[None, :] < lengths[:, None]
    flat = rows_in.reshape(token_count, width_d)
    merged = jnp.dot(flat, qkv_w, preferred_element_type=F32)
    merged = (merged + jnp.concatenate([bias_q, jnp.zeros_like(bias_q), bias_v])).astype(BF16)
    merged_rows = merged.reshape(row_count, full_len, 3 * width_d)
    mixed = lax.map(attend_row, (merged_rows, key_mask)).reshape(token_count, width_d)
    attn_out = jnp.dot(mixed, out_w, preferred_element_type=F32) + bias_o
    first_out, normed_one, inverse_one = normalize(flat.astype(F32) + attn_out, gain_one, shift_one)
    first_low = first_out.astype(BF16)
    pre_act = jnp.dot(first_low, up_w, preferred_element_type=F32) + bias_up
    activated, gelu_pull = jax.vjp(gelu_exact, pre_act)
    act_low = activated.astype(BF16)
    branch = jnp.dot(act_low, down_w, preferred_element_type=F32) + bias_down
    result, normed_two, inverse_two = normalize(first_out + branch, gain_two, shift_two)
    block_out = result.astype(BF16).reshape(row_count, full_len, width_d)
    grad_result = cot_in.astype(F32) * (token_weight * key_mask.astype(F32))[:, :, None]
    grad_result = grad_result.reshape(token_count, width_d)
    grad_gain_two = jnp.sum(grad_result * normed_two, axis=0)
    grad_shift_two = jnp.sum(grad_result, axis=0)
    grad_second = normalize_back(grad_result, normed_two, inverse_two, gain_two)
    grad_branch = grad_second.astype(BF16)
    grad_bias_down = jnp.sum(grad_branch, axis=0, dtype=F32)
    grad_down = jnp.einsum("tf,td->fd", act_low, grad_branch, preferred_element_type=F32)
    grad_act = jnp.einsum("td,fd->tf", grad_branch, down_w, preferred_element_type=F32)
    grad_pre = gelu_pull(grad_act)[0].astype(BF16)
    grad_bias_up = jnp.sum(grad_pre, axis=0, dtype=F32)
    grad_up = jnp.einsum("td,tf->df", first_low, grad_pre, preferred_element_type=F32)
    grad_first = grad_second + jnp.einsum("tf,df->td", grad_pre, up_w, preferred_element_type=F32)
    grad_gain_one = jnp.sum(grad_first * normed_one, axis=0)
    grad_shift_one = jnp.sum(grad_first, axis=0)
    grad_resid = normalize_back(grad_first, normed_one, inverse_one, gain_one)
    grad_attn = grad_resid.astype(BF16)
    grad_bias_o = jnp.sum(grad_attn, axis=0, dtype=F32)
    grad_out = jnp.einsum("td,te->de", mixed, grad_attn, preferred_element_type=F32)
    grad_mixed = jnp.einsum("te,de->td", grad_attn, out_w, preferred_element_type=F32).astype(BF16)
    grad_merged = lax.map(
        attend_back, (merged_rows, grad_mixed.reshape(row_count, full_len, width_d), key_mask)
    ).reshape(token_count, 3 * width_d)
    grad_qkv = jnp.einsum("td,te->de", flat, grad_merged, preferred_element_type=F32)
    column_sums = jnp.sum(grad_merged, axis=0, dtype=F32)
    input_grad = grad_resid + jnp.einsum("te,de->td", grad_merged, qkv_w, preferred_element_type=F32)
    input_grad = input_grad.astype(BF16).reshape(row_count, full_len, width_d)
    grad_vec = jnp.concatenate(
        [
            column_sums[:width_d],
            column_sums[2 * width_d :],
            grad_bias_o,
            grad_gain_one,
            grad_shift_one,
            grad_bias_up,
            grad_bias_down,
            grad_gain_two,
            grad_shift_two,
        ]
    )
    low = [g.astype(BF16) for g in (grad_qkv, grad_out, grad_up, grad_down)]
    return block_out, input_grad, *low, grad_vec


def body(
    tokens, cotangent, token_weight, lengths,
    qkv_master, out_master, up_master, down_master, vec_master,
    qkv_first, out_first, up_first, down_first, vec_first,
    qkv_second, out_second, up_second, down_second, vec_second,
):
    ndp, nsq = lax.axis_size("dp"), lax.axis_size("seq")
    devices = ndp * nsq
    row_count, local_len, width_d = tokens.shape
    full_len, part = local_len * nsq, row_count // nsq
    vec_size = vec_master.shape[0]
    sq = lax.axis_index("seq")
    my_lengths = lax.dynamic_slice_in_dim(lengths, sq * part, part)
    both = ("dp", "seq")
    own_kernels = qkv_master.shape[0] % 8 == 0 and down_master.shape[0] % 16 == 0 and nsq == 4 and ndp % 2 == 0
    low_vec = vec_master.astype(BF16)
    if own_kernels:
        rows_in, cot_in, weights, qkv_w, out_w, up_w, down_w, vec_w = gather_weights(
            tokens, cotangent, token_weight, qkv_master, out_master, up_master, down_master,
            pad_vec(low_vec, 1)[0],
        )
        qkv_w, out_w, up_w = (w.reshape(-1, w.shape[-1]) for w in (qkv_w, out_w, up_w))
        down_w = down_w.reshape(-1, down_w.shape[-1])
        vec_w = unpad_vec(vec_w.reshape(devices, 8, 128), vec_size)
    else:
        rows_in, cot_in = (
            lax.all_to_all(a, "seq", split_axis=0, concat_axis=1, tiled=True) for a in (tokens, cotangent)
        )
        weights = lax.all_gather(token_weight, "seq", axis=0)
        qkv_w, out_w, up_w, down_w = (
            lax.all_gather(m.astype(BF16), both, axis=0, tiled=True)
            for m in (qkv_master, out_master, up_master, down_master)
        )
        vec_w = lax.all_gather(low_vec, both, axis=0, tiled=True).astype(F32)
    my_weight = lax.dynamic_slice_in_dim(weights, sq * part, part, axis=1)
    my_weight = my_weight.transpose(1, 0, 2).reshape(part, full_len)
    block_rows, grad_rows, *grads, grad_vec = layer(
        rows_in, cot_in, my_weight, my_lengths, qkv_w, out_w, up_w, down_w, vec_w
    )
    if own_kernels:
        block_out, input_grad, *shards, vec_s, norm = scatter_grads(
            block_rows, grad_rows, *grads, pad_vec(grad_vec, devices)
        )
        shards.append(unpad_vec(vec_s[None], vec_size))
        norm_value = norm[0, 0]
    else:
        block_out, input_grad = (
            lax.all_to_all(a, "seq", split_axis=1, concat_axis=0, tiled=True) for a in (block_rows, grad_rows)
        )
        shards = [lax.psum_scatter(g.astype(F32), both, scatter_dimension=0, tiled=True) for g in grads]
        shards.append(lax.psum_scatter(grad_vec, both, scatter_dimension=0, tiled=True))
        norm_value = jnp.sqrt(lax.psum(sum(jnp.sum(s * s) for s in shards), both))
    factor = CLIP_NORM / jnp.maximum(norm_value, CLIP_NORM)
    outs = [block_out, input_grad, norm_value]
    for master, shard, first, second, decay, rate in (
        (qkv_master, shards[0], qkv_first, qkv_second, WEIGHT_DECAY, LEARN_RATE),
        (out_master, shards[1], out_first, out_second, WEIGHT_DECAY, LEARN_RATE),
        (up_master, shards[2], up_first, up_second, WEIGHT_DECAY, LEARN_RATE),
        (down_master, shards[3], down_first, down_second, WEIGHT_DECAY, LEARN_RATE),
        (vec_master, shards[4], vec_first, vec_second, 0.0, VEC_RATE),
    ):
        outs += adam_step(master, shard, first, second, factor, decay, rate)
    return tuple(outs)


def solution(mesh):
    tokens, both, flat = P("dp", "seq", None), P(("dp", "seq"), None), P(("dp", "seq"))
    weights = (both, both, both, both, flat)
    in_specs = (tokens, tokens, P("dp", "seq"), P("dp")) + 3 * weights
    out_specs = (tokens, tokens, P()) + 4 * (both,) * 4 + (flat,) * 4
    return jax.shard_map(body, mesh=mesh, in_specs=in_specs, out_specs=out_specs, check_vma=False)
```

```python
import functools
import math

import jax
import jax.numpy as jnp
from jax import lax
from jax.experimental import pallas as pl
from jax.experimental.pallas import tpu as pltpu
from jax.sharding import PartitionSpec as P

D = 768
HEADS = 12
HEAD_DIM = 64
FF = 3072
STEP_COUNT = 10
CLIP_NORM = 1.0
BETA_ONE = 0.9
BETA_TWO = 0.999
LEARN_RATE = 0.05
VEC_RATE = 0.3
WEIGHT_DECAY = 0.01
ADAM_EPS = 1e-08
NORM_EPS = 1e-05
MASK_FILL = -1e30
MESH = pl.DeviceIdType.MESH
F32 = jnp.float32
BF16 = jnp.bfloat16
VMEM_LIMIT = 62 << 20


class Place:
    def __init__(self):
        self.ndp, self.nsq = lax.axis_size("dp"), lax.axis_size("seq")
        self.dp, self.sq = lax.axis_index("dp"), lax.axis_index("seq")
        self.z, self.y = self.dp // 2, self.dp % 2
        self.x, self.c = self.sq // 2, self.sq % 2
        self.nz = self.ndp // 2
        self.core = (self.dp, self.x * 2 + 1 - self.c)
        self.across_x = (self.dp, (1 - self.x) * 2 + self.c)
        self.across_y = (self.z * 2 + 1 - self.y, self.sq)

    def along_z(self, k):
        return (self.z + k) % self.nz

    def at_z(self, z):
        return (z * 2 + self.y, self.sq)


def greet(targets):
    barrier = pltpu.get_barrier_semaphore()
    for target in targets:
        pl.semaphore_signal(barrier, inc=1, device_id=target, device_id_type=MESH)
    pl.semaphore_wait(barrier, len(targets))


class Sems:
    def __init__(self, send, recv, local):
        self.send, self.recv, self.local = send, recv, local
        self.n = self.m = 0

    def remote(self, src, dst, target):
        i = self.n
        self.n += 1
        return pltpu.make_async_remote_copy(
            src_ref=src,
            dst_ref=dst,
            send_sem=self.send.at[i],
            recv_sem=self.recv.at[i],
            device_id=target,
            device_id_type=MESH,
        )

    def here(self, src, dst):
        i = self.m
        self.m += 1
        return pltpu.make_async_copy(src, dst, self.local.at[i])


def begin(copies):
    for copy in copies:
        copy.start()


def finish(copies):
    for copy in copies:
        copy.wait()


class Gather:
    def __init__(self, place, sems, at, own, x_first):
        p = place
        whole = slice(None)
        mine = at(p.z, p.y, p.x)
        self.stages = [
            [sems.here(own, mine)]
            + [sems.remote(own, mine, p.at_z(p.along_z(k))) for k in range(1, p.nz)]
        ]
        line = at(whole, p.y, p.x)
        if x_first:
            plane, hops = at(whole, p.y, whole), (p.across_x, p.across_y)
        else:
            plane, hops = at(whole, whole, p.x), (p.across_y, p.across_x)
        everything = at(whole, whole, whole)
        self.stages.append([sems.remote(line, line, hops[0])])
        self.stages.append([sems.remote(plane, plane, hops[1])])
        self.stages.append([sems.remote(everything, everything, p.core)])


def pipeline(items):
    depth = len(items[0].stages)

    def step(t):
        for s in reversed(range(depth)):
            i = t - s
            if 0 <= i < len(items):
                if s:
                    finish(items[i].stages[s - 1])
                begin(items[i].stages[s])
        i = t - depth
        if 0 <= i < len(items):
            finish(items[i].stages[depth - 1])

    return [functools.partial(step, t) for t in range(len(items) + depth)]


def tokens_to_rows(place, sems, src, dst):
    p = place
    part, length = dst.shape[0], src.shape[1]
    spot = dst.at[:, pl.ds(p.sq * length, length)]
    copies = [sems.here(src.at[pl.ds(p.sq * part, part)], spot)]
    for k in range(1, p.nsq):
        to = (p.sq + k) % p.nsq
        copies.append(sems.remote(src.at[pl.ds(to * part, part)], spot, (p.dp, to)))
    return copies


def rows_to_tokens(place, sems, src, dst):
    p = place
    part, length = src.shape[0], dst.shape[1]
    spot = dst.at[pl.ds(p.sq * part, part)]
    copies = [sems.here(src.at[:, pl.ds(p.sq * length, length)], spot)]
    for k in range(1, p.nsq):
        to = (p.sq + k) % p.nsq
        copies.append(sems.remote(src.at[:, pl.ds(to * length, length)], spot, (p.dp, to)))
    return copies


PIECES = {
    "qkv": ((0, 640, True), (640, 512, False)),
    "out": ((0, 384, True),),
    "up": ((0, 768, True), (768, 768, False)),
    "down": ((0, 512, True), (512, 256, False)),
}
PAIRS = HEADS // 2
NT = (((1,), (1,)), ((), ()))
TN = (((0,), (0,)), ((), ()))
NN = (((1,), (0,)), ((), ()))
ERF_P = 0.3275911
ERF_B = (0.254829592, -0.284496736, 1.421413741, -1.453152027, 1.061405429)


def dot(a, b, dims=NN):
    return lax.dot_general(a, b, dims, preferred_element_type=F32)


def lanes(start, size):
    return pl.ds(pl.multiple_of(start, 128), size)


def mean(values):
    return jnp.sum(values, axis=-1, keepdims=True) * (1.0 / D)


def matrix(ref, *index):
    value = ref[index] if index else ref[...]
    return value.reshape(-1, value.shape[-1])


def columns(ref, cols):
    value = ref[:, :, :, :, cols]
    return value.reshape(-1, value.shape[-1])


def project(x, w, bias, merged, first, last, rows=512, cols=384):
    @pl.loop(first, last)
    def _(j):
        cs = lanes(j * cols, cols)
        part = columns(w, cs)
        for i in range(x.shape[0] // rows):
            rs = pl.ds(i * rows, rows)
            merged[rs, cs] = (dot(x[rs, :], part) + bias[0:1, cs]).astype(BF16)


def of_head(values, h):
    lane = lax.broadcasted_iota(jnp.int32, values.shape, 1)
    own = lane < HEAD_DIM if h == 0 else lane >= HEAD_DIM
    return jnp.where(own, values, jnp.zeros_like(values))


def attend(merged, key_bias, heads_out, lse, length, first, last):
    @pl.loop(first, last)
    def _(i):
        r, p = i // PAIRS, i % PAIRS
        rs = pl.ds(pl.multiple_of(r * length, 128), length)
        q2 = merged[rs, lanes(p * 128, 128)] * jnp.asarray(HEAD_DIM**-0.5, BF16)
        k2 = merged[rs, lanes(D + p * 128, 128)]
        v2t = merged[rs, lanes(2 * D + p * 128, 128)].T
        bias = key_bias[r]
        outs = []
        for h in range(2):
            scores = dot(of_head(k2, h), q2, NT) + bias
            peak = jnp.max(scores, axis=0, keepdims=True)
            weights = jnp.exp(scores - peak)
            total = jnp.sum(weights, axis=0, keepdims=True)
            outs.append(dot(v2t, weights.astype(BF16)) * (1.0 / total))
            lse[r, 2 * p + h] = peak + jnp.log(total)
        row = lax.broadcasted_iota(jnp.int32, outs[0].shape, 0)
        mixed = jnp.where(row < HEAD_DIM, outs[0], outs[1])
        heads_out[rs, lanes(p * 128, 128)] = mixed.T.astype(BF16)


def first_norm(x, heads_out, w, vec, normed, inverse, low, rows=256):
    @pl.loop(0, x.shape[0] // rows)
    def _(i):
        rs = pl.ds(pl.multiple_of(i * rows, rows), rows)
        hidden = x[rs, :].astype(F32) + (dot(heads_out[rs, :], matrix(w)) + vec[0:1, 2 * D : 3 * D])
        centre = hidden - mean(hidden)
        scale = lax.rsqrt(mean(centre * centre) + NORM_EPS)
        unit = centre * scale
        normed[rs, :] = unit
        inverse[rs, :] = scale
        low[rs, :] = (unit * vec[0:1, 3 * D : 4 * D] + vec[0:1, 4 * D : 5 * D]).astype(BF16)


def normal_cdf_pdf(x):
    t = 1.0 / (1.0 + (ERF_P * 0.5**0.5) * jnp.abs(x))
    bell = jnp.exp(-0.5 * (x * x))
    tail = 0.5 * ERF_B[4]
    for b in ERF_B[3::-1]:
        tail = tail * t + 0.5 * b
    tail = tail * t * bell
    return jnp.where(x >= 0, 1.0 - tail, tail), bell * (2 * math.pi) ** -0.5


class FeedForward:
    def __init__(self, low, up_w, vec, down_w, act, slope, branch, pre):
        self.__dict__.update(locals())
        self.n = down_w.shape[0]
        self.cols = FF // self.n
        self.rows = min(512, low.shape[0])

    def up(self, j, rs):
        cs = pl.ds(j * self.cols, self.cols)
        bias = self.vec[0:1, 5 * D + j * self.cols : 5 * D + (j + 1) * self.cols]
        self.pre[j % 2, rs, :] = dot(self.low[rs, :], columns(self.up_w, cs)) + bias

    def gelu(self, j, start):
        cs = pl.ds(j * self.cols, self.cols)
        step = 64
        for k in range(self.rows // step):
            rs = pl.ds(pl.multiple_of(start + k * step, step), step)
            value = self.pre[j % 2, rs, :]
            cdf, pdf = normal_cdf_pdf(value)
            self.act[rs, cs] = (value * cdf).astype(BF16)
            self.slope[rs, cs] = (cdf + value * pdf).astype(self.slope.dtype)

    def down(self, j, rs):
        cs = pl.ds(j * self.cols, self.cols)
        value = dot(self.act[rs, cs], matrix(self.down_w, j))
        self.branch[rs, :] = value if j == 0 else self.branch[rs, :] + value

    def step(self, j):
        @pl.loop(0, self.low.shape[0] // self.rows)
        def _(i):
            start = pl.multiple_of(i * self.rows, self.rows)
            rs = pl.ds(start, self.rows)
            if j + 1 < self.n:
                self.up(j + 1, rs)
            if 0 <= j < self.n:
                self.gelu(j, start)
            if 0 <= j - 1:
                self.down(j - 1, rs)


def second_norm(normed, vec, branch, cot, weight, block_out, grad_branch, sums, rows=128):
    sums[...] = jnp.zeros_like(sums)
    at = 5 * D + FF
    gain_one, shift_one, bias_down = (vec[0:1, s : s + D] for s in (3 * D, 4 * D, at))
    gain_two, shift_two = (vec[0:1, s : s + D] for s in (at + D, at + 2 * D))

    @pl.loop(0, normed.shape[0] // rows)
    def _(i):
        rs = pl.ds(pl.multiple_of(i * rows, rows), rows)
        hidden = normed[rs, :] * gain_one + shift_one + (branch[rs, :] + bias_down)
        centre = hidden - mean(hidden)
        scale = lax.rsqrt(mean(centre * centre) + NORM_EPS)
        unit = centre * scale
        block_out[rs, :] = (unit * gain_two + shift_two).astype(BF16)
        grad = cot[rs, :].astype(F32) * weight[rs, 0:1]
        sums[1:2, :] += jnp.sum(grad * unit, axis=0, keepdims=True)
        sums[2:3, :] += jnp.sum(grad, axis=0, keepdims=True)
        scaled = grad * gain_two
        second = scale * (scaled - mean(scaled) - unit * mean(scaled * unit))
        normed[rs, :] = second
        low = second.astype(BF16)
        grad_branch[rs, :] = low
        sums[0:1, :] += jnp.sum(low.astype(F32), axis=0, keepdims=True)


def forward_kernel(
    tokens, cotangent, weight, qkv_m, out_m, up_m, down_m, vec_m, key_bias,
    x_out, qkv_w, out_w, up_w, down_w, vec_out, merged_out, heads_out, lse_out, normed_out, inverse_out,
    low_out, act_out, slope_out, block_out, second_out, branch_out, sums_out,
    qkv_f, out_f, up_f, down_f, qkv_b, out_b, up_b, down_b,
    qkv_v, out_v, up_v, down_v, x, cot, wt, vec_near, vec_far, vec, bias, merged, heads, lse, normed, inverse,
    low, act, slope, branch, pre, grad_branch, sums, send, recv, local,
):
    p = Place()
    greet(
        [(p.dp, (p.sq + k) % p.nsq) for k in range(1, p.nsq)]
        + [((p.dp + k) % p.ndp, p.sq) for k in range(1, p.ndp)]
    )
    sems = Sems(send, recv, local)
    part, length = x.shape[0], x.shape[1]
    move_tokens = tokens_to_rows(p, sems, tokens, x)
    move_cot = tokens_to_rows(p, sems, cotangent, cot)
    move_weight = tokens_to_rows(p, sems, weight, wt)
    masters = {
        "qkv": (qkv_m, qkv_f, qkv_b, qkv_w),
        "out": (out_m, out_f, out_b, out_w),
        "up": (up_m, up_f, up_b, up_w),
    }
    rows = qkv_m.shape[0]
    mine = pl.ds(p.c * rows, rows)
    halves = {}
    for name, (master, wide, _, _) in masters.items():
        half = wide.shape[1]
        halves[name] = [
            sems.here(master.at[:, pl.ds(p.c * half, half)], wide.at[mine]),
            sems.remote(master.at[:, pl.ds((1 - p.c) * half, half)], wide.at[mine], p.core),
        ]
    load_down = [sems.here(down_m, down_f)]
    groups = {}
    for name, (_, wide, narrow, whole) in masters.items():
        half = wide.shape[1]
        groups[name] = []
        for offset, width, x_first in PIECES[name]:

            def at(z, y, x, whole=whole, half=half, offset=offset, width=width):
                return whole.at[z, y, x, :, pl.ds(p.c * half + offset, width)]

            groups[name].append(Gather(p, sems, at, narrow.at[:, pl.ds(offset, width)], x_first))
    groups["down"] = []
    for offset, width, x_first in PIECES["down"]:

        def at(z, y, x, offset=offset, width=width):
            return down_w.at[z, y, x, p.c, :, pl.ds(offset, width)]

        groups["down"].append(Gather(p, sems, at, down_b.at[:, pl.ds(offset, width)], x_first))
    load = {
        "qkv": [sems.here(qkv_w, qkv_v)],
        "out": [sems.here(out_w, out_v)],
        "up": [sems.here(up_w, up_v)],
        "down": [sems.here(down_w, down_v)],
    }
    near = vec_near.at[p.sq]
    vec_one = [sems.remote(near, near, (p.dp, (p.sq + k) % p.nsq)) for k in range(1, p.nsq)]
    far = vec_far.at[p.dp]
    vec_two = [sems.remote(far, far, ((p.dp + k) % p.ndp, p.sq)) for k in range(1, p.ndp)]

    def advance(name, stage):
        for item in groups[name]:
            if stage:
                finish(item.stages[stage - 1])
            if stage < 4:
                begin(item.stages[stage])

    begin(halves["qkv"])
    vec_near[p.sq] = vec_m[...].astype(BF16).astype(F32)
    begin(vec_one)
    begin(load_down)
    begin(halves["out"])
    begin(halves["up"])
    finish(halves["qkv"])
    qkv_b[...] = qkv_f[...].astype(BF16)
    advance("qkv", 0)
    begin(move_tokens)
    for name in ("out", "up"):
        finish(halves[name])
        masters[name][2][...] = masters[name][1][...].astype(BF16)
    finish(load_down)
    down_b[...] = down_f[...].astype(BF16)
    finish(vec_one)
    block = vec_near[0]
    for k in range(1, p.nsq):
        block = block + vec_near[k]
    vec_far[p.dp] = block
    begin(vec_two)
    advance("qkv", 1)
    advance("out", 0)
    advance("up", 0)
    advance("qkv", 2)
    advance("down", 0)
    advance("qkv", 3)
    advance("out", 1)
    advance("up", 1)
    finish(vec_two)
    tiles = vec.shape[1] // (128 * p.ndp)
    for d in range(p.ndp):
        for k in range(tiles):
            vec[0:1, pl.ds((d * tiles + k) * 128, 128)] = vec_far[d, k : k + 1, :]
    bias[0:1, 0:D] = vec[0:1, 0:D]
    bias[0:1, D : 2 * D] = jnp.zeros((1, D), F32)
    bias[0:1, 2 * D :] = vec[0:1, D : 2 * D]
    advance("qkv", 4)
    begin(load["qkv"])
    finish(move_tokens)
    keep = [sems.here(x, x_out)]
    finish(load["qkv"])
    flat = x.reshape(part * length, D)
    begin(keep)
    project(flat, qkv_v, bias, merged, 0, 3)
    advance("out", 2)
    advance("up", 2)
    advance("down", 1)
    project(flat, qkv_v, bias, merged, 3, 6)
    keep.append(sems.here(merged, merged_out))
    keep[-1].start()
    attend(merged, key_bias, heads, lse, length, 0, PAIRS)
    advance("out", 3)
    attend(merged, key_bias, heads, lse, length, PAIRS, 2 * PAIRS - 3)
    advance("out", 4)
    begin(load["out"])
    advance("up", 3)
    advance("down", 2)
    attend(merged, key_bias, heads, lse, length, 2 * PAIRS - 3, 2 * PAIRS)
    keep += [sems.here(heads, heads_out), sems.here(lse, lse_out)]
    begin(keep[-2:])
    advance("up", 4)
    begin(load["up"])
    begin(move_cot)
    begin(move_weight)
    finish(load["out"])
    first_norm(flat, heads, out_v, vec, normed, inverse, low)
    keep += [sems.here(normed, normed_out), sems.here(inverse, inverse_out), sems.here(low, low_out)]
    begin(keep[-3:])
    finish(load["up"])
    ffn = FeedForward(low, up_v, vec, down_v, act, slope, branch, pre)
    ffn.step(-1)
    advance("down", 3)
    ffn.step(0)
    advance("down", 4)
    begin(load["down"])
    finish(load["down"])
    for j in range(1, ffn.n + 1):
        ffn.step(j)
    keep += [sems.here(act, act_out), sems.here(slope, slope_out)]
    begin(keep[-2:])
    finish(move_cot + move_weight)
    finish(keep[2:3] + keep[4:5])
    second_norm(
        normed, vec, branch, cot.reshape(part * length, D), wt.reshape(part * length, 128), heads, grad_branch, sums
    )
    ends = [
        sems.here(heads, block_out),
        sems.here(normed, second_out),
        sems.here(grad_branch, branch_out),
        sems.here(sums, sums_out),
        sems.here(vec, vec_out),
    ]
    begin(ends)
    finish(keep[:2] + keep[3:4] + keep[5:] + ends)


def forward(tokens, cotangent, weight, qkv_m, out_m, up_m, down_m, vec_m, key_bias):
    ndp, nsq = lax.axis_size("dp"), lax.axis_size("seq")
    rows, length, width = tokens.shape
    part, full = rows // nsq, length * nsq
    count = part * full
    chip, low = 2 * qkv_m.shape[0], down_m.shape[0]
    grid = (ndp // 2, 2, nsq // 2)
    vec_len = 8 * D + FF
    any_space = pl.BlockSpec(memory_space=pl.ANY)
    vmem = pl.BlockSpec(memory_space=pltpu.VMEM)

    def both(shape, dtype):
        return jax.ShapeDtypeStruct(shape, dtype), pltpu.VMEM(shape, dtype)

    weights = [both(grid + (chip, m.shape[1]), BF16) for m in (qkv_m, out_m, up_m)]
    weights.append(both(grid + (2, low, width), BF16))
    x = both((part, full, width), BF16)
    vec = both((1, vec_len), F32)
    merged = both((count, 3 * width), BF16)
    heads = both((count, width), BF16)
    lse = both((part, HEADS, 1, full), F32)
    normed = both((count, width), F32)
    inverse = both((count, 1), F32)
    act = both((count, FF), BF16)
    sums = both((8, width), F32)
    half = [m.shape[1] // 2 for m in (qkv_m, out_m, up_m)]
    outs = [x[0]] + [w[0] for w in weights] + [vec[0], merged[0], heads[0], lse[0], normed[0], inverse[0]]
    outs += [heads[0], act[0], act[0], heads[0], normed[0], heads[0], sums[0]]
    scratch = [pltpu.VMEM((chip, h), F32) for h in half] + [pltpu.VMEM(down_m.shape, F32)]
    scratch += [pltpu.VMEM((chip, h), BF16) for h in half] + [pltpu.VMEM(down_m.shape, BF16)]
    scratch += [w[1] for w in weights]
    scratch += [x[1], x[1], pltpu.VMEM((part, full, 128), F32)]
    scratch += [pltpu.VMEM((nsq,) + vec_m.shape, F32), pltpu.VMEM((ndp,) + vec_m.shape, F32), vec[1]]
    scratch += [pltpu.VMEM((1, 3 * width), F32), merged[1], heads[1], lse[1], normed[1], inverse[1]]
    scratch += [heads[1], act[1], act[1], normed[1], pltpu.VMEM((2, count, FF // grid[0]), F32), heads[1], sums[1]]
    scratch += [pltpu.SemaphoreType.DMA((72,)), pltpu.SemaphoreType.DMA((72,)), pltpu.SemaphoreType.DMA((48,))]
    return pl.pallas_call(
        forward_kernel,
        out_shape=outs,
        in_specs=[any_space] * 7 + [vmem] * 2,
        out_specs=[any_space] * len(outs),
        scratch_shapes=scratch,
        compiler_params=pltpu.CompilerParams(
            collective_id=1, has_side_effects=True, vmem_limit_bytes=VMEM_LIMIT
        ),
    )(tokens, cotangent, weight, qkv_m, out_m, up_m, down_m, vec_m, key_bias)


class Scatter:
    def __init__(self, place, sems, at, near, bufs, x_first):
        p = place
        first, second, along, final = bufs
        nz = p.nz
        total = at(p.c)
        self.final = final
        self.stages = [[sems.remote(at(1 - p.c), near, p.core)]]
        if x_first:
            kept = total.at[:, :, p.x]
            self.stages.append([sems.remote(total.at[:, :, 1 - p.x], first, p.across_x)])
            self.stages.append([sems.remote(total.at[:, 1 - p.y, p.x], second, p.across_y)])
        else:
            kept = total.at[:, p.y]
            self.stages.append([sems.remote(total.at[:, 1 - p.y], first, p.across_y)])
            self.stages.append([sems.remote(total.at[:, p.y, 1 - p.x], second, p.across_x)])
        line = total.at[:, p.y, p.x]
        self.stages.append(
            [
                sems.remote(total.at[p.along_z(k), p.y, p.x], along.at[k - 1], p.at_z(p.along_z(k)))
                for k in range(1, nz)
            ]
        )

        def close():
            value = total[p.z, p.y, p.x].astype(F32)
            for k in range(1, nz):
                value = value + along[k - 1].astype(F32)
            final[...] = value

        self.after = [
            lambda: add_into(total, near, (nz, 2, 2)),
            lambda: add_into(kept, first, (nz, 2)),
            lambda: add_into(line, second, (nz,)),
            close,
        ]


def add_into(total, extra, lead):
    def one(i, carry):
        spot = []
        for size in reversed(lead):
            spot.insert(0, i % size)
            i = i // size
        spot = tuple(spot)
        total[spot] = (total[spot].astype(F32) + extra[spot].astype(F32)).astype(total.dtype)
        return carry

    lax.fori_loop(0, math.prod(lead), one, 0)


def feed_back_down(j, grad_branch, down_w, act, slope, grad_down, vec_sum, rows=512):
    n = grad_down.shape[0]
    cols = FF // n
    cs = pl.ds(j * cols, cols)
    weight = matrix(down_w, j)

    total = None
    for i in range(slope.shape[0] // rows):
        rs = pl.ds(i * rows, rows)
        grad = dot(grad_branch[rs, :], weight, NT) * slope[rs, cs].astype(F32)
        low = grad.astype(BF16)
        slope[rs, cs] = low
        part = jnp.sum(low.astype(F32), axis=0, keepdims=True)
        total = part if total is None else total + part
    vec_sum[0:1, 5 * D + j * cols : 5 * D + (j + 1) * cols] = total
    value = dot(columns(act, cs), grad_branch[...], TN)
    grad_down[j] = value.astype(BF16).reshape(grad_down.shape[1:])


def feed_back_up(j, low_t, grad_pre, up_w, grad_first, grad_up, rows=512):
    n = grad_up.shape[0]
    cols = FF // n
    cs = pl.ds(j * cols, cols)
    value = dot(low_t[...], grad_pre[:, cs])
    grad_up[:, :, :, :, cs] = value.astype(BF16).reshape(grad_up.shape[:4] + (cols,))
    weight = columns(up_w, cs)
    for i in range(grad_pre.shape[0] // rows):
        rs = pl.ds(i * rows, rows)
        grad_first[rs, :] += dot(grad_pre[rs, cs], weight, NT)


def first_norm_back(grad_first, normed, inverse, vec, grad_attn, vec_sum, rows=128):
    vec_sum[0:1, 2 * D : 5 * D] = jnp.zeros((1, 3 * D), F32)

    @pl.loop(0, normed.shape[0] // rows)
    def _(i):
        rs = pl.ds(pl.multiple_of(i * rows, rows), rows)
        grad, unit = grad_first[rs, :], normed[rs, :]
        vec_sum[0:1, 3 * D : 4 * D] += jnp.sum(grad * unit, axis=0, keepdims=True)
        vec_sum[0:1, 4 * D : 5 * D] += jnp.sum(grad, axis=0, keepdims=True)
        scaled = grad * vec[0:1, 3 * D : 4 * D]
        resid = inverse[rs, :] * (scaled - mean(scaled) - unit * mean(scaled * unit))
        grad_first[rs, :] = resid
        low = resid.astype(BF16)
        grad_attn[rs, :] = low
        vec_sum[0:1, 2 * D : 3 * D] += jnp.sum(low.astype(F32), axis=0, keepdims=True)


def attend_back(merged, grad_heads, key_bias, lse, grad_merged, length, first, last):
    per_row = merged.shape[0] // (grad_heads.shape[0] // length)

    @pl.loop(first, last)
    def _(i):
        r, p = i // PAIRS, i % PAIRS
        rs = pl.ds(pl.multiple_of(r * length, 128), length)
        zs = pl.ds(r * per_row, per_row)

        def piece(start):
            return merged[zs, :, :, :, lanes(start + p * 128, 128)].reshape(length, 128)

        q2 = piece(0) * jnp.asarray(HEAD_DIM**-0.5, BF16)
        k2, v2 = piece(D), piece(2 * D)
        out2 = grad_heads[rs, lanes(p * 128, 128)]
        k2t = k2.T
        bias = key_bias[r]
        queries, keys, values = [], [], []
        for h in range(2):
            scores = dot(of_head(k2, h), q2, NT) + bias
            probs = jnp.exp(scores - lse[r, 2 * p + h])
            grad_probs = dot(of_head(v2, h), out2, NT)
            weighted = probs * grad_probs
            delta = jnp.sum(weighted, axis=0, keepdims=True)
            grad_scores = (weighted - probs * delta).astype(BF16)
            queries.append(dot(k2t, grad_scores))
            keys.append(dot(grad_scores, q2))
            values.append(dot(probs.astype(BF16), out2))
        row = lax.broadcasted_iota(jnp.int32, queries[0].shape, 0)
        grad_q = jnp.where(row < HEAD_DIM, queries[0], queries[1]) * HEAD_DIM**-0.5
        lane = lax.broadcasted_iota(jnp.int32, keys[0].shape, 1)
        grad_merged[rs, lanes(p * 128, 128)] = grad_q.T.astype(BF16)
        grad_merged[rs, lanes(D + p * 128, 128)] = jnp.where(lane < HEAD_DIM, *keys).astype(BF16)
        grad_merged[rs, lanes(2 * D + p * 128, 128)] = jnp.where(lane < HEAD_DIM, *values).astype(BF16)


def project_back(x, grad_merged, grad_qkv, vec_sum, bias_sum, cols=384):
    lead = grad_qkv.shape[:4]

    @pl.loop(0, 3 * D // cols)
    def _(j):
        cs = lanes(j * cols, cols)
        grad = grad_merged[:, cs]
        bias_sum[0:1, cs] = jnp.sum(grad.astype(F32), axis=0, keepdims=True)
        grad_qkv[:, :, :, :, cs] = dot(x[...], grad, TN).astype(BF16).reshape(lead + (cols,))

    vec_sum[0:1, 0:D] = bias_sum[0:1, 0:D]
    vec_sum[0:1, D : 2 * D] = bias_sum[0:1, 2 * D :]


def backward_kernel(
    x_in, qkv_w, out_w, up_w, down_w, vec_in, merged_in, heads_in, lse_in, normed_in, inverse_in,
    low_in, act_in, slope_in, block_rows, second_in, branch_in, sums_in, key_bias,
    block_out, input_grad, qkv_s, out_s, up_s, down_s, vec_s, norm,
    up_v, down_v, out_v, act, slope, grad_branch, grad_first, low, low_t, x, normed, inverse, lse, vec, sums,
    grad_down, grad_up, grad_out, vec_sum, bias_sum, vec_parts, vec_recv, vec_near, near_sum, far_sum,
    down_near, out_near, *rest,
):
    send, recv, local, free = rest[-4:]
    pool = list(rest[:-4])
    p = Place()
    greet(
        [(p.dp, (p.sq + k) % p.nsq) for k in range(1, p.nsq)]
        + [((p.dp + k) % p.ndp, p.sq) for k in range(1, p.ndp)]
    )
    sems = Sems(send, recv, local)
    length = x_in.shape[1]
    n = down_v.shape[0]
    chunk = FF // n
    wide = 3 * D
    load_one = [sems.here(branch_in, grad_branch), sems.here(low_in, low)]
    load_chunk = [
        [
            sems.here(down_w.at[j], down_v.at[j]),
            sems.here(slope_in.at[:, pl.ds(j * chunk, chunk)], slope.at[:, pl.ds(j * chunk, chunk)]),
            sems.here(act_in.at[:, :, :, :, pl.ds(j * chunk, chunk)], act.at[:, :, :, :, pl.ds(j * chunk, chunk)]),
        ]
        for j in range(n)
    ]
    load_two = [sems.here(up_w, up_v), sems.here(second_in, grad_first), sems.here(sums_in, sums)]
    load_three = [
        sems.here(normed_in, normed),
        sems.here(inverse_in, inverse),
        sems.here(vec_in, vec),
        sems.here(out_w, out_v),
        sems.here(lse_in, lse),
        sems.here(x_in, x),
    ]
    load_merged = [sems.here(merged_in, act.at[:, :, :, :, pl.ds(0, wide)])]
    load_heads = [sems.here(heads_in, grad_branch)]
    load_qkv = [sems.here(qkv_w, up_v.at[:, :, :, :, pl.ds(0, wide)])]
    move_out = rows_to_tokens(p, sems, block_rows, block_out)
    grad_rows = grad_branch
    move_grad = rows_to_tokens(p, sems, grad_rows.reshape(x.shape), input_grad)

    rows = out_v.shape[3]
    grad_qkv = act.at[:, :, :, pl.ds(0, rows), pl.ds(0, wide)]
    groups = {name: [] for name in PIECES}
    for i, (offset, width, x_first) in enumerate(PIECES["down"]):
        near = down_near.at[:, :, :, :, pl.ds(offset, width)]

        def at(core, offset=offset, width=width):
            return grad_down.at[:, :, :, core, :, pl.ds(offset, width)]

        groups["down"].append(Scatter(p, sems, at, near, pool[:4], not x_first))
        pool = pool[4:]
    for name, grad, half, slot in (("up", grad_up, FF // 2, 0), ("out", grad_out, D // 2, None), ("qkv", act, wide // 2, 1)):
        for i, (offset, width, x_first) in enumerate(PIECES[name]):
            if slot is None:
                near = out_near
            else:
                near = down_v.at[:, :, :, slot, pl.ds(i * rows, rows), pl.ds(0, width)]

            def at(core, grad=grad, half=half, offset=offset, width=width):
                return grad.at[:, :, :, pl.ds(0, rows), lanes(core * half + offset, width)]

            groups[name].append(Scatter(p, sems, at, near, pool[:4], not x_first))
            pool = pool[4:]
    last = []
    for name, shard in (("qkv", qkv_s), ("out", out_s), ("up", up_s)):
        half = shard.shape[1] // 2
        for (offset, width, _), item in zip(PIECES[name], groups[name]):
            own = rows // 2
            spot = shard.at[:, lanes(p.c * half + offset, width)]
            last += [
                sems.here(item.final.at[pl.ds(p.c * own, own)], spot),
                sems.remote(item.final.at[pl.ds((1 - p.c) * own, own)], spot, p.core),
            ]
    for (offset, width, _), item in zip(PIECES["down"], groups["down"]):
        last.append(sems.here(item.final, down_s.at[:, pl.ds(offset, width)]))

    def advance(name, stage):
        for item in groups[name]:
            if stage:
                finish(item.stages[stage - 1])
                item.after[stage - 1]()
            if stage < 4:
                begin(item.stages[stage])

    begin(load_one)
    for part in load_chunk:
        begin(part)
    begin(load_two)
    begin(move_out)
    begin(load_three)
    finish(load_one)
    low_t[...] = low[...].T
    for j in range(n):
        finish(load_chunk[j])
        feed_back_down(j, grad_branch, down_v, act, slope, grad_down, vec_sum)
    advance("down", 0)
    pl.semaphore_signal(free, inc=1, device_id=p.core, device_id_type=MESH)
    begin(load_merged)
    begin(load_heads)
    finish(load_two)
    for j in range(n):
        feed_back_up(j, low_t, slope, up_v, grad_first, grad_up)
        if j == 1:
            advance("down", 1)
    pl.semaphore_wait(free, 1)
    advance("up", 0)
    begin(load_qkv)
    finish(load_three)
    grad_attn = low
    first_norm_back(grad_first, normed, inverse, vec, grad_attn, vec_sum)
    advance("up", 1)
    advance("down", 2)
    finish(load_heads)
    grad_out[...] = dot(grad_branch[...], grad_attn[...], TN).astype(BF16).reshape(grad_out.shape)
    advance("out", 0)
    grad_heads = grad_branch
    for i in range(grad_attn.shape[0] // 512):
        rs = pl.ds(i * 512, 512)
        grad_heads[rs, :] = dot(grad_attn[rs, :], matrix(out_v), NT).astype(BF16)
    finish(load_merged)
    attend_back(act, grad_heads, key_bias, lse, slope, length, 0, 4)
    advance("down", 3)
    advance("up", 2)
    advance("out", 1)
    attend_back(act, grad_heads, key_bias, lse, slope, length, 4, 8)
    advance("down", 4)
    advance("up", 3)
    advance("out", 2)
    attend_back(act, grad_heads, key_bias, lse, slope, length, 8, 12)
    advance("up", 4)
    advance("out", 3)
    project_back(matrix(x), slope, grad_qkv, vec_sum, bias_sum)
    advance("qkv", 0)
    vec_sum[0:1, 5 * D + FF :] = jnp.zeros((1, 3 * D), F32)
    for k in range(3):
        vec_sum[0:1, 5 * D + FF + k * D : 5 * D + FF + (k + 1) * D] = sums[k : k + 1, :]
    tiles = vec_sum.shape[1] // (128 * p.ndp)
    for d in range(p.ndp):
        for k in range(tiles):
            vec_parts[d, k : k + 1, :] = vec_sum[0:1, pl.ds((d * tiles + k) * 128, 128)]
        vec_parts[d, tiles:, :] = jnp.zeros((vec_parts.shape[1] - tiles, 128), F32)
    vec_one = [
        sems.remote(vec_parts.at[(p.dp + k) % p.ndp], vec_recv.at[p.dp], ((p.dp + k) % p.ndp, p.sq))
        for k in range(1, p.ndp)
    ]
    begin(vec_one)
    vec_recv[p.dp] = vec_parts[p.dp]
    finish(load_qkv)
    advance("out", 4)
    advance("qkv", 1)
    for i in range(grad_first.shape[0] // 512):
        rs = pl.ds(i * 512, 512)
        value = dot(slope[rs, pl.ds(0, wide)], columns(up_v, pl.ds(0, wide)), NT)
        grad_rows[rs, :] = (grad_first[rs, :] + value).astype(BF16)
    begin(move_grad)
    advance("qkv", 2)
    finish(vec_one)
    value = vec_recv[0]
    for k in range(1, p.ndp):
        value = value + vec_recv[k]
    vec_near[p.sq] = value
    near = vec_near.at[p.sq]
    vec_two = [sems.remote(near, near, (p.dp, (p.sq + k) % p.nsq)) for k in range(1, p.nsq)]
    begin(vec_two)
    advance("qkv", 3)
    finish(vec_two)
    value = vec_near[0]
    for k in range(1, p.nsq):
        value = value + vec_near[k]
    vec_s[...] = value

    def squares(value):
        return jnp.sum(jnp.sum(value * value, axis=0, keepdims=True), axis=1, keepdims=True)

    part = squares(value) * (1.0 / p.nsq)
    advance("qkv", 4)
    begin(last)
    for name in groups:
        for item in groups[name]:
            part = part + squares(item.final[...])
    near_sum[p.sq] = jnp.broadcast_to(part, near_sum.shape[1:])
    near = near_sum.at[p.sq]
    spread = [sems.remote(near, near, (p.dp, (p.sq + k) % p.nsq)) for k in range(1, p.nsq)]
    begin(spread)
    finish(spread)
    part = near_sum[0]
    for k in range(1, p.nsq):
        part = part + near_sum[k]
    far_sum[p.dp] = part
    far = far_sum.at[p.dp]
    spread = [sems.remote(far, far, ((p.dp + k) % p.ndp, p.sq)) for k in range(1, p.ndp)]
    begin(spread)
    finish(spread)
    part = far_sum[0]
    for k in range(1, p.ndp):
        part = part + far_sum[k]
    norm[...] = jnp.sqrt(part)
    finish(last + move_out + move_grad)


def backward(saved, key_bias):
    (x, qkv_w, out_w, up_w, down_w, vec, merged, heads, lse, normed, inverse, low, act, slope, block, second,
     grad_branch, sums) = saved
    ndp, nsq = lax.axis_size("dp"), lax.axis_size("seq")
    nz = ndp // 2
    part, full, width = x.shape
    count = part * full
    grid = qkv_w.shape[:3]
    rows, low_rows = qkv_w.shape[3], down_w.shape[4]
    merged = merged.reshape(grid + (count // math.prod(grid), 3 * width))
    act = act.reshape(grid + (count // math.prod(grid), FF))
    block = block.reshape(x.shape)
    token_shape = (part * nsq, full // nsq, width)
    any_space = pl.BlockSpec(memory_space=pl.ANY)
    vmem = pl.BlockSpec(memory_space=pltpu.VMEM)
    vec_tile = (16, 128)
    shapes = [jax.ShapeDtypeStruct(token_shape, BF16)] * 2
    shapes += [jax.ShapeDtypeStruct((rows // 2, w.shape[4]), F32) for w in (qkv_w, out_w, up_w)]
    shapes += [jax.ShapeDtypeStruct((low_rows, width), F32), jax.ShapeDtypeStruct(vec_tile, F32)]
    shapes += [jax.ShapeDtypeStruct((8, 128), F32)]

    def like(array):
        return pltpu.VMEM(array.shape, array.dtype)

    scratch = [like(a) for a in (up_w, down_w, out_w, act, slope, grad_branch, second, low)]
    scratch += [pltpu.VMEM((width, count), BF16)]
    scratch += [like(a) for a in (x, normed, inverse, lse, vec, sums, down_w, up_w, out_w, vec)]
    scratch += [pltpu.VMEM((1, 3 * width), F32)]
    scratch += [pltpu.VMEM((ndp,) + vec_tile, F32)] * 2 + [pltpu.VMEM((nsq,) + vec_tile, F32)]
    scratch += [pltpu.VMEM((nsq, 8, 128), F32), pltpu.VMEM((ndp, 8, 128), F32)]
    scratch += [pltpu.VMEM(grid + (low_rows, width), BF16), pltpu.VMEM(grid + (rows, width // 2), BF16)]
    for name in ("down", "up", "out", "qkv"):
        height = low_rows if name == "down" else rows
        for _, piece, _ in PIECES[name]:
            block_shape = (height, piece)
            scratch += [
                pltpu.VMEM((nz, 2) + block_shape, BF16),
                pltpu.VMEM((nz,) + block_shape, BF16),
                pltpu.VMEM((nz - 1,) + block_shape, BF16),
                pltpu.VMEM(block_shape, F32),
            ]
    scratch += [pltpu.SemaphoreType.DMA((96,)), pltpu.SemaphoreType.DMA((96,)), pltpu.SemaphoreType.DMA((48,))]
    scratch += [pltpu.SemaphoreType.REGULAR]
    return pl.pallas_call(
        backward_kernel,
        out_shape=shapes,
        in_specs=[any_space] * 18 + [vmem],
        out_specs=[any_space] * 6 + [vmem, vmem],
        scratch_shapes=scratch,
        compiler_params=pltpu.CompilerParams(
            collective_id=2, has_side_effects=True, vmem_limit_bytes=VMEM_LIMIT
        ),
    )(
        x, qkv_w, out_w, up_w, down_w, vec, merged, heads, lse, normed, inverse, low, act, slope, block, second,
        grad_branch, sums, key_bias,
    )


def unpack(vector):
    return (
        vector[:D],
        vector[D : 2 * D],
        vector[2 * D : 3 * D],
        vector[3 * D : 4 * D],
        vector[4 * D : 5 * D],
        vector[5 * D : 5 * D + FF],
        vector[5 * D + FF : 6 * D + FF],
        vector[6 * D + FF : 7 * D + FF],
        vector[7 * D + FF : 8 * D + FF],
    )


def normalize(hidden, gain_vec, shift_vec):
    centre = hidden - jnp.mean(hidden, axis=-1, keepdims=True)
    inverse = lax.rsqrt(jnp.mean(centre * centre, axis=-1, keepdims=True) + NORM_EPS)
    normed = centre * inverse
    return (normed * gain_vec + shift_vec, normed, inverse)


def normalize_back(grad_out, normed, inverse, gain_vec):
    scaled = grad_out * gain_vec
    centred = scaled - jnp.mean(scaled, axis=-1, keepdims=True)
    return inverse * (centred - normed * jnp.mean(scaled * normed, axis=-1, keepdims=True))


def gelu_exact(values):
    return jax.nn.gelu(values, approximate=False)


def split_parts(packed_rows):
    full_len = packed_rows.shape[0]
    group_count = packed_rows.shape[-1] // (3 * HEAD_DIM)
    parts = packed_rows.reshape(full_len, 3, group_count, HEAD_DIM)
    return (parts[:, 0], parts[:, 1], parts[:, 2])


def row_probs(queries, key_rows, key_mask):
    scale = 1.0 / math.sqrt(HEAD_DIM)
    scores = jnp.einsum("qhd,khd->hqk", queries, key_rows, preferred_element_type=F32) * scale
    scores = jnp.where(key_mask[None, None, :], scores, MASK_FILL)
    row_peak = jnp.max(scores, axis=-1, keepdims=True)
    row_exp = jnp.exp(scores - row_peak)
    return row_exp / jnp.sum(row_exp, axis=-1, keepdims=True)


def whole_row(packed):
    packed_rows, key_mask = packed
    queries, key_rows, value_rows = split_parts(packed_rows)
    attn_probs = row_probs(queries, key_rows, key_mask)
    mixed_rows = jnp.einsum("hqk,khd->qhd", attn_probs.astype(BF16), value_rows, preferred_element_type=F32)
    return mixed_rows.astype(BF16).reshape(packed_rows.shape[0], D)


def whole_back(packed):
    packed_rows, grad_rows, key_mask = packed
    full_len = packed_rows.shape[0]
    queries, key_rows, value_rows = split_parts(packed_rows)
    grad_mixed = grad_rows.reshape(full_len, HEADS, HEAD_DIM)
    attn_probs = row_probs(queries, key_rows, key_mask)
    grad_probs = jnp.einsum("qhd,khd->hqk", grad_mixed, value_rows, preferred_element_type=F32)
    row_delta = jnp.sum(attn_probs * grad_probs, axis=-1, keepdims=True)
    grad_scores = (attn_probs * (grad_probs - row_delta)).astype(BF16)
    scale = 1.0 / math.sqrt(HEAD_DIM)
    grad_query = jnp.einsum("hqk,khd->qhd", grad_scores, key_rows, preferred_element_type=F32) * scale
    grad_key = jnp.einsum("hqk,qhd->khd", grad_scores, queries, preferred_element_type=F32) * scale
    grad_value = jnp.einsum("hqk,qhd->khd", attn_probs.astype(BF16), grad_mixed, preferred_element_type=F32)
    stacked = jnp.stack([grad_query, grad_key, grad_value], axis=1).astype(BF16)
    return stacked.reshape(full_len, 3 * D)


def adam_step(master, gradient, moment_one, second, factor, decay_rate, step_rate):
    clipped = gradient * factor
    first_new = BETA_ONE * moment_one + (1.0 - BETA_ONE) * clipped
    second_new = BETA_TWO * second + (1.0 - BETA_TWO) * clipped * clipped
    first_hat = first_new / (1.0 - BETA_ONE**STEP_COUNT)
    second_hat = second_new / (1.0 - BETA_TWO**STEP_COUNT)
    updated = master - step_rate * (first_hat / (jnp.sqrt(second_hat) + ADAM_EPS) + decay_rate * master)
    return (updated, first_new, second_new, updated.astype(BF16))


def layer(rows_in, cot_in, token_weight, lengths, qkv_w, out_w, up_w, down_w, vec_w):
    row_count, full_len, width_d = rows_in.shape
    token_count = row_count * full_len
    bias_q, bias_v, bias_o, gain_one, shift_one, bias_up, bias_down, gain_two, shift_two = unpack(vec_w)
    key_mask = jnp.arange(full_len, dtype=jnp.int32)[None, :] < lengths[:, None]
    flat = rows_in.reshape(token_count, width_d)
    merged = jnp.dot(flat, qkv_w, preferred_element_type=F32)
    merged = (merged + jnp.concatenate([bias_q, jnp.zeros_like(bias_q), bias_v])).astype(BF16)
    merged_rows = merged.reshape(row_count, full_len, 3 * width_d)
    mixed = lax.map(whole_row, (merged_rows, key_mask)).reshape(token_count, width_d)
    attn_out = jnp.dot(mixed, out_w, preferred_element_type=F32) + bias_o
    first_out, normed_one, inverse_one = normalize(flat.astype(F32) + attn_out, gain_one, shift_one)
    first_low = first_out.astype(BF16)
    pre_act = jnp.dot(first_low, up_w, preferred_element_type=F32) + bias_up
    activated, gelu_pull = jax.vjp(gelu_exact, pre_act)
    act_low = activated.astype(BF16)
    branch = jnp.dot(act_low, down_w, preferred_element_type=F32) + bias_down
    result, normed_two, inverse_two = normalize(first_out + branch, gain_two, shift_two)
    block_out = result.astype(BF16).reshape(row_count, full_len, width_d)
    grad_result = cot_in.astype(F32) * (token_weight * key_mask.astype(F32))[:, :, None]
    grad_result = grad_result.reshape(token_count, width_d)
    grad_gain_two = jnp.sum(grad_result * normed_two, axis=0)
    grad_shift_two = jnp.sum(grad_result, axis=0)
    grad_second = normalize_back(grad_result, normed_two, inverse_two, gain_two)
    grad_branch = grad_second.astype(BF16)
    grad_bias_down = jnp.sum(grad_branch, axis=0, dtype=F32)
    grad_down = jnp.einsum("tf,td->fd", act_low, grad_branch, preferred_element_type=F32)
    grad_act = jnp.einsum("td,fd->tf", grad_branch, down_w, preferred_element_type=F32)
    grad_pre = gelu_pull(grad_act)[0].astype(BF16)
    grad_bias_up = jnp.sum(grad_pre, axis=0, dtype=F32)
    grad_up = jnp.einsum("td,tf->df", first_low, grad_pre, preferred_element_type=F32)
    grad_first = grad_second + jnp.einsum("tf,df->td", grad_pre, up_w, preferred_element_type=F32)
    grad_gain_one = jnp.sum(grad_first * normed_one, axis=0)
    grad_shift_one = jnp.sum(grad_first, axis=0)
    grad_resid = normalize_back(grad_first, normed_one, inverse_one, gain_one)
    grad_attn = grad_resid.astype(BF16)
    grad_bias_o = jnp.sum(grad_attn, axis=0, dtype=F32)
    grad_out = jnp.einsum("td,te->de", mixed, grad_attn, preferred_element_type=F32)
    grad_mixed = jnp.einsum("te,de->td", grad_attn, out_w, preferred_element_type=F32).astype(BF16)
    grad_merged = lax.map(
        whole_back, (merged_rows, grad_mixed.reshape(row_count, full_len, width_d), key_mask)
    ).reshape(token_count, 3 * width_d)
    grad_qkv = jnp.einsum("td,te->de", flat, grad_merged, preferred_element_type=F32)
    column_sums = jnp.sum(grad_merged, axis=0, dtype=F32)
    input_grad = grad_resid + jnp.einsum("te,de->td", grad_merged, qkv_w, preferred_element_type=F32)
    input_grad = input_grad.astype(BF16).reshape(row_count, full_len, width_d)
    grad_vec = jnp.concatenate(
        [
            column_sums[:width_d],
            column_sums[2 * width_d :],
            grad_bias_o,
            grad_gain_one,
            grad_shift_one,
            grad_bias_up,
            grad_bias_down,
            grad_gain_two,
            grad_shift_two,
        ]
    )
    low = [g.astype(BF16) for g in (grad_qkv, grad_out, grad_up, grad_down)]
    return block_out, input_grad, *low, grad_vec


def body(
    tokens, cotangent, token_weight, lengths,
    qkv_master, out_master, up_master, down_master, vec_master,
    qkv_first, out_first, up_first, down_first, vec_first,
    qkv_second, out_second, up_second, down_second, vec_second,
):
    ndp, nsq = lax.axis_size("dp"), lax.axis_size("seq")
    devices = ndp * nsq
    row_count, local_len, width_d = tokens.shape
    full_len, part = local_len * nsq, row_count // nsq
    vec_size = vec_master.shape[0]
    sq = lax.axis_index("seq")
    my_lengths = lax.dynamic_slice_in_dim(lengths, sq * part, part)
    both = ("dp", "seq")
    chip = 2 * qkv_master.shape[0]
    own_kernels = (
        qkv_master.shape[0] % 8 == 0
        and down_master.shape[0] % 16 == 0
        and nsq == 4
        and ndp % 2 == 0
        and vec_size * nsq % 128 == 0
        and part * full_len // (ndp * nsq // 2) >= chip
    )
    if own_kernels:
        position = sq * local_len + jnp.arange(local_len, dtype=jnp.int32)
        live = token_weight * (position[None, :] < lengths[:, None])
        live = jnp.broadcast_to(live[:, :, None], token_weight.shape + (128,))
        key_bias = jnp.where(jnp.arange(full_len)[None, :, None] < my_lengths[:, None, None], 0.0, MASK_FILL)
        spread = jnp.zeros((16 * 128,), F32)
        spread = lax.dynamic_update_slice(spread, vec_master, (sq * vec_size,)).reshape(16, 128)
        key_bias = key_bias.astype(F32)
        saved = forward(
            tokens, cotangent, live, qkv_master, out_master, up_master, down_master, spread, key_bias
        )
        block_out, input_grad, *shards, vec_s, norm = backward(saved, key_bias)
        shards.append(lax.dynamic_slice(vec_s.reshape(-1), (sq * vec_size,), (vec_size,)))
        norm_value = norm[0, 0]
    else:
        rows_in, cot_in = (
            lax.all_to_all(a, "seq", split_axis=0, concat_axis=1, tiled=True) for a in (tokens, cotangent)
        )
        weights = lax.all_gather(token_weight, "seq", axis=0)
        qkv_w, out_w, up_w, down_w, vec_w = (
            lax.all_gather(m.astype(BF16), both, axis=0, tiled=True)
            for m in (qkv_master, out_master, up_master, down_master, vec_master)
        )
        my_weight = lax.dynamic_slice_in_dim(weights, sq * part, part, axis=1)
        my_weight = my_weight.transpose(1, 0, 2).reshape(part, full_len)
        block_rows, grad_rows, *grads, grad_vec = layer(
            rows_in, cot_in, my_weight, my_lengths, qkv_w, out_w, up_w, down_w, vec_w.astype(F32)
        )
        block_out, input_grad = (
            lax.all_to_all(a, "seq", split_axis=1, concat_axis=0, tiled=True) for a in (block_rows, grad_rows)
        )
        shards = [lax.psum_scatter(g.astype(F32), both, scatter_dimension=0, tiled=True) for g in grads]
        shards.append(lax.psum_scatter(grad_vec, both, scatter_dimension=0, tiled=True))
        norm_value = jnp.sqrt(lax.psum(sum(jnp.sum(s * s) for s in shards), both))
    factor = CLIP_NORM / jnp.maximum(norm_value, CLIP_NORM)
    outs = [block_out, input_grad, norm_value]
    for master, shard, first, second, decay, rate in (
        (qkv_master, shards[0], qkv_first, qkv_second, WEIGHT_DECAY, LEARN_RATE),
        (out_master, shards[1], out_first, out_second, WEIGHT_DECAY, LEARN_RATE),
        (up_master, shards[2], up_first, up_second, WEIGHT_DECAY, LEARN_RATE),
        (down_master, shards[3], down_first, down_second, WEIGHT_DECAY, LEARN_RATE),
        (vec_master, shards[4], vec_first, vec_second, 0.0, VEC_RATE),
    ):
        outs += adam_step(master, shard, first, second, factor, decay, rate)
    return tuple(outs)


def solution(mesh):
    tokens, both, flat = P("dp", "seq", None), P(("dp", "seq"), None), P(("dp", "seq"))
    weights = (both, both, both, both, flat)
    in_specs = (tokens, tokens, P("dp", "seq"), P("dp")) + 3 * weights
    out_specs = (tokens, tokens, P()) + 4 * (both,) * 4 + (flat,) * 4
    return jax.shard_map(body, mesh=mesh, in_specs=in_specs, out_specs=out_specs, check_vma=False)
```

```python
import functools
import math

import jax
import jax.numpy as jnp
from jax import lax
from jax.experimental import pallas as pl
from jax.experimental.pallas import tpu as pltpu
from jax.sharding import PartitionSpec as P

D = 768
HEADS = 12
HEAD_DIM = 64
FF = 3072
STEP_COUNT = 10
CLIP_NORM = 1.0
BETA_ONE = 0.9
BETA_TWO = 0.999
LEARN_RATE = 0.05
VEC_RATE = 0.3
WEIGHT_DECAY = 0.01
ADAM_EPS = 1e-08
NORM_EPS = 1e-05
MASK_FILL = -1e30
MESH = pl.DeviceIdType.MESH
F32 = jnp.float32
BF16 = jnp.bfloat16
VMEM_LIMIT = 62 << 20


class Place:
    def __init__(self):
        self.ndp, self.nsq = lax.axis_size("dp"), lax.axis_size("seq")
        self.dp, self.sq = lax.axis_index("dp"), lax.axis_index("seq")
        self.z, self.y = self.dp // 2, self.dp % 2
        self.x, self.c = self.sq // 2, self.sq % 2
        self.nz = self.ndp // 2
        self.core = (self.dp, self.x * 2 + 1 - self.c)
        self.across_x = (self.dp, (1 - self.x) * 2 + self.c)
        self.across_y = (self.z * 2 + 1 - self.y, self.sq)

    def along_z(self, k):
        return (self.z + k) % self.nz

    def at_z(self, z):
        return (z * 2 + self.y, self.sq)

    def group(self):
        return [(self.dp, (self.sq + k) % self.nsq) for k in range(1, self.nsq)]

    def columns(self):
        return [((self.dp + k) % self.ndp, self.sq) for k in range(1, self.ndp)]


def greet(targets):
    barrier = pltpu.get_barrier_semaphore()
    for target in targets:
        pl.semaphore_signal(barrier, inc=1, device_id=target, device_id_type=MESH)
    pl.semaphore_wait(barrier, len(targets))


class Sems:
    def __init__(self, send, recv, local):
        self.send, self.recv, self.local = send, recv, local
        self.n = self.m = 0

    def remote(self, src, dst, target):
        i = self.n
        self.n += 1
        return pltpu.make_async_remote_copy(
            src_ref=src,
            dst_ref=dst,
            send_sem=self.send.at[i],
            recv_sem=self.recv.at[i],
            device_id=target,
            device_id_type=MESH,
        )

    def here(self, src, dst):
        i = self.m
        self.m += 1
        return pltpu.make_async_copy(src, dst, self.local.at[i])


def begin(copies):
    for copy in copies:
        copy.start()


def finish(copies):
    for copy in copies:
        copy.wait()


GATHER = (
    (('qkv', 0), 'zyx'),
    (('qkv', 1), 'xzy'),
    (('qkv', 2), 'xzy'),
    (('out', 0), 'zyx'),
    (('up', 0), 'zyx'),
    (('up', 1), 'zyx'),
    (('up', 3), 'xzy'),
    (('up', 2), 'zxy'),
    (('down', 0), 'yzx'),
    (('down', 1), 'xzy'),
    (('down', 2), 'xyz'),
)
SCATTER = (
    (('down', 1), 'yxz'),
    (('down', 0), 'xyz'),
    (('down', 2), 'xyz'),
    (('up', 0), 'yzx'),
    (('up', 1), 'yxz'),
    (('up', 2), 'yzx'),
    (('up', 3), 'xyz'),
    (('qkv', 0), 'yxz'),
    (('qkv', 1), 'yxz'),
    (('out', 0), 'zyx'),
    (('qkv', 2), 'yzx'),
)
FORWARD_PLAN = (
    ((('qkv', 0), 0), (('qkv', 1), 0), (('qkv', 2), 0)),
    ((('out', 0), 0), (('down', 0), 0)),
    (('tok', 0), (('up', 3), 0), (('qkv', 0), 1), (('qkv', 1), 1), (('down', 1), 0), (('qkv', 2), 1), (('out', 0), 1), (('down', 2), 0), (('qkv', 0), 2), (('down', 2), 1), (('qkv', 1), 2), (('up', 0), 0), (('qkv', 2), 2), (('up', 1), 0), (('up', 0), 1), (('up', 3), 1), (('up', 2), 0), (('qkv', 0), 3), (('out', 0), 2), (('qkv', 0), 4)),
    (),
    ((('qkv', 1), 3), (('up', 1), 1), (('up', 2), 1), (('down', 0), 1)),
    ((('qkv', 2), 3),),
    ((('qkv', 1), 4), (('out', 0), 3), (('up', 0), 2), (('up', 3), 2), (('down', 1), 1)),
    (),
    ((('qkv', 2), 4),),
    ((('out', 0), 4), (('up', 1), 2), (('up', 2), 2)),
    (),
    (),
    (),
    (),
    ((('up', 0), 3), (('up', 3), 3), (('down', 0), 2), (('down', 2), 2)),
    (),
    ((('up', 2), 3),),
    (),
    (('cot', 0), (('up', 0), 4), (('up', 1), 3), (('up', 3), 4), (('down', 1), 2)),
    ((('up', 2), 4),),
    ((('up', 1), 4),),
    ((('down', 0), 3),),
    ((('down', 0), 4), (('down', 1), 3), (('down', 2), 3)),
    (),
    ((('down', 1), 4), (('down', 2), 4)),
    (),
    (),
)
BACKWARD_PLAN = (
    (('out', 0), (('down', 1), 0), (('down', 0), 0), (('down', 2), 0)),
    (),
    ((('up', 0), 0),),
    (),
    ((('down', 1), 1), (('down', 0), 1), (('down', 2), 1), (('up', 0), 1), (('up', 1), 0), (('up', 2), 0), (('up', 3), 0)),
    (),
    ((('up', 1), 1), (('out', 0), 0)),
    (),
    ((('out', 0), 1),),
    (),
    ((('up', 0), 2), (('up', 2), 1)),
    ((('qkv', 0), 0),),
    ((('down', 1), 2), (('down', 0), 2), (('down', 2), 2), (('up', 1), 2), (('up', 3), 1)),
    (),
    ((('up', 2), 2), (('qkv', 0), 1)),
    ((('qkv', 1), 0),),
    ((('down', 1), 3), (('down', 0), 3), (('up', 0), 3), (('qkv', 1), 1), (('out', 0), 2)),
    (),
    ((('down', 2), 3), (('up', 0), 4), (('up', 2), 3), (('up', 3), 2), (('qkv', 0), 2), (('out', 0), 3)),
    ((('qkv', 2), 0),),
    ((('down', 1), 4), (('down', 0), 4), (('up', 1), 3), (('up', 2), 4), (('out', 0), 4), (('qkv', 2), 1)),
    (),
    ((('down', 2), 4), (('up', 3), 3), (('qkv', 0), 3), (('qkv', 1), 2)),
    ((('up', 1), 4),),
    ((('qkv', 2), 2), (('up', 3), 4), (('qkv', 0), 4), (('qkv', 1), 3), (('qkv', 2), 3), (('qkv', 1), 4), (('qkv', 2), 4)),
)
PAIRS = HEADS // 2
NT = (((1,), (1,)), ((), ()))
TN = (((0,), (0,)), ((), ()))
NN = (((1,), (0,)), ((), ()))
ERF_P = 0.3275911
ERF_B = (0.254829592, -0.284496736, 1.421413741, -1.453152027, 1.061405429)


def dot(a, b, dims=NN):
    return lax.dot_general(a, b, dims, preferred_element_type=F32)


def lanes(start, size):
    return pl.ds(pl.multiple_of(start, 128), size)


def mean(values):
    return jnp.sum(values, axis=-1, keepdims=True) * (1.0 / D)


def matrix(ref, *index):
    value = ref[index] if index else ref[...]
    return value.reshape(-1, value.shape[-1])


def columns(ref, cols):
    value = ref[:, :, :, :, cols]
    return value.reshape(-1, value.shape[-1])


class Gather:
    def __init__(self, place, sems, at, order):
        p = place
        spot = {"z": p.z, "y": p.y, "x": p.x}
        self.stages = []
        for axis in order:
            here = at(**spot)
            if axis == "z":
                targets = [p.at_z(p.along_z(k)) for k in range(1, p.nz)]
            else:
                targets = [p.across_x if axis == "x" else p.across_y]
            self.stages.append([sems.remote(here, here, target) for target in targets])
            spot[axis] = slice(None)
        here = at(**spot)
        self.stages.append([sems.remote(here, here, p.core)])

    def advance(self, stage):
        if stage:
            finish(self.stages[stage - 1])
        if stage < len(self.stages):
            begin(self.stages[stage])


class Scatter:
    def __init__(self, place, sems, at, near, bufs, order):
        p = place
        *bufs, final = bufs
        total = at(p.c)
        self.final = final
        self.stages = [[sems.remote(at(1 - p.c), near, p.core)]]
        sizes = {"z": p.nz, "y": 2, "x": 2}
        own = {"z": p.z, "y": p.y, "x": p.x}
        spot = {axis: slice(None) for axis in "zyx"}
        left = [axis for axis in "zyx"]

        def index(spot):
            return (spot["z"], spot["y"], spot["x"])

        self.after = [functools.partial(add_into, total, [near], [sizes[axis] for axis in left])]
        for buf, axis in zip(bufs, order):
            if axis == "z":
                targets = [(p.along_z(k), p.at_z(p.along_z(k)), buf.at[k - 1]) for k in range(1, p.nz)]
            elif axis == "y":
                targets = [(1 - p.y, p.across_y, buf)]
            else:
                targets = [(1 - p.x, p.across_x, buf)]
            self.stages.append(
                [sems.remote(total.at[index({**spot, axis: to})], into, device) for to, device, into in targets]
            )
            spot[axis] = own[axis]
            left.remove(axis)
            extra = [into for _, _, into in targets]
            kept = total.at[index(spot)]
            if left:
                self.after.append(functools.partial(add_into, kept, extra, [sizes[axis] for axis in left]))
            else:
                self.after.append(functools.partial(add_last, final, kept, extra))

    def advance(self, stage):
        if stage:
            finish(self.stages[stage - 1])
            self.after[stage - 1]()
        if stage < len(self.stages):
            begin(self.stages[stage])


def add_into(total, extra, lead):
    def one(i, carry):
        spot = []
        for size in reversed(lead):
            spot.insert(0, i % size)
            i = i // size
        spot = tuple(spot)
        value = total[spot].astype(F32)
        for part in extra:
            value = value + part[spot].astype(F32)
        total[spot] = value.astype(total.dtype)
        return carry

    lax.fori_loop(0, math.prod(lead), one, 0)


def add_last(final, total, extra):
    value = total[...].astype(F32)
    for part in extra:
        value = value + part[...].astype(F32)
    final[...] = value


def scatter_buffers(block, nz, order):
    sizes = {"z": nz, "y": 2, "x": 2}
    left, bufs = list("zyx"), []
    for axis in order:
        left.remove(axis)
        lead = tuple(sizes[a] for a in left)
        if axis == "z":
            lead = (nz - 1,) + lead
        bufs.append(pltpu.VMEM(lead + block, BF16))
    return bufs + [pltpu.VMEM(block, F32)]


def tokens_to_rows(place, sems, src, dst):
    p = place
    part, length = dst.shape[0], src.shape[1]
    spot = dst.at[:, pl.ds(p.sq * length, length)]
    copies = [sems.here(src.at[pl.ds(p.sq * part, part)], spot)]
    for k in range(1, p.nsq):
        to = (p.sq + k) % p.nsq
        copies.append(sems.remote(src.at[pl.ds(to * part, part)], spot, (p.dp, to)))
    return copies


def rows_to_tokens(place, sems, src, dst):
    p = place
    part, length = src.shape[0], dst.shape[1]
    spot = dst.at[pl.ds(p.sq * part, part)]
    copies = [sems.here(src.at[:, pl.ds(p.sq * length, length)], spot)]
    for k in range(1, p.nsq):
        to = (p.sq + k) % p.nsq
        copies.append(sems.remote(src.at[:, pl.ds(to * length, length)], spot, (p.dp, to)))
    return copies


def of_head(values, h):
    lane = lax.broadcasted_iota(jnp.int32, values.shape, 1)
    own = lane < HEAD_DIM if h == 0 else lane >= HEAD_DIM
    return jnp.where(own, values, jnp.zeros_like(values))


def pair_base(p):
    return (p % 2) * (3 * D // 2) + (p // 2) * (3 * 128)


def project(x, w, bias, merged, p, rows=512):
    cs = pl.ds(pair_base(p), 384)
    part = columns(w, cs)
    for i in range(x.shape[0] // rows):
        rs = pl.ds(i * rows, rows)
        merged[rs, cs] = (dot(x[rs, :], part) + bias[0:1, cs]).astype(BF16)


def attend(merged, key_bias, heads_out, lse, length, p):
    base = pair_base(p)

    @pl.loop(0, heads_out.shape[0] // length)
    def _(r):
        rs = pl.ds(pl.multiple_of(r * length, 128), length)
        q2 = merged[rs, pl.ds(base, 128)] * jnp.asarray(HEAD_DIM**-0.5, BF16)
        k2 = merged[rs, pl.ds(base + 128, 128)]
        v2t = merged[rs, pl.ds(base + 256, 128)].T
        bias = key_bias[r]
        outs = []
        for h in range(2):
            scores = dot(of_head(k2, h), q2, NT) + bias
            peak = jnp.max(scores, axis=0, keepdims=True)
            weights = jnp.exp(scores - peak)
            total = jnp.sum(weights, axis=0, keepdims=True)
            outs.append(dot(v2t, weights.astype(BF16)) * (1.0 / total))
            lse[r, 2 * p + h] = peak + jnp.log(total)
        row = lax.broadcasted_iota(jnp.int32, outs[0].shape, 0)
        mixed = jnp.where(row < HEAD_DIM, outs[0], outs[1])
        heads_out[rs, pl.ds(p * 128, 128)] = mixed.T.astype(BF16)


def first_norm(x, heads_out, w, vec, normed, inverse, low, start, count, rows=256):
    @pl.loop(0, count // rows)
    def _(i):
        rs = pl.ds(pl.multiple_of(start + i * rows, rows), rows)
        hidden = x[rs, :].astype(F32) + (dot(heads_out[rs, :], matrix(w)) + vec[0:1, 2 * D : 3 * D])
        centre = hidden - mean(hidden)
        scale = lax.rsqrt(mean(centre * centre) + NORM_EPS)
        unit = centre * scale
        normed[rs, :] = unit
        inverse[rs, :] = scale
        low[rs, :] = (unit * vec[0:1, 3 * D : 4 * D] + vec[0:1, 4 * D : 5 * D]).astype(BF16)


def normal_cdf_pdf(x):
    t = 1.0 / (1.0 + (ERF_P * 0.5**0.5) * jnp.abs(x))
    bell = jnp.exp(-0.5 * (x * x))
    tail = 0.5 * ERF_B[4]
    for b in ERF_B[3::-1]:
        tail = tail * t + 0.5 * b
    tail = tail * t * bell
    return jnp.where(x >= 0, 1.0 - tail, tail), bell * (2 * math.pi) ** -0.5


def feed_up(j, low, up_w, vec, act, slope, chunk, rows=256):
    cs = pl.ds(j * chunk, chunk)
    bias = vec[0:1, 5 * D + j * chunk : 5 * D + (j + 1) * chunk]

    @pl.loop(0, low.shape[0] // (2 * rows))
    def _(i):
        weight = columns(up_w, cs)
        for k in range(2):
            rs = pl.ds(pl.multiple_of((2 * i + k) * rows, rows), rows)
            value = dot(low[rs, :], weight) + bias
            cdf, pdf = normal_cdf_pdf(value)
            act[rs, cs] = (value * cdf).astype(BF16)
            slope[rs, cs] = (cdf + value * pdf).astype(slope.dtype)


def feed_down(act, down_w, branch, cs, rows=512):
    weight = down_w[:, :, :, :, :, cs]
    weight = weight.reshape(-1, weight.shape[-1])
    for i in range(act.shape[0] // rows):
        rs = pl.ds(i * rows, rows)
        branch[rs, cs] = dot(act[rs, :], weight)


def second_norm(normed, vec, branch, cot, weight, block_out, grad_branch, sums, rows=128):
    sums[...] = jnp.zeros_like(sums)
    at = 5 * D + FF
    gain_one, shift_one, bias_down = (vec[0:1, s : s + D] for s in (3 * D, 4 * D, at))
    gain_two, shift_two = (vec[0:1, s : s + D] for s in (at + D, at + 2 * D))

    @pl.loop(0, normed.shape[0] // rows)
    def _(i):
        rs = pl.ds(pl.multiple_of(i * rows, rows), rows)
        hidden = normed[rs, :] * gain_one + shift_one + (branch[rs, :] + bias_down)
        centre = hidden - mean(hidden)
        scale = lax.rsqrt(mean(centre * centre) + NORM_EPS)
        unit = centre * scale
        block_out[rs, :] = (unit * gain_two + shift_two).astype(BF16)
        grad = cot[rs, :].astype(F32) * weight[rs, 0:1]
        sums[1:2, :] += jnp.sum(grad * unit, axis=0, keepdims=True)
        sums[2:3, :] += jnp.sum(grad, axis=0, keepdims=True)
        scaled = grad * gain_two
        second = scale * (scaled - mean(scaled) - unit * mean(scaled * unit))
        normed[rs, :] = second
        low = second.astype(BF16)
        grad_branch[rs, :] = low
        sums[0:1, :] += jnp.sum(low.astype(F32), axis=0, keepdims=True)


def forward_kernel(
    tokens, cotangent, weight, qkv_m, out_m, up_m, down_m, vec_m, key_bias,
    x_out, qkv_w, out_w, up_w, down_w, vec_out, merged_out, heads_out, lse_out, normed_out, inverse_out,
    low_out, act_out, slope_out, block_out, second_out, branch_out, sums_out,
    qkv_f, out_f, up_f, down_f,
    qkv_v, out_v, up_v, down_v, x, cot, wt, wt_all, vec_near, vec_far, vec, bias, merged, heads, lse, normed, inverse,
    low, act, slope, branch, grad_branch, sums, send, recv, local,
):
    p = Place()
    greet(p.group() + p.columns())
    sems = Sems(send, recv, local)
    part, length = x.shape[0], x.shape[1]
    moves = {
        "tok": tokens_to_rows(p, sems, tokens, x),
        "cot": tokens_to_rows(p, sems, cotangent, cot),
    }
    spot = wt_all.at[p.sq]
    move_weight = [sems.here(weight, spot)] + [sems.remote(weight, spot, to) for to in p.group()]
    masters = {"qkv": (qkv_m, qkv_f), "out": (out_m, out_f), "up": (up_m, up_f)}
    rows = qkv_m.shape[0]
    mine = pl.ds(p.c * rows, rows)
    fetch = {
        name: [sems.here(master, wide.at[mine]), sems.remote(master, wide.at[mine], p.core)]
        for name, (master, wide) in masters.items()
    }
    fetch["down"] = [sems.here(down_m, down_f)]
    chunk = FF // len([name for name, _ in GATHER if name[0] == "up"])
    down_cols = D // len([name for name, _ in GATHER if name[0] == "down"])
    half = 3 * D // 2
    places = {
        "qkv": lambda g: lambda z, y, x: qkv_v.at[z, y, x, :, lanes(p.c * half + g * 384, 384)],
        "out": lambda g: lambda z, y, x: out_v.at[z, y, x, :, lanes(p.c * (D // 2), D // 2)],
        "up": lambda g: lambda z, y, x: up_v.at[z, y, x, :, lanes(g * chunk + p.c * (chunk // 2), chunk // 2)],
        "down": lambda g: lambda z, y, x: down_v.at[z, y, x, p.c, :, pl.ds(g * down_cols, down_cols)],
    }
    items = {key: Gather(p, sems, places[key[0]](key[1]), order) for key, order in GATHER}
    near = vec_near.at[p.sq]
    vec_one = [sems.remote(near, near, to) for to in p.group()]
    far = vec_far.at[p.dp]
    vec_two = [sems.remote(far, far, to) for to in p.columns()]

    def cast(name):
        finish(fetch[name])
        own = (p.z, p.y, p.x)
        if name == "qkv":
            for g in range(PAIRS // 2):
                for s in range(3):
                    to = lanes(p.c * half + g * 384 + s * 128, 128)
                    qkv_v[own + (slice(None), to)] = qkv_f[:, lanes(s * D + (2 * g + p.c) * 128, 128)].astype(BF16)
        elif name == "out":
            cs = lanes(p.c * (D // 2), D // 2)
            out_v[own + (slice(None), cs)] = out_f[:, cs].astype(BF16)
        elif name == "up":
            for g in range(FF // chunk):
                cs = lanes(g * chunk + p.c * (chunk // 2), chunk // 2)
                up_v[own + (slice(None), cs)] = up_f[:, cs].astype(BF16)
        else:
            down_v[own + (p.c,)] = down_f[...].astype(BF16)

    plan = iter(FORWARD_PLAN)

    def go():
        for key, stage in next(plan):
            if key in moves:
                begin(moves[key])
            else:
                items[key].advance(stage)

    begin(fetch["qkv"])
    vec_near[p.sq] = vec_m[...].astype(BF16).astype(F32)
    begin(fetch["out"] + fetch["up"] + fetch["down"])
    cast("qkv")
    go()
    begin(vec_one + move_weight)
    for name in ("out", "up", "down"):
        cast(name)
    finish(vec_one)
    block = vec_near[0]
    for k in range(1, p.nsq):
        block = block + vec_near[k]
    vec_far[p.dp] = block
    begin(vec_two)
    go()
    finish(vec_two)
    tiles = vec.shape[1] // (128 * p.ndp)
    for d in range(p.ndp):
        for k in range(tiles):
            vec[0:1, pl.ds((d * tiles + k) * 128, 128)] = vec_far[d, k : k + 1, :]
    for pair in range(PAIRS):
        base = pair_base(pair)
        bias[0:1, base : base + 128] = vec[0:1, pair * 128 : (pair + 1) * 128]
        bias[0:1, base + 128 : base + 256] = jnp.zeros((1, 128), F32)
        bias[0:1, base + 256 : base + 384] = vec[0:1, D + pair * 128 : D + (pair + 1) * 128]
    finish(move_weight)
    for r in range(part):
        for k in range(p.nsq):
            row = wt_all[k, pl.ds(p.sq * part + r, 1), :]
            size = row.shape[1]
            wt[pl.ds(r * length + k * size, size), :] = jnp.broadcast_to(row, (size, size)).T
    flat = x.reshape(part * length, D)
    keep = {}

    def save(name, src, dst):
        keep[name] = sems.here(src, dst)
        keep[name].start()

    for g in range(PAIRS // 2):
        go()
        if g == 0:
            finish(moves["tok"])
            save("x", x, x_out)
        for pair in (2 * g, 2 * g + 1):
            project(flat, qkv_v, bias, merged, pair)
            go()
            attend(merged, key_bias, heads, lse, length, pair)
            go()
    save("qkv", qkv_v, qkv_w)
    save("merged", merged, merged_out)
    save("heads", heads, heads_out)
    save("lse", lse, lse_out)
    go()
    save("out", out_v, out_w)
    first_norm(flat, heads, out_v, vec, normed, inverse, low, 0, part * length // 2)
    go()
    first_norm(flat, heads, out_v, vec, normed, inverse, low, part * length // 2, part * length // 2)
    save("normed", normed, normed_out)
    save("inverse", inverse, inverse_out)
    save("low", low, low_out)
    for j in range(FF // chunk):
        go()
        feed_up(j, low, up_v, vec, act, slope, chunk)
    save("up", up_v, up_w)
    save("act", act, act_out)
    save("slope", slope, slope_out)
    for j in range(D // down_cols):
        go()
        feed_down(act, down_v, branch, pl.ds(j * down_cols, down_cols))
    save("down", down_v, down_w)
    go()
    finish(moves["cot"])
    keep.pop("heads").wait()
    keep.pop("normed").wait()
    second_norm(normed, vec, branch, cot.reshape(part * length, D), wt, heads, grad_branch, sums)
    save("block", heads, block_out)
    save("second", normed, second_out)
    save("branch", grad_branch, branch_out)
    save("sums", sums, sums_out)
    save("vec", vec, vec_out)
    finish(keep.values())


def forward(tokens, cotangent, weight, qkv_m, out_m, up_m, down_m, vec_m, key_bias):
    ndp, nsq = lax.axis_size("dp"), lax.axis_size("seq")
    rows, length, width = tokens.shape
    part, full = rows // nsq, length * nsq
    count = part * full
    chip, low = 2 * qkv_m.shape[0], down_m.shape[0]
    grid = (ndp // 2, 2, nsq // 2)
    vec_len = 8 * D + FF
    any_space = pl.BlockSpec(memory_space=pl.ANY)
    vmem = pl.BlockSpec(memory_space=pltpu.VMEM)

    def both(shape, dtype):
        return jax.ShapeDtypeStruct(shape, dtype), pltpu.VMEM(shape, dtype)

    weights = [both(grid + (chip, m.shape[1]), BF16) for m in (qkv_m, out_m, up_m)]
    weights.append(both(grid + (2, low, width), BF16))
    x = both((part, full, width), BF16)
    vec = both((1, vec_len), F32)
    merged = both((count, 3 * width), BF16)
    heads = both((count, width), BF16)
    lse = both((part, HEADS, 1, full), F32)
    normed = both((count, width), F32)
    inverse = both((count, 1), F32)
    act = both((count, FF), BF16)
    sums = both((8, width), F32)
    outs = [x[0]] + [w[0] for w in weights] + [vec[0], merged[0], heads[0], lse[0], normed[0], inverse[0]]
    outs += [heads[0], act[0], act[0], heads[0], normed[0], heads[0], sums[0]]
    scratch = [pltpu.VMEM((chip, m.shape[1]), F32) for m in (qkv_m, out_m, up_m)] + [pltpu.VMEM(down_m.shape, F32)]
    scratch += [w[1] for w in weights]
    scratch += [x[1], x[1], pltpu.VMEM((count, length), F32), pltpu.VMEM((nsq,) + weight.shape, F32)]
    scratch += [pltpu.VMEM((nsq,) + vec_m.shape, F32), pltpu.VMEM((ndp,) + vec_m.shape, F32), vec[1]]
    scratch += [pltpu.VMEM((1, 3 * width), F32), merged[1], heads[1], lse[1], normed[1], inverse[1]]
    scratch += [heads[1], act[1], act[1], normed[1], heads[1], sums[1]]
    scratch += [pltpu.SemaphoreType.DMA((96,)), pltpu.SemaphoreType.DMA((96,)), pltpu.SemaphoreType.DMA((48,))]
    return pl.pallas_call(
        forward_kernel,
        out_shape=outs,
        in_specs=[any_space] * 7 + [vmem] * 2,
        out_specs=[any_space] * len(outs),
        scratch_shapes=scratch,
        compiler_params=pltpu.CompilerParams(
            collective_id=1, has_side_effects=True, vmem_limit_bytes=VMEM_LIMIT
        ),
    )(tokens, cotangent, weight, qkv_m, out_m, up_m, down_m, vec_m, key_bias)


def feed_back_down(j, grad_branch, down_w, act, slope, grad_down, vec_sum, rows=512):
    n = grad_down.shape[0]
    cols = FF // n
    cs = pl.ds(j * cols, cols)
    weight = matrix(down_w, j)

    total = None
    for i in range(slope.shape[0] // rows):
        rs = pl.ds(i * rows, rows)
        grad = dot(grad_branch[rs, :], weight, NT) * slope[rs, cs].astype(F32)
        low = grad.astype(BF16)
        slope[rs, cs] = low
        part = jnp.sum(low.astype(F32), axis=0, keepdims=True)
        total = part if total is None else total + part
    vec_sum[0:1, 5 * D + j * cols : 5 * D + (j + 1) * cols] = total
    value = dot(columns(act, cs), grad_branch[...], TN)
    grad_down[j] = value.astype(BF16).reshape(grad_down.shape[1:])


def feed_back_up(j, low_t, grad_pre, up_w, grad_first, grad_up, rows=512):
    n = grad_up.shape[0]
    cols = FF // n
    cs = pl.ds(j * cols, cols)
    value = dot(low_t[...], grad_pre[:, cs])
    grad_up[:, :, :, :, cs] = value.astype(BF16).reshape(grad_up.shape[:4] + (cols,))
    weight = columns(up_w, cs)
    for i in range(grad_pre.shape[0] // rows):
        rs = pl.ds(i * rows, rows)
        grad_first[rs, :] += dot(grad_pre[rs, cs], weight, NT)


def first_norm_back(grad_first, normed, inverse, vec, grad_attn, vec_sum, rows=128):
    vec_sum[0:1, 2 * D : 5 * D] = jnp.zeros((1, 3 * D), F32)

    @pl.loop(0, normed.shape[0] // rows)
    def _(i):
        rs = pl.ds(pl.multiple_of(i * rows, rows), rows)
        grad, unit = grad_first[rs, :], normed[rs, :]
        vec_sum[0:1, 3 * D : 4 * D] += jnp.sum(grad * unit, axis=0, keepdims=True)
        vec_sum[0:1, 4 * D : 5 * D] += jnp.sum(grad, axis=0, keepdims=True)
        scaled = grad * vec[0:1, 3 * D : 4 * D]
        resid = inverse[rs, :] * (scaled - mean(scaled) - unit * mean(scaled * unit))
        grad_first[rs, :] = resid
        low = resid.astype(BF16)
        grad_attn[rs, :] = low
        vec_sum[0:1, 2 * D : 3 * D] += jnp.sum(low.astype(F32), axis=0, keepdims=True)


def attend_back(merged, grad_heads, key_bias, lse, grad_merged, length, p):
    per_row = merged.shape[0] // (grad_heads.shape[0] // length)
    base = pair_base(p)

    @pl.loop(0, grad_heads.shape[0] // length)
    def _(r):
        rs = pl.ds(pl.multiple_of(r * length, 128), length)
        zs = pl.ds(r * per_row, per_row)

        def piece(start):
            return merged[zs, :, :, :, pl.ds(base + start, 128)].reshape(length, 128)

        q2 = piece(0) * jnp.asarray(HEAD_DIM**-0.5, BF16)
        k2, v2 = piece(128), piece(256)
        out2 = grad_heads[rs, pl.ds(p * 128, 128)]
        k2t = k2.T
        bias = key_bias[r]
        queries, keys, values = [], [], []
        for h in range(2):
            scores = dot(of_head(k2, h), q2, NT) + bias
            probs = jnp.exp(scores - lse[r, 2 * p + h])
            grad_probs = dot(of_head(v2, h), out2, NT)
            weighted = probs * grad_probs
            delta = jnp.sum(weighted, axis=0, keepdims=True)
            grad_scores = (weighted - probs * delta).astype(BF16)
            queries.append(dot(k2t, grad_scores))
            keys.append(dot(grad_scores, q2))
            values.append(dot(probs.astype(BF16), out2))
        row = lax.broadcasted_iota(jnp.int32, queries[0].shape, 0)
        grad_q = jnp.where(row < HEAD_DIM, queries[0], queries[1]) * HEAD_DIM**-0.5
        lane = lax.broadcasted_iota(jnp.int32, keys[0].shape, 1)
        grad_merged[rs, pl.ds(base, 128)] = grad_q.T.astype(BF16)
        grad_merged[rs, pl.ds(base + 128, 128)] = jnp.where(lane < HEAD_DIM, *keys).astype(BF16)
        grad_merged[rs, pl.ds(base + 256, 128)] = jnp.where(lane < HEAD_DIM, *values).astype(BF16)


def project_back(x_t, grad_merged, grad_qkv, vec_sum, p):
    cs = pl.ds(pair_base(p), 384)
    grad = grad_merged[:, cs]
    total = jnp.sum(grad.astype(F32), axis=0, keepdims=True)
    vec_sum[0:1, p * 128 : (p + 1) * 128] = total[:, :128]
    vec_sum[0:1, D + p * 128 : D + (p + 1) * 128] = total[:, 256:]
    value = dot(x_t[...], grad).astype(BF16)
    grad_qkv[:, :, :, :, cs] = value.reshape(grad_qkv.shape[:4] + (384,))


def backward_kernel(
    x_in, qkv_w, out_w, up_w, down_w, vec_in, merged_in, heads_in, lse_in, normed_in, inverse_in,
    low_in, act_in, slope_in, block_rows, second_in, branch_in, sums_in, key_bias,
    block_out, input_grad, qkv_s, out_s, up_s, down_s, vec_s, norm,
    up_v, down_v, out_v, act, slope, grad_branch, grad_first, low, low_t, x, normed, inverse, lse, vec, sums,
    grad_down, grad_up, grad_out, vec_sum, vec_parts, vec_recv, vec_near, near_sum, far_sum, down_near, *rest,
):
    send, recv, local, free = rest[-4:]
    pool = list(rest[:-4])
    p = Place()
    greet(p.group() + p.columns())
    sems = Sems(send, recv, local)
    part, length = x_in.shape[:2]
    n = down_v.shape[0]
    chunk = FF // n
    wide = 3 * D
    load_one = [sems.here(branch_in, grad_branch), sems.here(low_in, low)]
    load_chunk = [
        [
            sems.here(down_w.at[j], down_v.at[j]),
            sems.here(slope_in.at[:, pl.ds(j * chunk, chunk)], slope.at[:, pl.ds(j * chunk, chunk)]),
            sems.here(act_in.at[:, :, :, :, pl.ds(j * chunk, chunk)], act.at[:, :, :, :, pl.ds(j * chunk, chunk)]),
        ]
        for j in range(n)
    ]
    load_two = [sems.here(up_w, up_v), sems.here(second_in, grad_first), sems.here(sums_in, sums)]
    load_three = [
        sems.here(normed_in, normed),
        sems.here(inverse_in, inverse),
        sems.here(vec_in, vec),
        sems.here(out_w, out_v),
        sems.here(lse_in, lse),
        sems.here(x_in, x),
    ]
    load_merged = [sems.here(merged_in, act.at[:, :, :, :, pl.ds(0, wide)])]
    load_heads = [sems.here(heads_in, grad_branch)]
    load_qkv = [sems.here(qkv_w, up_v.at[:, :, :, :, pl.ds(0, wide)])]
    grad_rows = grad_branch
    moves = {"out": rows_to_tokens(p, sems, block_rows, block_out)}
    move_grad = rows_to_tokens(p, sems, grad_rows.reshape(x.shape), input_grad)

    rows = out_v.shape[3]
    grad_qkv = act.at[:, :, :, pl.ds(0, rows), pl.ds(0, wide)]
    down_cols = D // len([name for name, _ in SCATTER if name[0] == "down"])

    def nearby(slot, i):
        row, col = (i // 2) * rows, (i % 2) * 384
        return down_v.at[:, :, :, slot, pl.ds(row, rows), pl.ds(col, 384)]

    places = {
        "down": lambda g: lambda core: grad_down.at[:, :, :, core, :, pl.ds(g * down_cols, down_cols)],
        "up": lambda g: lambda core: grad_up.at[:, :, :, :, lanes(g * chunk + core * (chunk // 2), chunk // 2)],
        "out": lambda g: lambda core: grad_out.at[:, :, :, :, lanes(core * (D // 2), D // 2)],
        "qkv": lambda g: lambda core: act.at[:, :, :, pl.ds(0, rows), lanes(core * (wide // 2) + g * 384, 384)],
    }
    nears = {
        "down": lambda g: down_near.at[:, :, :, :, pl.ds(g * down_cols, down_cols)],
        "up": lambda g: nearby(0, g),
        "out": lambda g: nearby(1, 3),
        "qkv": lambda g: nearby(1, g),
    }
    items = {}
    for (name, g), order in SCATTER:
        items[name, g] = Scatter(p, sems, places[name](g), nears[name](g), pool[:4], order)
        pool = pool[4:]
    last = []

    def close(key):
        (name, g), final = key, items[key].final
        if name == "down":
            copies = [sems.here(final, down_s.at[:, pl.ds(g * down_cols, down_cols)])]
        else:
            own = rows // 2
            if name == "qkv":
                parts = [(qkv_s, s * 128, s * D + (2 * g + p.c) * 128, 128) for s in range(3)]
            elif name == "out":
                parts = [(out_s, 0, p.c * (D // 2), D // 2)]
            else:
                parts = [(up_s, 0, g * chunk + p.c * (chunk // 2), chunk // 2)]
            copies = []
            for shard, start, to, size in parts:
                spot = shard.at[:, lanes(to, size)]
                copies.append(sems.here(final.at[pl.ds(p.c * own, own), pl.ds(start, size)], spot))
                copies.append(
                    sems.remote(final.at[pl.ds((1 - p.c) * own, own), pl.ds(start, size)], spot, p.core)
                )
        begin(copies)
        last.extend(copies)

    plan = iter(BACKWARD_PLAN)

    def go():
        for key, stage in next(plan):
            if key in moves:
                begin(moves[key])
            else:
                items[key].advance(stage)
                if stage == 4:
                    close(key)

    begin(load_one)
    for copies in load_chunk:
        begin(copies)
    begin(load_two + load_three)
    finish(load_one)
    low_t[...] = low[...].T
    for j in range(n):
        finish(load_chunk[j])
        feed_back_down(j, grad_branch, down_v, act, slope, grad_down, vec_sum)
    pl.semaphore_signal(free, inc=1, device_id=p.core, device_id_type=MESH)
    begin(load_merged + load_heads)
    finish(load_two)
    for j in range(n):
        go()
        if j == 1:
            pl.semaphore_wait(free, 1)
        feed_back_up(j, low_t, slope, up_v, grad_first, grad_up)
    begin(load_qkv)
    finish(load_three)
    go()
    grad_attn = low
    first_norm_back(grad_first, normed, inverse, vec, grad_attn, vec_sum)
    go()
    finish(load_heads)
    grad_out[...] = dot(grad_branch[...], grad_attn[...], TN).astype(BF16).reshape(grad_out.shape)
    go()
    grad_heads = grad_branch
    for i in range(grad_attn.shape[0] // 512):
        rs = pl.ds(i * 512, 512)
        grad_heads[rs, :] = dot(grad_attn[rs, :], matrix(out_v), NT).astype(BF16)
    x_t = low_t
    x_t[...] = matrix(x).T
    finish(load_merged)
    for g in range(PAIRS // 2):
        for pair in (2 * g, 2 * g + 1):
            go()
            attend_back(act, grad_heads, key_bias, lse, slope, length, pair)
            go()
            project_back(x_t, slope, grad_qkv, vec_sum, pair)
    go()
    vec_sum[0:1, 5 * D + FF :] = jnp.zeros((1, 3 * D), F32)
    for k in range(3):
        vec_sum[0:1, 5 * D + FF + k * D : 5 * D + FF + (k + 1) * D] = sums[k : k + 1, :]
    tiles = vec_sum.shape[1] // (128 * p.ndp)
    for d in range(p.ndp):
        for k in range(tiles):
            vec_parts[d, k : k + 1, :] = vec_sum[0:1, pl.ds((d * tiles + k) * 128, 128)]
        vec_parts[d, tiles:, :] = jnp.zeros((vec_parts.shape[1] - tiles, 128), F32)
    vec_one = [
        sems.remote(vec_parts.at[(p.dp + k) % p.ndp], vec_recv.at[p.dp], ((p.dp + k) % p.ndp, p.sq))
        for k in range(1, p.ndp)
    ]
    begin(vec_one)
    vec_recv[p.dp] = vec_parts[p.dp]
    finish(load_qkv)
    for k in (2, 3, 1, 0):
        to = (p.sq + k) % p.nsq
        for r in range(part):
            rs = pl.ds(pl.multiple_of(r * length + to * (length // p.nsq), 128), length // p.nsq)
            value = dot(slope[rs, pl.ds(0, wide)], columns(up_v, pl.ds(0, wide)), NT)
            grad_rows[rs, :] = (grad_first[rs, :] + value).astype(BF16)
        begin([move_grad[k]])
        go()
    finish(vec_one)
    value = vec_recv[0]
    for k in range(1, p.ndp):
        value = value + vec_recv[k]
    vec_near[p.sq] = value
    near = vec_near.at[p.sq]
    vec_two = [sems.remote(near, near, to) for to in p.group()]
    begin(vec_two)
    go()
    finish(vec_two)
    value = vec_near[0]
    for k in range(1, p.nsq):
        value = value + vec_near[k]
    vec_s[...] = value

    def squares(value):
        return jnp.sum(jnp.sum(value * value, axis=0, keepdims=True), axis=1, keepdims=True)

    total = squares(value) * (1.0 / p.nsq)
    for item in items.values():
        total = total + squares(item.final[...])
    near_sum[p.sq] = jnp.broadcast_to(total, near_sum.shape[1:])
    near = near_sum.at[p.sq]
    spread = [sems.remote(near, near, to) for to in p.group()]
    begin(spread)
    finish(spread)
    total = near_sum[0]
    for k in range(1, p.nsq):
        total = total + near_sum[k]
    far_sum[p.dp] = total
    far = far_sum.at[p.dp]
    spread = [sems.remote(far, far, to) for to in p.columns()]
    begin(spread)
    finish(spread)
    total = far_sum[0]
    for k in range(1, p.ndp):
        total = total + far_sum[k]
    norm[...] = jnp.sqrt(total)
    finish(last + moves["out"] + move_grad)


def backward(saved, key_bias):
    (x, qkv_w, out_w, up_w, down_w, vec, merged, heads, lse, normed, inverse, low, act, slope, block, second,
     grad_branch, sums) = saved
    ndp, nsq = lax.axis_size("dp"), lax.axis_size("seq")
    nz = ndp // 2
    part, full, width = x.shape
    count = part * full
    grid = qkv_w.shape[:3]
    rows, low_rows = qkv_w.shape[3], down_w.shape[4]
    merged = merged.reshape(grid + (count // math.prod(grid), 3 * width))
    act = act.reshape(grid + (count // math.prod(grid), FF))
    block = block.reshape(x.shape)
    token_shape = (part * nsq, full // nsq, width)
    any_space = pl.BlockSpec(memory_space=pl.ANY)
    vmem = pl.BlockSpec(memory_space=pltpu.VMEM)
    vec_tile = (16, 128)
    shapes = [jax.ShapeDtypeStruct(token_shape, BF16)] * 2
    shapes += [jax.ShapeDtypeStruct((rows // 2, w.shape[4]), F32) for w in (qkv_w, out_w, up_w)]
    shapes += [jax.ShapeDtypeStruct((low_rows, width), F32), jax.ShapeDtypeStruct(vec_tile, F32)]
    shapes += [jax.ShapeDtypeStruct((8, 128), F32)]

    def like(array):
        return pltpu.VMEM(array.shape, array.dtype)

    scratch = [like(a) for a in (up_w, down_w, out_w, act, slope, grad_branch, second, low)]
    scratch += [pltpu.VMEM((width, count), BF16)]
    scratch += [like(a) for a in (x, normed, inverse, lse, vec, sums, down_w, up_w, out_w, vec)]
    scratch += [pltpu.VMEM((ndp,) + vec_tile, F32)] * 2 + [pltpu.VMEM((nsq,) + vec_tile, F32)]
    scratch += [pltpu.VMEM((nsq, 8, 128), F32), pltpu.VMEM((ndp, 8, 128), F32)]
    scratch += [pltpu.VMEM(grid + (low_rows, width), BF16)]
    down_cols = width // len([name for name, _ in SCATTER if name[0] == "down"])
    for (name, _), order in SCATTER:
        scratch += scatter_buffers((low_rows, down_cols) if name == "down" else (rows, 384), nz, order)
    scratch += [pltpu.SemaphoreType.DMA((128,)), pltpu.SemaphoreType.DMA((128,)), pltpu.SemaphoreType.DMA((64,))]
    scratch += [pltpu.SemaphoreType.REGULAR]
    return pl.pallas_call(
        backward_kernel,
        out_shape=shapes,
        in_specs=[any_space] * 18 + [vmem],
        out_specs=[any_space] * 6 + [vmem, vmem],
        scratch_shapes=scratch,
        compiler_params=pltpu.CompilerParams(
            collective_id=2, has_side_effects=True, vmem_limit_bytes=VMEM_LIMIT
        ),
    )(
        x, qkv_w, out_w, up_w, down_w, vec, merged, heads, lse, normed, inverse, low, act, slope, block, second,
        grad_branch, sums, key_bias,
    )


def unpack(vector):
    return (
        vector[:D],
        vector[D : 2 * D],
        vector[2 * D : 3 * D],
        vector[3 * D : 4 * D],
        vector[4 * D : 5 * D],
        vector[5 * D : 5 * D + FF],
        vector[5 * D + FF : 6 * D + FF],
        vector[6 * D + FF : 7 * D + FF],
        vector[7 * D + FF : 8 * D + FF],
    )


def normalize(hidden, gain_vec, shift_vec):
    centre = hidden - jnp.mean(hidden, axis=-1, keepdims=True)
    inverse = lax.rsqrt(jnp.mean(centre * centre, axis=-1, keepdims=True) + NORM_EPS)
    normed = centre * inverse
    return (normed * gain_vec + shift_vec, normed, inverse)


def normalize_back(grad_out, normed, inverse, gain_vec):
    scaled = grad_out * gain_vec
    centred = scaled - jnp.mean(scaled, axis=-1, keepdims=True)
    return inverse * (centred - normed * jnp.mean(scaled * normed, axis=-1, keepdims=True))


def gelu_exact(values):
    return jax.nn.gelu(values, approximate=False)


def split_parts(packed_rows):
    full_len = packed_rows.shape[0]
    group_count = packed_rows.shape[-1] // (3 * HEAD_DIM)
    parts = packed_rows.reshape(full_len, 3, group_count, HEAD_DIM)
    return (parts[:, 0], parts[:, 1], parts[:, 2])


def row_probs(queries, key_rows, key_mask):
    scale = 1.0 / math.sqrt(HEAD_DIM)
    scores = jnp.einsum("qhd,khd->hqk", queries, key_rows, preferred_element_type=F32) * scale
    scores = jnp.where(key_mask[None, None, :], scores, MASK_FILL)
    row_peak = jnp.max(scores, axis=-1, keepdims=True)
    row_exp = jnp.exp(scores - row_peak)
    return row_exp / jnp.sum(row_exp, axis=-1, keepdims=True)


def whole_row(packed):
    packed_rows, key_mask = packed
    queries, key_rows, value_rows = split_parts(packed_rows)
    attn_probs = row_probs(queries, key_rows, key_mask)
    mixed_rows = jnp.einsum("hqk,khd->qhd", attn_probs.astype(BF16), value_rows, preferred_element_type=F32)
    return mixed_rows.astype(BF16).reshape(packed_rows.shape[0], D)


def whole_back(packed):
    packed_rows, grad_rows, key_mask = packed
    full_len = packed_rows.shape[0]
    queries, key_rows, value_rows = split_parts(packed_rows)
    grad_mixed = grad_rows.reshape(full_len, HEADS, HEAD_DIM)
    attn_probs = row_probs(queries, key_rows, key_mask)
    grad_probs = jnp.einsum("qhd,khd->hqk", grad_mixed, value_rows, preferred_element_type=F32)
    row_delta = jnp.sum(attn_probs * grad_probs, axis=-1, keepdims=True)
    grad_scores = (attn_probs * (grad_probs - row_delta)).astype(BF16)
    scale = 1.0 / math.sqrt(HEAD_DIM)
    grad_query = jnp.einsum("hqk,khd->qhd", grad_scores, key_rows, preferred_element_type=F32) * scale
    grad_key = jnp.einsum("hqk,qhd->khd", grad_scores, queries, preferred_element_type=F32) * scale
    grad_value = jnp.einsum("hqk,qhd->khd", attn_probs.astype(BF16), grad_mixed, preferred_element_type=F32)
    stacked = jnp.stack([grad_query, grad_key, grad_value], axis=1).astype(BF16)
    return stacked.reshape(full_len, 3 * D)


def adam_step(master, gradient, moment_one, second, factor, decay_rate, step_rate):
    clipped = gradient * factor
    first_new = BETA_ONE * moment_one + (1.0 - BETA_ONE) * clipped
    second_new = BETA_TWO * second + (1.0 - BETA_TWO) * clipped * clipped
    first_hat = first_new / (1.0 - BETA_ONE**STEP_COUNT)
    second_hat = second_new / (1.0 - BETA_TWO**STEP_COUNT)
    updated = master - step_rate * (first_hat / (jnp.sqrt(second_hat) + ADAM_EPS) + decay_rate * master)
    return (updated, first_new, second_new, updated.astype(BF16))


def layer(rows_in, cot_in, token_weight, lengths, qkv_w, out_w, up_w, down_w, vec_w):
    row_count, full_len, width_d = rows_in.shape
    token_count = row_count * full_len
    bias_q, bias_v, bias_o, gain_one, shift_one, bias_up, bias_down, gain_two, shift_two = unpack(vec_w)
    key_mask = jnp.arange(full_len, dtype=jnp.int32)[None, :] < lengths[:, None]
    flat = rows_in.reshape(token_count, width_d)
    merged = jnp.dot(flat, qkv_w, preferred_element_type=F32)
    merged = (merged + jnp.concatenate([bias_q, jnp.zeros_like(bias_q), bias_v])).astype(BF16)
    merged_rows = merged.reshape(row_count, full_len, 3 * width_d)
    mixed = lax.map(whole_row, (merged_rows, key_mask)).reshape(token_count, width_d)
    attn_out = jnp.dot(mixed, out_w, preferred_element_type=F32) + bias_o
    first_out, normed_one, inverse_one = normalize(flat.astype(F32) + attn_out, gain_one, shift_one)
    first_low = first_out.astype(BF16)
    pre_act = jnp.dot(first_low, up_w, preferred_element_type=F32) + bias_up
    activated, gelu_pull = jax.vjp(gelu_exact, pre_act)
    act_low = activated.astype(BF16)
    branch = jnp.dot(act_low, down_w, preferred_element_type=F32) + bias_down
    result, normed_two, inverse_two = normalize(first_out + branch, gain_two, shift_two)
    block_out = result.astype(BF16).reshape(row_count, full_len, width_d)
    grad_result = cot_in.astype(F32) * (token_weight * key_mask.astype(F32))[:, :, None]
    grad_result = grad_result.reshape(token_count, width_d)
    grad_gain_two = jnp.sum(grad_result * normed_two, axis=0)
    grad_shift_two = jnp.sum(grad_result, axis=0)
    grad_second = normalize_back(grad_result, normed_two, inverse_two, gain_two)
    grad_branch = grad_second.astype(BF16)
    grad_bias_down = jnp.sum(grad_branch, axis=0, dtype=F32)
    grad_down = jnp.einsum("tf,td->fd", act_low, grad_branch, preferred_element_type=F32)
    grad_act = jnp.einsum("td,fd->tf", grad_branch, down_w, preferred_element_type=F32)
    grad_pre = gelu_pull(grad_act)[0].astype(BF16)
    grad_bias_up = jnp.sum(grad_pre, axis=0, dtype=F32)
    grad_up = jnp.einsum("td,tf->df", first_low, grad_pre, preferred_element_type=F32)
    grad_first = grad_second + jnp.einsum("tf,df->td", grad_pre, up_w, preferred_element_type=F32)
    grad_gain_one = jnp.sum(grad_first * normed_one, axis=0)
    grad_shift_one = jnp.sum(grad_first, axis=0)
    grad_resid = normalize_back(grad_first, normed_one, inverse_one, gain_one)
    grad_attn = grad_resid.astype(BF16)
    grad_bias_o = jnp.sum(grad_attn, axis=0, dtype=F32)
    grad_out = jnp.einsum("td,te->de", mixed, grad_attn, preferred_element_type=F32)
    grad_mixed = jnp.einsum("te,de->td", grad_attn, out_w, preferred_element_type=F32).astype(BF16)
    grad_merged = lax.map(
        whole_back, (merged_rows, grad_mixed.reshape(row_count, full_len, width_d), key_mask)
    ).reshape(token_count, 3 * width_d)
    grad_qkv = jnp.einsum("td,te->de", flat, grad_merged, preferred_element_type=F32)
    column_sums = jnp.sum(grad_merged, axis=0, dtype=F32)
    input_grad = grad_resid + jnp.einsum("te,de->td", grad_merged, qkv_w, preferred_element_type=F32)
    input_grad = input_grad.astype(BF16).reshape(row_count, full_len, width_d)
    grad_vec = jnp.concatenate(
        [
            column_sums[:width_d],
            column_sums[2 * width_d :],
            grad_bias_o,
            grad_gain_one,
            grad_shift_one,
            grad_bias_up,
            grad_bias_down,
            grad_gain_two,
            grad_shift_two,
        ]
    )
    low = [g.astype(BF16) for g in (grad_qkv, grad_out, grad_up, grad_down)]
    return block_out, input_grad, *low, grad_vec


def body(
    tokens, cotangent, token_weight, lengths,
    qkv_master, out_master, up_master, down_master, vec_master,
    qkv_first, out_first, up_first, down_first, vec_first,
    qkv_second, out_second, up_second, down_second, vec_second,
):
    ndp, nsq = lax.axis_size("dp"), lax.axis_size("seq")
    devices = ndp * nsq
    row_count, local_len, width_d = tokens.shape
    full_len, part = local_len * nsq, row_count // nsq
    vec_size = vec_master.shape[0]
    sq = lax.axis_index("seq")
    my_lengths = lax.dynamic_slice_in_dim(lengths, sq * part, part)
    both = ("dp", "seq")
    chip = 2 * qkv_master.shape[0]
    own_kernels = (
        qkv_master.shape[0] % 8 == 0
        and down_master.shape[0] % 16 == 0
        and nsq == 4
        and ndp % 2 == 0
        and vec_size * nsq % 128 == 0
        and part * full_len // (ndp * nsq // 2) >= chip
        and local_len == 128
    )
    if own_kernels:
        position = sq * local_len + jnp.arange(local_len, dtype=jnp.int32)
        live = token_weight * (position[None, :] < lengths[:, None])
        key_bias = jnp.where(jnp.arange(full_len)[None, :, None] < my_lengths[:, None, None], 0.0, MASK_FILL)
        spread = jnp.zeros((16 * 128,), F32)
        spread = lax.dynamic_update_slice(spread, vec_master, (sq * vec_size,)).reshape(16, 128)
        key_bias = key_bias.astype(F32)
        saved = forward(
            tokens, cotangent, live, qkv_master, out_master, up_master, down_master, spread, key_bias
        )
        block_out, input_grad, *shards, vec_s, norm = backward(saved, key_bias)
        shards.append(lax.dynamic_slice(vec_s.reshape(-1), (sq * vec_size,), (vec_size,)))
        norm_value = norm[0, 0]
    else:
        rows_in, cot_in = (
            lax.all_to_all(a, "seq", split_axis=0, concat_axis=1, tiled=True) for a in (tokens, cotangent)
        )
        weights = lax.all_gather(token_weight, "seq", axis=0)
        qkv_w, out_w, up_w, down_w, vec_w = (
            lax.all_gather(m.astype(BF16), both, axis=0, tiled=True)
            for m in (qkv_master, out_master, up_master, down_master, vec_master)
        )
        my_weight = lax.dynamic_slice_in_dim(weights, sq * part, part, axis=1)
        my_weight = my_weight.transpose(1, 0, 2).reshape(part, full_len)
        block_rows, grad_rows, *grads, grad_vec = layer(
            rows_in, cot_in, my_weight, my_lengths, qkv_w, out_w, up_w, down_w, vec_w.astype(F32)
        )
        block_out, input_grad = (
            lax.all_to_all(a, "seq", split_axis=1, concat_axis=0, tiled=True) for a in (block_rows, grad_rows)
        )
        shards = [lax.psum_scatter(g.astype(F32), both, scatter_dimension=0, tiled=True) for g in grads]
        shards.append(lax.psum_scatter(grad_vec, both, scatter_dimension=0, tiled=True))
        norm_value = jnp.sqrt(lax.psum(sum(jnp.sum(s * s) for s in shards), both))
    factor = CLIP_NORM / jnp.maximum(norm_value, CLIP_NORM)
    outs = [block_out, input_grad, norm_value]
    for master, shard, first, second, decay, rate in (
        (qkv_master, shards[0], qkv_first, qkv_second, WEIGHT_DECAY, LEARN_RATE),
        (out_master, shards[1], out_first, out_second, WEIGHT_DECAY, LEARN_RATE),
        (up_master, shards[2], up_first, up_second, WEIGHT_DECAY, LEARN_RATE),
        (down_master, shards[3], down_first, down_second, WEIGHT_DECAY, LEARN_RATE),
        (vec_master, shards[4], vec_first, vec_second, 0.0, VEC_RATE),
    ):
        outs += adam_step(master, shard, first, second, factor, decay, rate)
    return tuple(outs)


def solution(mesh):
    tokens, both, flat = P("dp", "seq", None), P(("dp", "seq"), None), P(("dp", "seq"))
    weights = (both, both, both, both, flat)
    in_specs = (tokens, tokens, P("dp", "seq"), P("dp")) + 3 * weights
    out_specs = (tokens, tokens, P()) + 4 * (both,) * 4 + (flat,) * 4
    return jax.shard_map(body, mesh=mesh, in_specs=in_specs, out_specs=out_specs, check_vma=False)
```

```python
import functools
import math

import jax
import jax.numpy as jnp
from jax import lax
from jax.experimental import pallas as pl
from jax.experimental.pallas import tpu as pltpu
from jax.sharding import PartitionSpec as P

D = 768
HEADS = 12
HEAD_DIM = 64
FF = 3072
STEP_COUNT = 10
CLIP_NORM = 1.0
BETA_ONE = 0.9
BETA_TWO = 0.999
LEARN_RATE = 0.05
VEC_RATE = 0.3
WEIGHT_DECAY = 0.01
ADAM_EPS = 1e-08
NORM_EPS = 1e-05
MASK_FILL = -1e30
MESH = pl.DeviceIdType.MESH
F32 = jnp.float32
BF16 = jnp.bfloat16
VMEM_LIMIT = 62 << 20


class Place:
    def __init__(self):
        self.ndp, self.nsq = lax.axis_size("dp"), lax.axis_size("seq")
        self.dp, self.sq = lax.axis_index("dp"), lax.axis_index("seq")
        self.z, self.y = self.dp // 2, self.dp % 2
        self.x, self.c = self.sq // 2, self.sq % 2
        self.nz = self.ndp // 2
        self.core = (self.dp, self.x * 2 + 1 - self.c)
        self.across_x = (self.dp, (1 - self.x) * 2 + self.c)
        self.across_y = (self.z * 2 + 1 - self.y, self.sq)

    def along_z(self, k):
        return (self.z + k) % self.nz

    def at_z(self, z):
        return (z * 2 + self.y, self.sq)

    def group(self):
        return [(self.dp, (self.sq + k) % self.nsq) for k in range(1, self.nsq)]

    def columns(self):
        return [((self.dp + k) % self.ndp, self.sq) for k in range(1, self.ndp)]


def greet(targets):
    barrier = pltpu.get_barrier_semaphore()
    for target in targets:
        pl.semaphore_signal(barrier, inc=1, device_id=target, device_id_type=MESH)
    pl.semaphore_wait(barrier, len(targets))


class Sems:
    def __init__(self, send, recv, local):
        self.send, self.recv, self.local = send, recv, local
        self.n = self.m = 0

    def remote(self, src, dst, target):
        i = self.n
        self.n += 1
        return pltpu.make_async_remote_copy(
            src_ref=src,
            dst_ref=dst,
            send_sem=self.send.at[i],
            recv_sem=self.recv.at[i],
            device_id=target,
            device_id_type=MESH,
        )

    def here(self, src, dst):
        i = self.m
        self.m += 1
        return pltpu.make_async_copy(src, dst, self.local.at[i])


def begin(copies):
    for copy in copies:
        copy.start()


def finish(copies):
    for copy in copies:
        copy.wait()


GATHER = (
    (('qkv', 0), 'zxy'),
    (('qkv', 1), 'xzy'),
    (('up', 0), 'yzx'),
    (('out', 0), 'zyx'),
    (('qkv', 2), 'xzy'),
    (('up', 2), 'zyx'),
    (('down', 0), 'zyx'),
    (('up', 1), 'xzy'),
    (('up', 3), 'zxy'),
    (('down', 2), 'xzy'),
    (('down', 1), 'xyz'),
)
SCATTER = (
    (('up', 2), 'yxz'),
    (('qkv', 2), 'yzx'),
    (('down', 0), 'yxz'),
    (('up', 3), 'xyz'),
    (('qkv', 1), 'yxz'),
    (('qkv', 0), 'yxz'),
    (('up', 0), 'yxz'),
    (('up', 1), 'xzy'),
    (('down', 1), 'zyx'),
    (('out', 0), 'xyz'),
)
FORWARD_PLAN = (
    ((('qkv', 0), 0), (('qkv', 1), 0), (('qkv', 2), 0)),
    ((('up', 0), 0), (('out', 0), 0), (('up', 2), 0), (('up', 1), 0)),
    (('tokA', 0), ('tokB', 0), (('down', 2), 0), (('qkv', 1), 1), (('qkv', 0), 1), (('up', 0), 1), (('out', 0), 1), (('qkv', 2), 1), (('up', 2), 1), (('qkv', 0), 2), (('out', 0), 2), (('qkv', 1), 2), (('down', 0), 0), (('up', 2), 2), (('down', 1), 0), (('up', 1), 1), (('up', 3), 0), (('qkv', 0), 3), (('qkv', 2), 2), (('up', 0), 2), (('down', 2), 1), (('qkv', 0), 4)),
    ((('out', 0), 3),),
    ((('qkv', 1), 3), (('down', 0), 1)),
    (),
    ((('out', 0), 4),),
    ((('up', 3), 1), (('qkv', 1), 4)),
    ((('qkv', 2), 3), (('down', 1), 1)),
    ((('up', 2), 3),),
    (),
    ((('qkv', 2), 4), (('down', 0), 2), (('up', 1), 2)),
    (),
    ((('up', 0), 3), (('up', 2), 4), (('down', 1), 2)),
    ((('up', 3), 2),),
    (),
    (('cotA', 0), ('cotB', 0), (('up', 0), 4)),
    (),
    (),
    (),
    ((('up', 1), 3), (('down', 2), 2), (('down', 0), 3), (('up', 1), 4)),
    ((('up', 3), 3),),
    ((('down', 0), 4), (('down', 1), 3), (('up', 3), 4)),
    ((('down', 2), 3),),
    ((('down', 1), 4),),
    ((('down', 2), 4),),
    (),
)
BACKWARD_PLAN = (
    (('outA', 0), (('down', 0), 0), (('down', 1), 0)),
    (),
    ((('up', 0), 0), (('up', 1), 0)),
    (),
    (('outB', 0), (('up', 2), 0), (('down', 0), 1), (('up', 3), 0), (('down', 1), 1), (('up', 0), 1), (('up', 1), 1)),
    ((('up', 2), 1), (('up', 3), 1)),
    ((('out', 0), 0),),
    (),
    (),
    (),
    (),
    ((('qkv', 0), 0),),
    ((('up', 0), 2), (('up', 1), 2), (('out', 0), 1), (('up', 3), 2)),
    ((('up', 2), 2), (('qkv', 0), 1)),
    (),
    ((('qkv', 1), 0),),
    ((('down', 0), 2), (('up', 3), 3), (('qkv', 1), 1), (('up', 0), 3), (('down', 1), 2), (('up', 2), 3)),
    (),
    ((('qkv', 0), 2), (('up', 1), 3)),
    ((('qkv', 2), 0),),
    ((('down', 0), 3), (('up', 3), 4), (('down', 1), 3), (('out', 0), 2), (('up', 2), 4), (('qkv', 2), 1), (('up', 0), 4), (('up', 1), 4), (('qkv', 0), 3)),
    (),
    (),
    ((('qkv', 1), 2), (('down', 1), 4)),
    ((('out', 0), 3), (('qkv', 0), 4), (('down', 0), 4), (('qkv', 2), 2), (('out', 0), 4), (('qkv', 1), 3), (('qkv', 2), 3), (('qkv', 1), 4), (('qkv', 2), 4)),
)
PAIRS = HEADS // 2
NT = (((1,), (1,)), ((), ()))
TN = (((0,), (0,)), ((), ()))
NN = (((1,), (0,)), ((), ()))
def dot(a, b, dims=NN):
    return lax.dot_general(a, b, dims, preferred_element_type=F32)


def lanes(start, size):
    return pl.ds(pl.multiple_of(start, 128), size)


def mean(values):
    return jnp.sum(values, axis=-1, keepdims=True) * (1.0 / D)


def matrix(ref, *index):
    value = ref[index] if index else ref[...]
    return value.reshape(-1, value.shape[-1])


def columns(ref, cols):
    value = ref[:, :, :, :, cols]
    return value.reshape(-1, value.shape[-1])


class Gather:
    def __init__(self, place, sems, at, order):
        p = place
        spot = {"z": p.z, "y": p.y, "x": p.x}
        self.stages = []
        for axis in order:
            here = at(**spot)
            if axis == "z":
                targets = [p.at_z(p.along_z(k)) for k in range(1, p.nz)]
            else:
                targets = [p.across_x if axis == "x" else p.across_y]
            self.stages.append([sems.remote(here, here, target) for target in targets])
            spot[axis] = slice(None)
        here = at(**spot)
        self.stages.append([sems.remote(here, here, p.core)])

    def advance(self, stage):
        if stage:
            finish(self.stages[stage - 1])
        if stage < len(self.stages):
            begin(self.stages[stage])


class Scatter:
    def __init__(self, place, sems, at, near, bufs, order):
        p = place
        *bufs, final = bufs
        total = at(p.c)
        self.final = final
        self.stages = [[sems.remote(at(1 - p.c), near, p.core)]]
        sizes = {"z": p.nz, "y": 2, "x": 2}
        own = {"z": p.z, "y": p.y, "x": p.x}
        spot = {axis: slice(None) for axis in "zyx"}
        left = [axis for axis in "zyx"]

        def index(spot):
            return (spot["z"], spot["y"], spot["x"])

        self.after = [functools.partial(add_into, total, [near], [sizes[axis] for axis in left])]
        for buf, axis in zip(bufs, order):
            if axis == "z":
                targets = [(p.along_z(k), p.at_z(p.along_z(k)), buf.at[k - 1]) for k in range(1, p.nz)]
            elif axis == "y":
                targets = [(1 - p.y, p.across_y, buf)]
            else:
                targets = [(1 - p.x, p.across_x, buf)]
            self.stages.append(
                [sems.remote(total.at[index({**spot, axis: to})], into, device) for to, device, into in targets]
            )
            spot[axis] = own[axis]
            left.remove(axis)
            extra = [into for _, _, into in targets]
            kept = total.at[index(spot)]
            if left:
                self.after.append(functools.partial(add_into, kept, extra, [sizes[axis] for axis in left]))
            else:
                self.after.append(functools.partial(add_last, final, kept, extra))

    def advance(self, stage):
        if stage:
            finish(self.stages[stage - 1])
            self.after[stage - 1]()
        if stage < len(self.stages):
            begin(self.stages[stage])


def add_into(total, extra, lead):
    def one(i, carry):
        spot = []
        for size in reversed(lead):
            spot.insert(0, i % size)
            i = i // size
        spot = tuple(spot)
        value = total[spot].astype(F32)
        for part in extra:
            value = value + part[spot].astype(F32)
        total[spot] = value.astype(total.dtype)
        return carry

    lax.fori_loop(0, math.prod(lead), one, 0)


def add_last(final, total, extra):
    value = total[...].astype(F32)
    for part in extra:
        value = value + part[...].astype(F32)
    final[...] = value


def scatter_buffers(block, nz, order):
    sizes = {"z": nz, "y": 2, "x": 2}
    left, bufs = list("zyx"), []
    for axis in order:
        left.remove(axis)
        lead = tuple(sizes[a] for a in left)
        if axis == "z":
            lead = (nz - 1,) + lead
        bufs.append(pltpu.VMEM(lead + block, BF16))
    return bufs + [pltpu.VMEM(block, F32)]


def tokens_to_rows(place, sems, src, dst):
    p = place
    part, length = dst.shape[0], src.shape[1]
    spot = dst.at[:, pl.ds(p.sq * length, length)]
    copies = [sems.here(src.at[pl.ds(p.sq * part, part)], spot)]
    for k in range(1, p.nsq):
        to = (p.sq + k) % p.nsq
        copies.append(sems.remote(src.at[pl.ds(to * part, part)], spot, (p.dp, to)))
    return copies


def rows_to_tokens(place, sems, src, dst):
    p = place
    part, length = src.shape[0], dst.shape[1]
    spot = dst.at[pl.ds(p.sq * part, part)]
    copies = [sems.here(src.at[:, pl.ds(p.sq * length, length)], spot)]
    for k in range(1, p.nsq):
        to = (p.sq + k) % p.nsq
        copies.append(sems.remote(src.at[:, pl.ds(to * length, length)], spot, (p.dp, to)))
    return copies


def of_head(values, h):
    lane = lax.broadcasted_iota(jnp.int32, values.shape, 1)
    own = lane < HEAD_DIM if h == 0 else lane >= HEAD_DIM
    return jnp.where(own, values, jnp.zeros_like(values))


def pair_base(p):
    return (p % 2) * (3 * D // 2) + (p // 2) * (3 * 128)


def project(x, w, bias, merged, p, rows=512):
    cs = pl.ds(pair_base(p), 384)
    part = columns(w, cs)
    for i in range(x.shape[0] // rows):
        rs = pl.ds(i * rows, rows)
        merged[rs, cs] = (dot(x[rs, :], part) + bias[0:1, cs]).astype(BF16)


def key_bias(lengths, row, count):
    key = lax.broadcasted_iota(jnp.int32, (count, 1), 0)
    return jnp.where(key < lengths[row], 0.0, MASK_FILL).astype(F32)


def attend(merged, lengths, first_row, heads_out, lse, length, p):
    base = pair_base(p)
    pair = range(2)
    for r in range(heads_out.shape[0] // length):
        rs = pl.ds(r * length, length)
        q2 = merged[rs, pl.ds(base, 128)] * jnp.asarray(HEAD_DIM**-0.5, BF16)
        k2 = merged[rs, pl.ds(base + 128, 128)]
        v2t = merged[rs, pl.ds(base + 256, 128)].T
        bias = key_bias(lengths, first_row + r, length)
        scores = [dot(of_head(k2, h), q2, NT) for h in pair]
        weights, totals = [], []
        for h in pair:
            biased = scores[h] + bias
            peak = jnp.max(biased, axis=0, keepdims=True)
            value = jnp.exp(biased - peak)
            total = jnp.sum(value, axis=0, keepdims=True)
            lse[r, 2 * p + h] = peak + jnp.log(total)
            weights.append(value.astype(BF16))
            totals.append(total)
        own = [v2t[HEAD_DIM * h : HEAD_DIM * (h + 1)] for h in pair]
        mixed = jnp.concatenate([dot(own[h], weights[h]) * (1.0 / totals[h]) for h in pair], axis=0)
        heads_out[rs, pl.ds(p * 128, 128)] = mixed.T.astype(BF16)


def first_norm(x, heads_out, w, vec, normed, inverse, low, start, count, rows=512):
    @pl.loop(0, count // rows)
    def _(i):
        rs = pl.ds(pl.multiple_of(start + i * rows, rows), rows)
        hidden = x[rs, :].astype(F32) + (dot(heads_out[rs, :], matrix(w)) + vec[0:1, 2 * D : 3 * D])
        centre = hidden - mean(hidden)
        scale = lax.rsqrt(mean(centre * centre) + NORM_EPS)
        unit = centre * scale
        normed[rs, :] = unit
        inverse[rs, :] = scale
        low[rs, :] = (unit * vec[0:1, 3 * D : 4 * D] + vec[0:1, 4 * D : 5 * D]).astype(BF16)


def feed_up(j, low, up_w, vec, act, slope, chunk, rows=256):
    cs = pl.ds(j * chunk, chunk)
    bias = vec[0:1, 5 * D + j * chunk : 5 * D + (j + 1) * chunk]

    @pl.loop(0, low.shape[0] // (2 * rows))
    def _(i):
        weight = columns(up_w, cs)
        for k in range(2):
            rs = pl.ds(pl.multiple_of((2 * i + k) * rows, rows), rows)
            value = dot(low[rs, :], weight) + bias
            cdf = 0.5 + 0.5 * lax.erf(value * 0.5**0.5)
            bell = jnp.exp(-0.5 * (value * value)) * (2 * math.pi) ** -0.5
            act[rs, cs] = (value * cdf).astype(BF16)
            slope[rs, cs] = (cdf + value * bell).astype(slope.dtype)


def feed_down(act, down_w, branch, cs, rows=512):
    weight = down_w[:, :, :, :, :, cs]
    weight = weight.reshape(-1, weight.shape[-1])
    for i in range(act.shape[0] // rows):
        rs = pl.ds(i * rows, rows)
        branch[rs, cs] = dot(act[rs, :], weight)


def second_norm(normed, vec, branch, cot, weight, block_out, grad_branch, sums, rows=256):
    sums[...] = jnp.zeros_like(sums)
    at = 5 * D + FF
    gain_one, shift_one, bias_down = (vec[0:1, s : s + D] for s in (3 * D, 4 * D, at))
    gain_two, shift_two = (vec[0:1, s : s + D] for s in (at + D, at + 2 * D))

    @pl.loop(0, normed.shape[0] // rows)
    def _(i):
        rs = pl.ds(pl.multiple_of(i * rows, rows), rows)
        hidden = normed[rs, :] * gain_one + shift_one + (branch[rs, :] + bias_down)
        centre = hidden - mean(hidden)
        scale = lax.rsqrt(mean(centre * centre) + NORM_EPS)
        unit = centre * scale
        block_out[rs, :] = (unit * gain_two + shift_two).astype(BF16)
        grad = cot[rs, :].astype(F32) * weight[rs, 0:1]
        sums[1:2, :] += jnp.sum(grad * unit, axis=0, keepdims=True)
        sums[2:3, :] += jnp.sum(grad, axis=0, keepdims=True)
        scaled = grad * gain_two
        second = scale * (scaled - mean(scaled) - unit * mean(scaled * unit))
        normed[rs, :] = second
        low = second.astype(BF16)
        grad_branch[rs, :] = low
        sums[0:1, :] += jnp.sum(low.astype(F32), axis=0, keepdims=True)


def forward_kernel(
    tokens, cotangent, weight, qkv_m, out_m, up_m, down_m, vec_m, lengths,
    x_out, qkv_w, out_w, up_w, down_w, vec_out, merged_out, heads_out, lse_out, normed_out, inverse_out,
    low_out, act_out, slope_out, block_out, second_out, branch_out, sums_out,
    qkv_f, out_f, up_f, down_f,
    qkv_v, out_v, up_v, down_v, x, cot, wt, wt_all, vec_near, vec_far, vec, bias, merged, heads, lse, normed, inverse,
    low, act, slope, branch, grad_branch, sums, send, recv, local,
):
    p = Place()
    greet(p.group() + p.columns())
    sems = Sems(send, recv, local)
    part, length = x.shape[0], x.shape[1]
    moves = {}
    move_tokens = tokens_to_rows(p, sems, tokens, x)
    move_cot = tokens_to_rows(p, sems, cotangent, cot)
    for name, copies in (("tok", move_tokens), ("cot", move_cot)):
        moves[name + "A"], moves[name + "B"] = [copies[2]], [copies[3]]
    spot = wt_all.at[p.sq]
    move_weight = [sems.here(weight, spot)] + [sems.remote(weight, spot, to) for to in p.group()]
    masters = {"qkv": (qkv_m, qkv_f), "out": (out_m, out_f), "up": (up_m, up_f)}
    rows = qkv_m.shape[0]
    mine = pl.ds(p.c * rows, rows)
    fetch = {
        name: [sems.here(master, wide.at[mine]), sems.remote(master, wide.at[mine], p.core)]
        for name, (master, wide) in masters.items()
    }
    fetch["down"] = [sems.here(down_m, down_f)]
    chunk = FF // len([name for name, _ in GATHER if name[0] == "up"])
    down_cols = D // len([name for name, _ in GATHER if name[0] == "down"])
    half = 3 * D // 2
    places = {
        "qkv": lambda g: lambda z, y, x: qkv_v.at[z, y, x, :, lanes(p.c * half + g * 384, 384)],
        "out": lambda g: lambda z, y, x: out_v.at[z, y, x, :, lanes(p.c * (D // 2), D // 2)],
        "up": lambda g: lambda z, y, x: up_v.at[z, y, x, :, lanes(g * chunk + p.c * (chunk // 2), chunk // 2)],
        "down": lambda g: lambda z, y, x: down_v.at[z, y, x, p.c, :, pl.ds(g * down_cols, down_cols)],
    }
    items = {key: Gather(p, sems, places[key[0]](key[1]), order) for key, order in GATHER}
    near = vec_near.at[p.sq]
    vec_one = [sems.remote(near, near, to) for to in p.group()]
    far = vec_far.at[p.dp]
    vec_two = [sems.remote(far, far, to) for to in p.columns()]

    def cast(name):
        finish(fetch[name])
        own = (p.z, p.y, p.x)
        if name == "qkv":
            for g in range(PAIRS // 2):
                for s in range(3):
                    to = lanes(p.c * half + g * 384 + s * 128, 128)
                    qkv_v[own + (slice(None), to)] = qkv_f[:, lanes(s * D + (2 * g + p.c) * 128, 128)].astype(BF16)
        elif name == "out":
            cs = lanes(p.c * (D // 2), D // 2)
            out_v[own + (slice(None), cs)] = out_f[:, cs].astype(BF16)
        elif name == "up":
            for g in range(FF // chunk):
                cs = lanes(g * chunk + p.c * (chunk // 2), chunk // 2)
                up_v[own + (slice(None), cs)] = up_f[:, cs].astype(BF16)
        else:
            down_v[own + (p.c,)] = down_f[...].astype(BF16)

    plan = iter(FORWARD_PLAN)

    def go():
        for key, stage in next(plan):
            if key in moves:
                begin(moves[key])
            else:
                items[key].advance(stage)

    begin(fetch["qkv"])
    vec_near[p.sq] = vec_m[...].astype(BF16).astype(F32)
    begin(fetch["out"] + fetch["up"] + fetch["down"])
    cast("qkv")
    go()
    begin(vec_one + move_weight + move_tokens[:2] + move_cot[:2])
    for name in ("out", "up", "down"):
        cast(name)
    finish(vec_one)
    block = vec_near[0]
    for k in range(1, p.nsq):
        block = block + vec_near[k]
    vec_far[p.dp] = block
    begin(vec_two)
    go()
    finish(vec_two)
    tiles = vec.shape[1] // (128 * p.ndp)
    for d in range(p.ndp):
        for k in range(tiles):
            vec[0:1, pl.ds((d * tiles + k) * 128, 128)] = vec_far[d, k : k + 1, :]
    for pair in range(PAIRS):
        base = pair_base(pair)
        bias[0:1, base : base + 128] = vec[0:1, pair * 128 : (pair + 1) * 128]
        bias[0:1, base + 128 : base + 256] = jnp.zeros((1, 128), F32)
        bias[0:1, base + 256 : base + 384] = vec[0:1, D + pair * 128 : D + (pair + 1) * 128]
    finish(move_weight)
    for r in range(part):
        for k in range(p.nsq):
            row = wt_all[k, pl.ds(p.sq * part + r, 1), :]
            size = row.shape[1]
            live = lax.broadcasted_iota(jnp.int32, (size, size), 0) + k * size < lengths[p.sq * part + r]
            column = jnp.broadcast_to(row, (size, size)).T
            wt[pl.ds(r * length + k * size, size), :] = jnp.where(live, column, 0.0)
    flat = x.reshape(part * length, D)
    keep = {}

    def save(name, src, dst):
        keep[name] = sems.here(src, dst)
        keep[name].start()

    for g in range(PAIRS // 2):
        go()
        if g == 0:
            finish(move_tokens)
            save("x", x, x_out)
        for pair in (2 * g, 2 * g + 1):
            project(flat, qkv_v, bias, merged, pair)
            go()
            attend(merged, lengths, p.sq * part, heads, lse, length, pair)
            go()
    save("qkv", qkv_v, qkv_w)
    save("merged", merged, merged_out)
    save("heads", heads, heads_out)
    save("lse", lse, lse_out)
    go()
    save("out", out_v, out_w)
    first_norm(flat, heads, out_v, vec, normed, inverse, low, 0, part * length // 2)
    go()
    first_norm(flat, heads, out_v, vec, normed, inverse, low, part * length // 2, part * length // 2)
    save("normed", normed, normed_out)
    save("inverse", inverse, inverse_out)
    save("low", low, low_out)
    for j in range(FF // chunk):
        go()
        feed_up(j, low, up_v, vec, act, slope, chunk)
    save("up", up_v, up_w)
    save("act", act, act_out)
    save("slope", slope, slope_out)
    for j in range(D // down_cols):
        go()
        feed_down(act, down_v, branch, pl.ds(j * down_cols, down_cols))
    save("down", down_v, down_w)
    go()
    finish(move_cot)
    keep.pop("heads").wait()
    keep.pop("normed").wait()
    second_norm(normed, vec, branch, cot.reshape(part * length, D), wt, heads, grad_branch, sums)
    save("block", heads, block_out)
    save("second", normed, second_out)
    save("branch", grad_branch, branch_out)
    save("sums", sums, sums_out)
    save("vec", vec, vec_out)
    finish(keep.values())


def forward(tokens, cotangent, weight, qkv_m, out_m, up_m, down_m, vec_m, lengths):
    ndp, nsq = lax.axis_size("dp"), lax.axis_size("seq")
    rows, length, width = tokens.shape
    part, full = rows // nsq, length * nsq
    count = part * full
    chip, low = 2 * qkv_m.shape[0], down_m.shape[0]
    grid = (ndp // 2, 2, nsq // 2)
    vec_len = 8 * D + FF
    any_space = pl.BlockSpec(memory_space=pl.ANY)
    vmem = pl.BlockSpec(memory_space=pltpu.VMEM)

    def both(shape, dtype):
        return jax.ShapeDtypeStruct(shape, dtype), pltpu.VMEM(shape, dtype)

    weights = [both(grid + (chip, m.shape[1]), BF16) for m in (qkv_m, out_m, up_m)]
    weights.append(both(grid + (2, low, width), BF16))
    x = both((part, full, width), BF16)
    vec = both((1, vec_len), F32)
    merged = both((count, 3 * width), BF16)
    heads = both((count, width), BF16)
    lse = both((part, HEADS, 1, full), F32)
    normed = both((count, width), F32)
    inverse = both((count, 1), F32)
    act = both((count, FF), BF16)
    sums = both((8, width), F32)
    outs = [x[0]] + [w[0] for w in weights] + [vec[0], merged[0], heads[0], lse[0], normed[0], inverse[0]]
    outs += [heads[0], act[0], act[0], heads[0], normed[0], heads[0], sums[0]]
    scratch = [pltpu.VMEM((chip, m.shape[1]), F32) for m in (qkv_m, out_m, up_m)] + [pltpu.VMEM(down_m.shape, F32)]
    scratch += [w[1] for w in weights]
    scratch += [x[1], x[1], pltpu.VMEM((count, length), F32), pltpu.VMEM((nsq,) + weight.shape, F32)]
    scratch += [pltpu.VMEM((nsq,) + vec_m.shape, F32), pltpu.VMEM((ndp,) + vec_m.shape, F32), vec[1]]
    scratch += [pltpu.VMEM((1, 3 * width), F32), merged[1], heads[1], lse[1], normed[1], inverse[1]]
    scratch += [heads[1], act[1], act[1], normed[1], heads[1], sums[1]]
    scratch += [pltpu.SemaphoreType.DMA((96,)), pltpu.SemaphoreType.DMA((96,)), pltpu.SemaphoreType.DMA((48,))]
    return pl.pallas_call(
        forward_kernel,
        out_shape=outs,
        in_specs=[any_space] * 7 + [vmem, pl.BlockSpec(memory_space=pltpu.SMEM)],
        out_specs=[any_space] * len(outs),
        scratch_shapes=scratch,
        compiler_params=pltpu.CompilerParams(
            collective_id=1, has_side_effects=True, vmem_limit_bytes=VMEM_LIMIT
        ),
    )(tokens, cotangent, weight, qkv_m, out_m, up_m, down_m, vec_m, lengths)


def feed_back_down(j, grad_branch, down_w, act, slope, grad_down, vec_sum, rows=512):
    n = grad_down.shape[0]
    cols = FF // n
    cs = pl.ds(j * cols, cols)
    weight = matrix(down_w, j)

    total = None
    for i in range(slope.shape[0] // rows):
        rs = pl.ds(i * rows, rows)
        grad = dot(grad_branch[rs, :], weight, NT) * slope[rs, cs].astype(F32)
        low = grad.astype(BF16)
        slope[rs, cs] = low
        part = jnp.sum(low.astype(F32), axis=0, keepdims=True)
        total = part if total is None else total + part
    vec_sum[0:1, 5 * D + j * cols : 5 * D + (j + 1) * cols] = total
    value = dot(columns(act, cs), grad_branch[...], TN)
    grad_down[j] = value.astype(BF16).reshape(grad_down.shape[1:])


def feed_back_up(j, low_t, grad_pre, up_w, grad_first, grad_up, rows=512):
    n = grad_up.shape[0]
    cols = FF // n
    cs = pl.ds(j * cols, cols)
    value = dot(low_t[...], grad_pre[:, cs])
    grad_up[:, :, :, :, cs] = value.astype(BF16).reshape(grad_up.shape[:4] + (cols,))
    weight = columns(up_w, cs)
    for i in range(grad_pre.shape[0] // rows):
        rs = pl.ds(i * rows, rows)
        grad_first[rs, :] += dot(grad_pre[rs, cs], weight, NT)


def first_norm_back(grad_first, normed, inverse, vec, grad_attn, vec_sum, rows=256):
    vec_sum[0:1, 2 * D : 5 * D] = jnp.zeros((1, 3 * D), F32)

    @pl.loop(0, normed.shape[0] // rows)
    def _(i):
        rs = pl.ds(pl.multiple_of(i * rows, rows), rows)
        grad, unit = grad_first[rs, :], normed[rs, :]
        vec_sum[0:1, 3 * D : 4 * D] += jnp.sum(grad * unit, axis=0, keepdims=True)
        vec_sum[0:1, 4 * D : 5 * D] += jnp.sum(grad, axis=0, keepdims=True)
        scaled = grad * vec[0:1, 3 * D : 4 * D]
        resid = inverse[rs, :] * (scaled - mean(scaled) - unit * mean(scaled * unit))
        grad_first[rs, :] = resid
        low = resid.astype(BF16)
        grad_attn[rs, :] = low
        vec_sum[0:1, 2 * D : 3 * D] += jnp.sum(low.astype(F32), axis=0, keepdims=True)


def attend_back(merged, grad_heads, lengths, first_row, lse, grad_merged, length, p):
    per_row = merged.shape[0] // (grad_heads.shape[0] // length)
    base = pair_base(p)
    pair = range(2)

    @pl.loop(0, grad_heads.shape[0] // length)
    def _(r):
        rs = pl.ds(pl.multiple_of(r * length, 128), length)
        zs = pl.ds(r * per_row, per_row)

        def piece(start):
            return merged[zs, :, :, :, pl.ds(base + start, 128)].reshape(length, 128)

        q2 = piece(0) * jnp.asarray(HEAD_DIM**-0.5, BF16)
        k2, v2 = piece(128), piece(256)
        out2 = grad_heads[rs, pl.ds(p * 128, 128)]
        k2t = k2.T
        bias = key_bias(lengths, first_row + r, length)
        scores = [dot(of_head(k2, h), q2, NT) for h in pair]
        grad_probs = [dot(of_head(v2, h), out2, NT) for h in pair]
        low_probs, grad_scores = [], []
        for h in pair:
            probs = jnp.exp(scores[h] + bias - lse[r, 2 * p + h])
            weighted = probs * grad_probs[h]
            delta = jnp.sum(weighted, axis=0, keepdims=True)
            grad_scores.append((weighted - probs * delta).astype(BF16))
            low_probs.append(probs.astype(BF16))
        own = [k2t[HEAD_DIM * h : HEAD_DIM * (h + 1)] for h in pair]
        grad_q = jnp.concatenate([dot(own[h], grad_scores[h]) for h in pair], axis=0) * HEAD_DIM**-0.5
        keys = [dot(grad_scores[h], q2) for h in pair]
        values = [dot(low_probs[h], out2) for h in pair]
        lane = lax.broadcasted_iota(jnp.int32, keys[0].shape, 1)
        grad_merged[rs, pl.ds(base, 128)] = grad_q.T.astype(BF16)
        grad_merged[rs, pl.ds(base + 128, 128)] = jnp.where(lane < HEAD_DIM, *keys).astype(BF16)
        grad_merged[rs, pl.ds(base + 256, 128)] = jnp.where(lane < HEAD_DIM, *values).astype(BF16)


def project_back(x_t, grad_merged, grad_qkv, vec_sum, p):
    cs = pl.ds(pair_base(p), 384)
    grad = grad_merged[:, cs]
    total = jnp.sum(grad.astype(F32), axis=0, keepdims=True)
    vec_sum[0:1, p * 128 : (p + 1) * 128] = total[:, :128]
    vec_sum[0:1, D + p * 128 : D + (p + 1) * 128] = total[:, 256:]
    value = dot(x_t[...], grad).astype(BF16)
    grad_qkv[:, :, :, :, cs] = value.reshape(grad_qkv.shape[:4] + (384,))


def backward_kernel(
    x_in, qkv_w, out_w, up_w, down_w, vec_in, merged_in, heads_in, lse_in, normed_in, inverse_in,
    low_in, act_in, slope_in, block_rows, second_in, branch_in, sums_in, lengths,
    block_out, input_grad, qkv_s, out_s, up_s, down_s, vec_s, norm,
    up_v, down_v, out_v, act, slope, grad_branch, grad_first, low, low_t, x, normed, inverse, lse, vec, sums,
    grad_down, grad_up, grad_out, vec_sum, vec_parts, vec_recv, vec_near, near_sum, far_sum, down_near, *rest,
):
    send, recv, local, free = rest[-4:]
    pool = list(rest[:-4])
    p = Place()
    greet(p.group() + p.columns())
    sems = Sems(send, recv, local)
    part, length = x_in.shape[:2]
    n = down_v.shape[0]
    chunk = FF // n
    wide = 3 * D
    load_one = [sems.here(branch_in, grad_branch), sems.here(low_in, low)]
    load_chunk = [
        [
            sems.here(down_w.at[j], down_v.at[j]),
            sems.here(slope_in.at[:, pl.ds(j * chunk, chunk)], slope.at[:, pl.ds(j * chunk, chunk)]),
            sems.here(act_in.at[:, :, :, :, pl.ds(j * chunk, chunk)], act.at[:, :, :, :, pl.ds(j * chunk, chunk)]),
        ]
        for j in range(n)
    ]
    load_two = [sems.here(up_w, up_v), sems.here(second_in, grad_first), sems.here(sums_in, sums)]
    load_three = [
        sems.here(normed_in, normed),
        sems.here(inverse_in, inverse),
        sems.here(vec_in, vec),
        sems.here(out_w, out_v),
        sems.here(lse_in, lse),
        sems.here(x_in, x),
    ]
    load_merged = [sems.here(merged_in, act.at[:, :, :, :, pl.ds(0, wide)])]
    load_heads = [sems.here(heads_in, grad_branch)]
    load_qkv = [sems.here(qkv_w, up_v.at[:, :, :, :, pl.ds(0, wide)])]
    grad_rows = grad_branch
    move_out = rows_to_tokens(p, sems, block_rows, block_out)
    moves = {"outA": [move_out[2]], "outB": [move_out[3]]}
    move_grad = rows_to_tokens(p, sems, grad_rows.reshape(x.shape), input_grad)

    rows = out_v.shape[3]
    grad_qkv = act.at[:, :, :, pl.ds(0, rows), pl.ds(0, wide)]
    down_cols = D // len([name for name, _ in SCATTER if name[0] == "down"])

    def nearby(slot, i):
        row, col = (i // 2) * rows, (i % 2) * 384
        return down_v.at[:, :, :, slot, pl.ds(row, rows), pl.ds(col, 384)]

    places = {
        "down": lambda g: lambda core: grad_down.at[:, :, :, core, :, pl.ds(g * down_cols, down_cols)],
        "up": lambda g: lambda core: grad_up.at[:, :, :, :, lanes(g * chunk + core * (chunk // 2), chunk // 2)],
        "out": lambda g: lambda core: grad_out.at[:, :, :, :, lanes(core * (D // 2), D // 2)],
        "qkv": lambda g: lambda core: act.at[:, :, :, pl.ds(0, rows), lanes(core * (wide // 2) + g * 384, 384)],
    }
    nears = {
        "down": lambda g: down_near.at[:, :, :, :, pl.ds(g * down_cols, down_cols)],
        "up": lambda g: nearby(0, g),
        "out": lambda g: nearby(1, 3),
        "qkv": lambda g: nearby(1, g),
    }
    items = {}
    for (name, g), order in SCATTER:
        items[name, g] = Scatter(p, sems, places[name](g), nears[name](g), pool[:4], order)
        pool = pool[4:]
    last = []

    def close(key):
        (name, g), final = key, items[key].final
        if name == "down":
            copies = [sems.here(final, down_s.at[:, pl.ds(g * down_cols, down_cols)])]
        else:
            own = rows // 2
            if name == "qkv":
                parts = [(qkv_s, s * 128, s * D + (2 * g + p.c) * 128, 128) for s in range(3)]
            elif name == "out":
                parts = [(out_s, 0, p.c * (D // 2), D // 2)]
            else:
                parts = [(up_s, 0, g * chunk + p.c * (chunk // 2), chunk // 2)]
            copies = []
            for shard, start, to, size in parts:
                spot = shard.at[:, lanes(to, size)]
                copies.append(sems.here(final.at[pl.ds(p.c * own, own), pl.ds(start, size)], spot))
                copies.append(
                    sems.remote(final.at[pl.ds((1 - p.c) * own, own), pl.ds(start, size)], spot, p.core)
                )
        begin(copies)
        last.extend(copies)

    plan = iter(BACKWARD_PLAN)

    def go():
        for key, stage in next(plan):
            if key in moves:
                begin(moves[key])
            else:
                items[key].advance(stage)
                if stage == 4:
                    close(key)

    begin(load_one)
    for copies in load_chunk:
        begin(copies)
    begin(load_two + load_three + move_out[:2])
    finish(load_one)
    low_t[...] = low[...].T
    for j in range(n):
        finish(load_chunk[j])
        feed_back_down(j, grad_branch, down_v, act, slope, grad_down, vec_sum)
    pl.semaphore_signal(free, inc=1, device_id=p.core, device_id_type=MESH)
    begin(load_merged + load_heads)
    finish(load_two)
    for j in range(n):
        go()
        if j == 1:
            pl.semaphore_wait(free, 1)
        feed_back_up(j, low_t, slope, up_v, grad_first, grad_up)
    begin(load_qkv)
    finish(load_three)
    go()
    grad_attn = low
    first_norm_back(grad_first, normed, inverse, vec, grad_attn, vec_sum)
    go()
    finish(load_heads)
    grad_out[...] = dot(grad_branch[...], grad_attn[...], TN).astype(BF16).reshape(grad_out.shape)
    go()
    grad_heads = grad_branch
    for i in range(grad_attn.shape[0] // 512):
        rs = pl.ds(i * 512, 512)
        grad_heads[rs, :] = dot(grad_attn[rs, :], matrix(out_v), NT).astype(BF16)
    x_t = low_t
    x_t[...] = matrix(x).T
    finish(load_merged)
    for g in range(PAIRS // 2):
        for pair in (2 * g, 2 * g + 1):
            go()
            attend_back(act, grad_heads, lengths, p.sq * part, lse, slope, length, pair)
            go()
            project_back(x_t, slope, grad_qkv, vec_sum, pair)
    go()
    vec_sum[0:1, 5 * D + FF :] = jnp.zeros((1, 3 * D), F32)
    for k in range(3):
        vec_sum[0:1, 5 * D + FF + k * D : 5 * D + FF + (k + 1) * D] = sums[k : k + 1, :]
    tiles = vec_sum.shape[1] // (128 * p.ndp)
    for d in range(p.ndp):
        for k in range(tiles):
            vec_parts[d, k : k + 1, :] = vec_sum[0:1, pl.ds((d * tiles + k) * 128, 128)]
        vec_parts[d, tiles:, :] = jnp.zeros((vec_parts.shape[1] - tiles, 128), F32)
    vec_one = [
        sems.remote(vec_parts.at[(p.dp + k) % p.ndp], vec_recv.at[p.dp], ((p.dp + k) % p.ndp, p.sq))
        for k in range(1, p.ndp)
    ]
    begin(vec_one)
    vec_recv[p.dp] = vec_parts[p.dp]
    finish(load_qkv)
    for k in (2, 3, 1, 0):
        to = (p.sq + k) % p.nsq
        for r in range(part):
            rs = pl.ds(pl.multiple_of(r * length + to * (length // p.nsq), 128), length // p.nsq)
            value = dot(slope[rs, pl.ds(0, wide)], columns(up_v, pl.ds(0, wide)), NT)
            grad_rows[rs, :] = (grad_first[rs, :] + value).astype(BF16)
        begin([move_grad[k]])
        go()
    finish(vec_one)
    value = vec_recv[0]
    for k in range(1, p.ndp):
        value = value + vec_recv[k]
    vec_near[p.sq] = value
    near = vec_near.at[p.sq]
    vec_two = [sems.remote(near, near, to) for to in p.group()]
    begin(vec_two)
    go()
    finish(vec_two)
    value = vec_near[0]
    for k in range(1, p.nsq):
        value = value + vec_near[k]
    vec_s[...] = value

    def squares(value):
        return jnp.sum(jnp.sum(value * value, axis=0, keepdims=True), axis=1, keepdims=True)

    total = squares(value) * (1.0 / p.nsq)
    for item in items.values():
        total = total + squares(item.final[...])
    near_sum[p.sq] = jnp.broadcast_to(total, near_sum.shape[1:])
    near = near_sum.at[p.sq]
    spread = [sems.remote(near, near, to) for to in p.group()]
    begin(spread)
    finish(spread)
    total = near_sum[0]
    for k in range(1, p.nsq):
        total = total + near_sum[k]
    far_sum[p.dp] = total
    far = far_sum.at[p.dp]
    spread = [sems.remote(far, far, to) for to in p.columns()]
    begin(spread)
    finish(spread)
    total = far_sum[0]
    for k in range(1, p.ndp):
        total = total + far_sum[k]
    norm[...] = jnp.sqrt(total)
    finish(last + move_out + move_grad)


def backward(saved, lengths):
    (x, qkv_w, out_w, up_w, down_w, vec, merged, heads, lse, normed, inverse, low, act, slope, block, second,
     grad_branch, sums) = saved
    ndp, nsq = lax.axis_size("dp"), lax.axis_size("seq")
    nz = ndp // 2
    part, full, width = x.shape
    count = part * full
    grid = qkv_w.shape[:3]
    rows, low_rows = qkv_w.shape[3], down_w.shape[4]
    merged = merged.reshape(grid + (count // math.prod(grid), 3 * width))
    act = act.reshape(grid + (count // math.prod(grid), FF))
    block = block.reshape(x.shape)
    token_shape = (part * nsq, full // nsq, width)
    any_space = pl.BlockSpec(memory_space=pl.ANY)
    vmem = pl.BlockSpec(memory_space=pltpu.VMEM)
    vec_tile = (16, 128)
    shapes = [jax.ShapeDtypeStruct(token_shape, BF16)] * 2
    shapes += [jax.ShapeDtypeStruct((rows // 2, w.shape[4]), F32) for w in (qkv_w, out_w, up_w)]
    shapes += [jax.ShapeDtypeStruct((low_rows, width), F32), jax.ShapeDtypeStruct(vec_tile, F32)]
    shapes += [jax.ShapeDtypeStruct((8, 128), F32)]

    def like(array):
        return pltpu.VMEM(array.shape, array.dtype)

    scratch = [like(a) for a in (up_w, down_w, out_w, act, slope, grad_branch, second, low)]
    scratch += [pltpu.VMEM((width, count), BF16)]
    scratch += [like(a) for a in (x, normed, inverse, lse, vec, sums, down_w, up_w, out_w, vec)]
    scratch += [pltpu.VMEM((ndp,) + vec_tile, F32)] * 2 + [pltpu.VMEM((nsq,) + vec_tile, F32)]
    scratch += [pltpu.VMEM((nsq, 8, 128), F32), pltpu.VMEM((ndp, 8, 128), F32)]
    scratch += [pltpu.VMEM(grid + (low_rows, width), BF16)]
    down_cols = width // len([name for name, _ in SCATTER if name[0] == "down"])
    for (name, _), order in SCATTER:
        scratch += scatter_buffers((low_rows, down_cols) if name == "down" else (rows, 384), nz, order)
    scratch += [pltpu.SemaphoreType.DMA((128,)), pltpu.SemaphoreType.DMA((128,)), pltpu.SemaphoreType.DMA((64,))]
    scratch += [pltpu.SemaphoreType.REGULAR]
    return pl.pallas_call(
        backward_kernel,
        out_shape=shapes,
        in_specs=[any_space] * 18 + [pl.BlockSpec(memory_space=pltpu.SMEM)],
        out_specs=[any_space] * 6 + [vmem, vmem],
        scratch_shapes=scratch,
        compiler_params=pltpu.CompilerParams(
            collective_id=2, has_side_effects=True, vmem_limit_bytes=VMEM_LIMIT
        ),
    )(
        x, qkv_w, out_w, up_w, down_w, vec, merged, heads, lse, normed, inverse, low, act, slope, block, second,
        grad_branch, sums, lengths,
    )


def adam_kernel(norm, *refs):
    ins, outs, bufs, sems = refs[:16], refs[16:32], refs[32:64], refs[64]
    factor = CLIP_NORM / jnp.maximum(norm[0:1, 0:1], CLIP_NORM)
    loads = [pltpu.make_async_copy(ref, buf, sems.at[i]) for i, (ref, buf) in enumerate(zip(ins, bufs))]
    stores = [pltpu.make_async_copy(buf, ref, sems.at[16 + i]) for i, (ref, buf) in enumerate(zip(outs, bufs[16:]))]
    begin(loads)
    for k in range(4):
        finish(loads[4 * k : 4 * k + 4])
        master, first, second, shard = (buf[...] for buf in bufs[4 * k : 4 * k + 4])
        for out, value in zip(
            bufs[16 + 4 * k : 20 + 4 * k], adam_step(master, shard, first, second, factor, WEIGHT_DECAY, LEARN_RATE)
        ):
            out[...] = value
        begin(stores[4 * k : 4 * k + 4])
    finish(stores)


def adam_matrices(norm, masters, firsts, seconds, shards):
    args, shapes = [], []
    for master, first, second, shard in zip(masters, firsts, seconds, shards):
        args += [master, first, second, shard]
        shapes += [jax.ShapeDtypeStruct(master.shape, F32)] * 3 + [jax.ShapeDtypeStruct(master.shape, BF16)]
    any_space = pl.BlockSpec(memory_space=pl.ANY)
    return pl.pallas_call(
        adam_kernel,
        out_shape=shapes,
        in_specs=[pl.BlockSpec(memory_space=pltpu.VMEM)] + [any_space] * 16,
        out_specs=[any_space] * 16,
        scratch_shapes=[pltpu.VMEM(a.shape, a.dtype) for a in args + shapes] + [pltpu.SemaphoreType.DMA((32,))],
        compiler_params=pltpu.CompilerParams(vmem_limit_bytes=VMEM_LIMIT),
    )(norm, *args)


def unpack(vector):
    return (
        vector[:D],
        vector[D : 2 * D],
        vector[2 * D : 3 * D],
        vector[3 * D : 4 * D],
        vector[4 * D : 5 * D],
        vector[5 * D : 5 * D + FF],
        vector[5 * D + FF : 6 * D + FF],
        vector[6 * D + FF : 7 * D + FF],
        vector[7 * D + FF : 8 * D + FF],
    )


def normalize(hidden, gain_vec, shift_vec):
    centre = hidden - jnp.mean(hidden, axis=-1, keepdims=True)
    inverse = lax.rsqrt(jnp.mean(centre * centre, axis=-1, keepdims=True) + NORM_EPS)
    normed = centre * inverse
    return (normed * gain_vec + shift_vec, normed, inverse)


def normalize_back(grad_out, normed, inverse, gain_vec):
    scaled = grad_out * gain_vec
    centred = scaled - jnp.mean(scaled, axis=-1, keepdims=True)
    return inverse * (centred - normed * jnp.mean(scaled * normed, axis=-1, keepdims=True))


def gelu_exact(values):
    return jax.nn.gelu(values, approximate=False)


def split_parts(packed_rows):
    full_len = packed_rows.shape[0]
    group_count = packed_rows.shape[-1] // (3 * HEAD_DIM)
    parts = packed_rows.reshape(full_len, 3, group_count, HEAD_DIM)
    return (parts[:, 0], parts[:, 1], parts[:, 2])


def row_probs(queries, key_rows, key_mask):
    scale = 1.0 / math.sqrt(HEAD_DIM)
    scores = jnp.einsum("qhd,khd->hqk", queries, key_rows, preferred_element_type=F32) * scale
    scores = jnp.where(key_mask[None, None, :], scores, MASK_FILL)
    row_peak = jnp.max(scores, axis=-1, keepdims=True)
    row_exp = jnp.exp(scores - row_peak)
    return row_exp / jnp.sum(row_exp, axis=-1, keepdims=True)


def whole_row(packed):
    packed_rows, key_mask = packed
    queries, key_rows, value_rows = split_parts(packed_rows)
    attn_probs = row_probs(queries, key_rows, key_mask)
    mixed_rows = jnp.einsum("hqk,khd->qhd", attn_probs.astype(BF16), value_rows, preferred_element_type=F32)
    return mixed_rows.astype(BF16).reshape(packed_rows.shape[0], D)


def whole_back(packed):
    packed_rows, grad_rows, key_mask = packed
    full_len = packed_rows.shape[0]
    queries, key_rows, value_rows = split_parts(packed_rows)
    grad_mixed = grad_rows.reshape(full_len, HEADS, HEAD_DIM)
    attn_probs = row_probs(queries, key_rows, key_mask)
    grad_probs = jnp.einsum("qhd,khd->hqk", grad_mixed, value_rows, preferred_element_type=F32)
    row_delta = jnp.sum(attn_probs * grad_probs, axis=-1, keepdims=True)
    grad_scores = (attn_probs * (grad_probs - row_delta)).astype(BF16)
    scale = 1.0 / math.sqrt(HEAD_DIM)
    grad_query = jnp.einsum("hqk,khd->qhd", grad_scores, key_rows, preferred_element_type=F32) * scale
    grad_key = jnp.einsum("hqk,qhd->khd", grad_scores, queries, preferred_element_type=F32) * scale
    grad_value = jnp.einsum("hqk,qhd->khd", attn_probs.astype(BF16), grad_mixed, preferred_element_type=F32)
    stacked = jnp.stack([grad_query, grad_key, grad_value], axis=1).astype(BF16)
    return stacked.reshape(full_len, 3 * D)


def adam_step(master, gradient, moment_one, second, factor, decay_rate, step_rate):
    clipped = gradient * factor
    first_new = BETA_ONE * moment_one + (1.0 - BETA_ONE) * clipped
    second_new = BETA_TWO * second + (1.0 - BETA_TWO) * clipped * clipped
    first_hat = first_new / (1.0 - BETA_ONE**STEP_COUNT)
    second_hat = second_new / (1.0 - BETA_TWO**STEP_COUNT)
    updated = master - step_rate * (first_hat / (jnp.sqrt(second_hat) + ADAM_EPS) + decay_rate * master)
    return (updated, first_new, second_new, updated.astype(BF16))


def layer(rows_in, cot_in, token_weight, lengths, qkv_w, out_w, up_w, down_w, vec_w):
    row_count, full_len, width_d = rows_in.shape
    token_count = row_count * full_len
    bias_q, bias_v, bias_o, gain_one, shift_one, bias_up, bias_down, gain_two, shift_two = unpack(vec_w)
    key_mask = jnp.arange(full_len, dtype=jnp.int32)[None, :] < lengths[:, None]
    flat = rows_in.reshape(token_count, width_d)
    merged = jnp.dot(flat, qkv_w, preferred_element_type=F32)
    merged = (merged + jnp.concatenate([bias_q, jnp.zeros_like(bias_q), bias_v])).astype(BF16)
    merged_rows = merged.reshape(row_count, full_len, 3 * width_d)
    mixed = lax.map(whole_row, (merged_rows, key_mask)).reshape(token_count, width_d)
    attn_out = jnp.dot(mixed, out_w, preferred_element_type=F32) + bias_o
    first_out, normed_one, inverse_one = normalize(flat.astype(F32) + attn_out, gain_one, shift_one)
    first_low = first_out.astype(BF16)
    pre_act = jnp.dot(first_low, up_w, preferred_element_type=F32) + bias_up
    activated, gelu_pull = jax.vjp(gelu_exact, pre_act)
    act_low = activated.astype(BF16)
    branch = jnp.dot(act_low, down_w, preferred_element_type=F32) + bias_down
    result, normed_two, inverse_two = normalize(first_out + branch, gain_two, shift_two)
    block_out = result.astype(BF16).reshape(row_count, full_len, width_d)
    grad_result = cot_in.astype(F32) * (token_weight * key_mask.astype(F32))[:, :, None]
    grad_result = grad_result.reshape(token_count, width_d)
    grad_gain_two = jnp.sum(grad_result * normed_two, axis=0)
    grad_shift_two = jnp.sum(grad_result, axis=0)
    grad_second = normalize_back(grad_result, normed_two, inverse_two, gain_two)
    grad_branch = grad_second.astype(BF16)
    grad_bias_down = jnp.sum(grad_branch, axis=0, dtype=F32)
    grad_down = jnp.einsum("tf,td->fd", act_low, grad_branch, preferred_element_type=F32)
    grad_act = jnp.einsum("td,fd->tf", grad_branch, down_w, preferred_element_type=F32)
    grad_pre = gelu_pull(grad_act)[0].astype(BF16)
    grad_bias_up = jnp.sum(grad_pre, axis=0, dtype=F32)
    grad_up = jnp.einsum("td,tf->df", first_low, grad_pre, preferred_element_type=F32)
    grad_first = grad_second + jnp.einsum("tf,df->td", grad_pre, up_w, preferred_element_type=F32)
    grad_gain_one = jnp.sum(grad_first * normed_one, axis=0)
    grad_shift_one = jnp.sum(grad_first, axis=0)
    grad_resid = normalize_back(grad_first, normed_one, inverse_one, gain_one)
    grad_attn = grad_resid.astype(BF16)
    grad_bias_o = jnp.sum(grad_attn, axis=0, dtype=F32)
    grad_out = jnp.einsum("td,te->de", mixed, grad_attn, preferred_element_type=F32)
    grad_mixed = jnp.einsum("te,de->td", grad_attn, out_w, preferred_element_type=F32).astype(BF16)
    grad_merged = lax.map(
        whole_back, (merged_rows, grad_mixed.reshape(row_count, full_len, width_d), key_mask)
    ).reshape(token_count, 3 * width_d)
    grad_qkv = jnp.einsum("td,te->de", flat, grad_merged, preferred_element_type=F32)
    column_sums = jnp.sum(grad_merged, axis=0, dtype=F32)
    input_grad = grad_resid + jnp.einsum("te,de->td", grad_merged, qkv_w, preferred_element_type=F32)
    input_grad = input_grad.astype(BF16).reshape(row_count, full_len, width_d)
    grad_vec = jnp.concatenate(
        [
            column_sums[:width_d],
            column_sums[2 * width_d :],
            grad_bias_o,
            grad_gain_one,
            grad_shift_one,
            grad_bias_up,
            grad_bias_down,
            grad_gain_two,
            grad_shift_two,
        ]
    )
    low = [g.astype(BF16) for g in (grad_qkv, grad_out, grad_up, grad_down)]
    return block_out, input_grad, *low, grad_vec


def body(
    tokens, cotangent, token_weight, lengths,
    qkv_master, out_master, up_master, down_master, vec_master,
    qkv_first, out_first, up_first, down_first, vec_first,
    qkv_second, out_second, up_second, down_second, vec_second,
):
    ndp, nsq = lax.axis_size("dp"), lax.axis_size("seq")
    devices = ndp * nsq
    row_count, local_len, width_d = tokens.shape
    full_len, part = local_len * nsq, row_count // nsq
    vec_size = vec_master.shape[0]
    sq = lax.axis_index("seq")
    my_lengths = lax.dynamic_slice_in_dim(lengths, sq * part, part)
    both = ("dp", "seq")
    chip = 2 * qkv_master.shape[0]
    own_kernels = (
        qkv_master.shape[0] % 8 == 0
        and down_master.shape[0] % 16 == 0
        and nsq == 4
        and ndp % 2 == 0
        and vec_size * nsq % 128 == 0
        and part * full_len // (ndp * nsq // 2) >= chip
        and local_len == 128
    )
    if own_kernels:
        spread = jnp.zeros((16 * 128,), F32)
        spread = lax.dynamic_update_slice(spread, vec_master, (sq * vec_size,)).reshape(16, 128)
        saved = forward(
            tokens, cotangent, token_weight, qkv_master, out_master, up_master, down_master, spread, lengths
        )
        block_out, input_grad, *shards, vec_s, norm = backward(saved, lengths)
        shards.append(lax.dynamic_slice(vec_s.reshape(-1), (sq * vec_size,), (vec_size,)))
        norm_value = norm[0, 0]
        matrices = adam_matrices(
            norm,
            (qkv_master, out_master, up_master, down_master),
            (qkv_first, out_first, up_first, down_first),
            (qkv_second, out_second, up_second, down_second),
            shards[:4],
        )
    else:
        rows_in, cot_in = (
            lax.all_to_all(a, "seq", split_axis=0, concat_axis=1, tiled=True) for a in (tokens, cotangent)
        )
        weights = lax.all_gather(token_weight, "seq", axis=0)
        qkv_w, out_w, up_w, down_w, vec_w = (
            lax.all_gather(m.astype(BF16), both, axis=0, tiled=True)
            for m in (qkv_master, out_master, up_master, down_master, vec_master)
        )
        my_weight = lax.dynamic_slice_in_dim(weights, sq * part, part, axis=1)
        my_weight = my_weight.transpose(1, 0, 2).reshape(part, full_len)
        block_rows, grad_rows, *grads, grad_vec = layer(
            rows_in, cot_in, my_weight, my_lengths, qkv_w, out_w, up_w, down_w, vec_w.astype(F32)
        )
        block_out, input_grad = (
            lax.all_to_all(a, "seq", split_axis=1, concat_axis=0, tiled=True) for a in (block_rows, grad_rows)
        )
        shards = [lax.psum_scatter(g.astype(F32), both, scatter_dimension=0, tiled=True) for g in grads]
        shards.append(lax.psum_scatter(grad_vec, both, scatter_dimension=0, tiled=True))
        norm_value = jnp.sqrt(lax.psum(sum(jnp.sum(s * s) for s in shards), both))
    factor = CLIP_NORM / jnp.maximum(norm_value, CLIP_NORM)
    outs = [block_out, input_grad, norm_value]
    if own_kernels:
        outs += matrices
    else:
        for master, shard, first, second in (
            (qkv_master, shards[0], qkv_first, qkv_second),
            (out_master, shards[1], out_first, out_second),
            (up_master, shards[2], up_first, up_second),
            (down_master, shards[3], down_first, down_second),
        ):
            outs += adam_step(master, shard, first, second, factor, WEIGHT_DECAY, LEARN_RATE)
    outs += adam_step(vec_master, shards[4], vec_first, vec_second, factor, 0.0, VEC_RATE)
    return tuple(outs)


def solution(mesh):
    tokens, both, flat = P("dp", "seq", None), P(("dp", "seq"), None), P(("dp", "seq"))
    weights = (both, both, both, both, flat)
    in_specs = (tokens, tokens, P("dp", "seq"), P("dp")) + 3 * weights
    out_specs = (tokens, tokens, P()) + 4 * (both,) * 4 + (flat,) * 4
    return jax.shard_map(body, mesh=mesh, in_specs=in_specs, out_specs=out_specs, check_vma=False)
```

```python
import functools
import math

import jax
import jax.numpy as jnp
from jax import lax
from jax.experimental import pallas as pl
from jax.experimental.pallas import tpu as pltpu
from jax.sharding import PartitionSpec as P

D = 768
HEADS = 12
HEAD_DIM = 64
FF = 3072
STEP_COUNT = 10
CLIP_NORM = 1.0
BETA_ONE = 0.9
BETA_TWO = 0.999
LEARN_RATE = 0.05
VEC_RATE = 0.3
WEIGHT_DECAY = 0.01
ADAM_EPS = 1e-08
NORM_EPS = 1e-05
MASK_FILL = -1e30
MESH = pl.DeviceIdType.MESH
F32 = jnp.float32
BF16 = jnp.bfloat16
VMEM_LIMIT = 62 << 20


class Place:
    def __init__(self):
        self.ndp, self.nsq = lax.axis_size("dp"), lax.axis_size("seq")
        self.dp, self.sq = lax.axis_index("dp"), lax.axis_index("seq")
        self.z, self.y = self.dp // 2, self.dp % 2
        self.x, self.c = self.sq // 2, self.sq % 2
        self.nz = self.ndp // 2
        self.core = (self.dp, self.x * 2 + 1 - self.c)
        self.across_x = (self.dp, (1 - self.x) * 2 + self.c)
        self.across_y = (self.z * 2 + 1 - self.y, self.sq)

    def along_z(self, k):
        return (self.z + k) % self.nz

    def at_z(self, z):
        return (z * 2 + self.y, self.sq)

    def group(self):
        return [(self.dp, (self.sq + k) % self.nsq) for k in range(1, self.nsq)]

    def columns(self):
        return [((self.dp + k) % self.ndp, self.sq) for k in range(1, self.ndp)]


def greet(targets):
    barrier = pltpu.get_barrier_semaphore()
    for target in targets:
        pl.semaphore_signal(barrier, inc=1, device_id=target, device_id_type=MESH)
    pl.semaphore_wait(barrier, len(targets))


class Sems:
    def __init__(self, send, recv, local):
        self.send, self.recv, self.local = send, recv, local
        self.n = self.m = 0

    def remote(self, src, dst, target):
        i = self.n
        self.n += 1
        return pltpu.make_async_remote_copy(
            src_ref=src,
            dst_ref=dst,
            send_sem=self.send.at[i],
            recv_sem=self.recv.at[i],
            device_id=target,
            device_id_type=MESH,
        )

    def here(self, src, dst):
        i = self.m
        self.m += 1
        return pltpu.make_async_copy(src, dst, self.local.at[i])


def begin(copies):
    for copy in copies:
        copy.start()


def finish(copies):
    for copy in copies:
        copy.wait()


GATHER = (
    (('qkv', 0), 'zxy'),
    (('qkv', 1), 'xzy'),
    (('up', 0), 'yzx'),
    (('out', 0), 'zyx'),
    (('qkv', 2), 'xzy'),
    (('up', 2), 'zyx'),
    (('down', 0), 'zyx'),
    (('up', 1), 'xzy'),
    (('up', 3), 'zxy'),
    (('down', 2), 'xzy'),
    (('down', 1), 'xyz'),
)
SCATTER = (
    (('up', 2), 'yxz'),
    (('qkv', 2), 'yzx'),
    (('down', 0), 'yxz'),
    (('up', 3), 'xyz'),
    (('qkv', 1), 'yxz'),
    (('qkv', 0), 'yxz'),
    (('up', 0), 'yxz'),
    (('up', 1), 'xzy'),
    (('down', 1), 'zyx'),
    (('out', 0), 'xyz'),
)
FORWARD_PLAN = (
    ((('qkv', 0), 0), (('qkv', 1), 0), (('qkv', 2), 0)),
    ((('up', 0), 0), (('out', 0), 0), (('up', 2), 0), (('up', 1), 0)),
    (('tokA', 0), ('tokB', 0), (('down', 2), 0), (('qkv', 1), 1), (('qkv', 0), 1), (('up', 0), 1), (('out', 0), 1), (('qkv', 2), 1), (('up', 2), 1), (('qkv', 0), 2), (('out', 0), 2), (('qkv', 1), 2), (('down', 0), 0), (('up', 2), 2), (('down', 1), 0), (('up', 1), 1), (('up', 3), 0), (('qkv', 0), 3), (('qkv', 2), 2), (('up', 0), 2), (('down', 2), 1), (('qkv', 0), 4)),
    ((('out', 0), 3),),
    ((('qkv', 1), 3), (('down', 0), 1)),
    (),
    ((('out', 0), 4),),
    ((('up', 3), 1), (('qkv', 1), 4)),
    ((('qkv', 2), 3), (('down', 1), 1)),
    ((('up', 2), 3),),
    (),
    ((('qkv', 2), 4), (('down', 0), 2), (('up', 1), 2)),
    (),
    ((('up', 0), 3), (('up', 2), 4), (('down', 1), 2)),
    ((('up', 3), 2),),
    (),
    (('cotA', 0), ('cotB', 0), (('up', 0), 4)),
    (),
    (),
    (),
    ((('up', 1), 3), (('down', 2), 2), (('down', 0), 3), (('up', 1), 4)),
    ((('up', 3), 3),),
    ((('down', 0), 4), (('down', 1), 3), (('up', 3), 4)),
    ((('down', 2), 3),),
    ((('down', 1), 4),),
    ((('down', 2), 4),),
    (),
)
BACKWARD_PLAN = (
    (('outA', 0), (('down', 0), 0), (('down', 1), 0)),
    (),
    ((('up', 0), 0), (('up', 1), 0)),
    (),
    (('outB', 0), (('up', 2), 0), (('down', 0), 1), (('up', 3), 0), (('down', 1), 1), (('up', 0), 1), (('up', 1), 1)),
    ((('up', 2), 1), (('up', 3), 1)),
    ((('out', 0), 0),),
    (),
    (),
    (),
    (),
    ((('qkv', 0), 0),),
    ((('up', 0), 2), (('up', 1), 2), (('out', 0), 1), (('up', 3), 2)),
    ((('up', 2), 2), (('qkv', 0), 1)),
    (),
    ((('qkv', 1), 0),),
    ((('down', 0), 2), (('up', 3), 3), (('qkv', 1), 1), (('up', 0), 3), (('down', 1), 2), (('up', 2), 3)),
    (),
    ((('qkv', 0), 2), (('up', 1), 3)),
    ((('qkv', 2), 0),),
    ((('down', 0), 3), (('up', 3), 4), (('down', 1), 3), (('out', 0), 2), (('up', 2), 4), (('qkv', 2), 1), (('up', 0), 4), (('up', 1), 4), (('qkv', 0), 3)),
    (),
    (),
    ((('qkv', 1), 2), (('down', 1), 4)),
    ((('out', 0), 3), (('qkv', 0), 4), (('down', 0), 4), (('qkv', 2), 2), (('out', 0), 4), (('qkv', 1), 3), (('qkv', 2), 3), (('qkv', 1), 4), (('qkv', 2), 4)),
)
PAIRS = HEADS // 2
QKV_PARTS = ((0, 0, 3), (1, 0, 3), (2, 0, 3))
NT = (((1,), (1,)), ((), ()))
TN = (((0,), (0,)), ((), ()))
NN = (((1,), (0,)), ((), ()))
def dot(a, b, dims=NN):
    return lax.dot_general(a, b, dims, preferred_element_type=F32)


def lanes(start, size):
    return pl.ds(pl.multiple_of(start, 128), size)


def mean(values):
    return jnp.sum(values, axis=-1, keepdims=True) * (1.0 / D)


def matrix(ref, *index):
    value = ref[index] if index else ref[...]
    return value.reshape(-1, value.shape[-1])


def columns(ref, cols):
    value = ref[:, :, :, :, cols]
    return value.reshape(-1, value.shape[-1])


class Gather:
    def __init__(self, place, sems, at, order):
        p = place
        spot = {"z": p.z, "y": p.y, "x": p.x}
        self.stages = []
        for axis in order:
            here = at(**spot)
            if axis == "z":
                targets = [p.at_z(p.along_z(k)) for k in range(1, p.nz)]
            else:
                targets = [p.across_x if axis == "x" else p.across_y]
            self.stages.append([sems.remote(here, here, target) for target in targets])
            spot[axis] = slice(None)
        here = at(**spot)
        self.stages.append([sems.remote(here, here, p.core)])

    def advance(self, stage):
        if stage:
            finish(self.stages[stage - 1])
        if stage < len(self.stages):
            begin(self.stages[stage])


class Scatter:
    def __init__(self, place, sems, at, near, bufs, order):
        p = place
        *bufs, final = bufs
        total = at(p.c)
        self.final = final
        self.stages = [[sems.remote(at(1 - p.c), near, p.core)]]
        sizes = {"z": p.nz, "y": 2, "x": 2}
        own = {"z": p.z, "y": p.y, "x": p.x}
        spot = {axis: slice(None) for axis in "zyx"}
        left = [axis for axis in "zyx"]

        def index(spot):
            return (spot["z"], spot["y"], spot["x"])

        self.after = [functools.partial(add_into, total, [near], [sizes[axis] for axis in left])]
        for buf, axis in zip(bufs, order):
            if axis == "z":
                targets = [(p.along_z(k), p.at_z(p.along_z(k)), buf.at[k - 1]) for k in range(1, p.nz)]
            elif axis == "y":
                targets = [(1 - p.y, p.across_y, buf)]
            else:
                targets = [(1 - p.x, p.across_x, buf)]
            self.stages.append(
                [sems.remote(total.at[index({**spot, axis: to})], into, device) for to, device, into in targets]
            )
            spot[axis] = own[axis]
            left.remove(axis)
            extra = [into for _, _, into in targets]
            kept = total.at[index(spot)]
            if left:
                self.after.append(functools.partial(add_into, kept, extra, [sizes[axis] for axis in left]))
            else:
                self.after.append(functools.partial(add_last, final, kept, extra))

    def advance(self, stage):
        if stage:
            finish(self.stages[stage - 1])
            self.after[stage - 1]()
        if stage < len(self.stages):
            begin(self.stages[stage])


def add_into(total, extra, lead):
    def one(i, carry):
        spot = []
        for size in reversed(lead):
            spot.insert(0, i % size)
            i = i // size
        spot = tuple(spot)
        if len(extra) == 1:
            total[spot] = total[spot] + extra[0][spot]
            return carry
        value = total[spot].astype(F32)
        for part in extra:
            value = value + part[spot].astype(F32)
        total[spot] = value.astype(total.dtype)
        return carry

    lax.fori_loop(0, math.prod(lead), one, 0)


def add_last(final, total, extra):
    value = total[...].astype(F32)
    for part in extra:
        value = value + part[...].astype(F32)
    final[...] = value


def scatter_buffers(block, nz, order):
    sizes = {"z": nz, "y": 2, "x": 2}
    left, bufs = list("zyx"), []
    for axis in order:
        left.remove(axis)
        lead = tuple(sizes[a] for a in left)
        if axis == "z":
            lead = (nz - 1,) + lead
        bufs.append(pltpu.VMEM(lead + block, BF16))
    return bufs + [pltpu.VMEM(block, F32)]


def tokens_to_rows(place, sems, src, dst):
    p = place
    part, length = dst.shape[0], src.shape[1]
    spot = dst.at[:, pl.ds(p.sq * length, length)]
    copies = [sems.here(src.at[pl.ds(p.sq * part, part)], spot)]
    for k in range(1, p.nsq):
        to = (p.sq + k) % p.nsq
        copies.append(sems.remote(src.at[pl.ds(to * part, part)], spot, (p.dp, to)))
    return copies


def rows_to_tokens(place, sems, src, dst):
    p = place
    part, length = src.shape[0], dst.shape[1]
    spot = dst.at[pl.ds(p.sq * part, part)]
    copies = [sems.here(src.at[:, pl.ds(p.sq * length, length)], spot)]
    for k in range(1, p.nsq):
        to = (p.sq + k) % p.nsq
        copies.append(sems.remote(src.at[:, pl.ds(to * length, length)], spot, (p.dp, to)))
    return copies


def of_head(values, h):
    lane = lax.broadcasted_iota(jnp.int32, values.shape, 1)
    own = lane < HEAD_DIM if h == 0 else lane >= HEAD_DIM
    return jnp.where(own, values, jnp.zeros_like(values))


def pair_base(p):
    return (p % 2) * (3 * D // 2) + (p // 2) * (3 * 128)


def project(x, w, bias, merged, p, rows=512):
    cs = pl.ds(pair_base(p), 384)
    part = columns(w, cs)
    for i in range(x.shape[0] // rows):
        rs = pl.ds(i * rows, rows)
        merged[rs, cs] = (dot(x[rs, :], part) + bias[0:1, cs]).astype(BF16)


def key_bias(lengths, row, count):
    key = lax.broadcasted_iota(jnp.int32, (count, 1), 0)
    return jnp.where(key < lengths[row], 0.0, MASK_FILL).astype(F32)


def attend(merged, lengths, first_row, heads_out, lse, length, p):
    base = pair_base(p)
    pair = range(2)
    for r in range(heads_out.shape[0] // length):
        rs = pl.ds(r * length, length)
        q2 = merged[rs, pl.ds(base, 128)] * jnp.asarray(HEAD_DIM**-0.5, BF16)
        k2 = merged[rs, pl.ds(base + 128, 128)]
        v2t = merged[rs, pl.ds(base + 256, 128)].T
        bias = key_bias(lengths, first_row + r, length)
        scores = [dot(of_head(k2, h), q2, NT) for h in pair]
        weights, totals = [], []
        for h in pair:
            biased = scores[h] + bias
            peak = jnp.max(biased, axis=0, keepdims=True)
            value = jnp.exp(biased - peak)
            total = jnp.sum(value, axis=0, keepdims=True)
            lse[r, 2 * p + h] = peak + jnp.log(total)
            weights.append(value.astype(BF16))
            totals.append(total)
        own = [v2t[HEAD_DIM * h : HEAD_DIM * (h + 1)] for h in pair]
        mixed = jnp.concatenate([dot(own[h], weights[h]) * (1.0 / totals[h]) for h in pair], axis=0)
        heads_out[rs, pl.ds(p * 128, 128)] = mixed.T.astype(BF16)


def first_norm(x, heads_out, w, vec, normed, inverse, low, start, count, rows=512):
    @pl.loop(0, count // rows)
    def _(i):
        rs = pl.ds(pl.multiple_of(start + i * rows, rows), rows)
        hidden = x[rs, :].astype(F32) + (dot(heads_out[rs, :], matrix(w)) + vec[0:1, 2 * D : 3 * D])
        centre = hidden - mean(hidden)
        scale = lax.rsqrt(mean(centre * centre) + NORM_EPS)
        unit = centre * scale
        normed[rs, :] = unit
        inverse[rs, :] = scale
        low[rs, :] = (unit * vec[0:1, 3 * D : 4 * D] + vec[0:1, 4 * D : 5 * D]).astype(BF16)


def feed_up(j, low, up_w, vec, act, slope, chunk, rows=256):
    cs = pl.ds(j * chunk, chunk)
    bias = vec[0:1, 5 * D + j * chunk : 5 * D + (j + 1) * chunk]

    @pl.loop(0, low.shape[0] // (2 * rows))
    def _(i):
        weight = columns(up_w, cs)
        for k in range(2):
            rs = pl.ds(pl.multiple_of((2 * i + k) * rows, rows), rows)
            value = dot(low[rs, :], weight) + bias
            cdf = 0.5 + 0.5 * lax.erf(value * 0.5**0.5)
            bell = jnp.exp(-0.5 * (value * value)) * (2 * math.pi) ** -0.5
            act[rs, cs] = (value * cdf).astype(BF16)
            slope[rs, cs] = (cdf + value * bell).astype(slope.dtype)


def feed_down(act, down_w, branch, cs, rows=512):
    weight = down_w[:, :, :, :, :, cs]
    weight = weight.reshape(-1, weight.shape[-1])
    for i in range(act.shape[0] // rows):
        rs = pl.ds(i * rows, rows)
        branch[rs, cs] = dot(act[rs, :], weight)


def second_norm(normed, vec, branch, cot, weight, block_out, grad_branch, sums, rows=256):
    sums[...] = jnp.zeros_like(sums)
    at = 5 * D + FF
    gain_one, shift_one, bias_down = (vec[0:1, s : s + D] for s in (3 * D, 4 * D, at))
    gain_two, shift_two = (vec[0:1, s : s + D] for s in (at + D, at + 2 * D))

    @pl.loop(0, normed.shape[0] // rows)
    def _(i):
        rs = pl.ds(pl.multiple_of(i * rows, rows), rows)
        hidden = normed[rs, :] * gain_one + shift_one + (branch[rs, :] + bias_down)
        centre = hidden - mean(hidden)
        scale = lax.rsqrt(mean(centre * centre) + NORM_EPS)
        unit = centre * scale
        block_out[rs, :] = (unit * gain_two + shift_two).astype(BF16)
        grad = cot[rs, :].astype(F32) * weight[rs, 0:1]
        sums[1:2, :] += jnp.sum(grad * unit, axis=0, keepdims=True)
        sums[2:3, :] += jnp.sum(grad, axis=0, keepdims=True)
        scaled = grad * gain_two
        second = scale * (scaled - mean(scaled) - unit * mean(scaled * unit))
        normed[rs, :] = second
        low = second.astype(BF16)
        grad_branch[rs, :] = low
        sums[0:1, :] += jnp.sum(low.astype(F32), axis=0, keepdims=True)


def forward_kernel(
    tokens, cotangent, weight, qkv_m, out_m, up_m, down_m, vec_m, lengths,
    x_out, qkv_w, out_w, up_w, down_w, vec_out, merged_out, heads_out, lse_out, normed_out, inverse_out,
    low_out, act_out, slope_out, block_out, second_out, branch_out, sums_out,
    qkv_f, out_f, up_f, down_f,
    qkv_v, out_v, up_v, down_v, x, cot, wt, wt_all, vec_near, vec_far, vec, bias, merged, heads, lse, normed, inverse,
    low, act, slope, branch, grad_branch, sums, send, recv, local,
):
    p = Place()
    greet(p.group() + p.columns())
    sems = Sems(send, recv, local)
    part, length = x.shape[0], x.shape[1]
    moves = {}
    move_tokens = tokens_to_rows(p, sems, tokens, x)
    move_cot = tokens_to_rows(p, sems, cotangent, cot)
    for name, copies in (("tok", move_tokens), ("cot", move_cot)):
        moves[name + "A"], moves[name + "B"] = [copies[2]], [copies[3]]
    spot = wt_all.at[p.sq]
    move_weight = [sems.here(weight, spot)] + [sems.remote(weight, spot, to) for to in p.group()]
    masters = {"qkv": (qkv_m, qkv_f), "out": (out_m, out_f), "up": (up_m, up_f)}
    rows = qkv_m.shape[0]
    mine = pl.ds(p.c * rows, rows)
    fetch = {
        name: [sems.here(master, wide.at[mine]), sems.remote(master, wide.at[mine], p.core)]
        for name, (master, wide) in masters.items()
    }
    fetch["down"] = [sems.here(down_m, down_f)]
    chunk = FF // len([name for name, _ in GATHER if name[0] == "up"])
    down_cols = D // len([name for name, _ in GATHER if name[0] == "down"])
    half = 3 * D // 2
    places = {
        "qkv": lambda g: lambda z, y, x: qkv_v.at[z, y, x, :, lanes(p.c * half + g * 384, 384)],
        "out": lambda g: lambda z, y, x: out_v.at[z, y, x, :, lanes(p.c * (D // 2), D // 2)],
        "up": lambda g: lambda z, y, x: up_v.at[z, y, x, :, lanes(g * chunk + p.c * (chunk // 2), chunk // 2)],
        "down": lambda g: lambda z, y, x: down_v.at[z, y, x, p.c, :, pl.ds(g * down_cols, down_cols)],
    }
    items = {key: Gather(p, sems, places[key[0]](key[1]), order) for key, order in GATHER}
    near = vec_near.at[p.sq]
    vec_one = [sems.remote(near, near, to) for to in p.group()]
    far = vec_far.at[p.dp]
    vec_two = [sems.remote(far, far, to) for to in p.columns()]

    def cast(name):
        finish(fetch[name])
        own = (p.z, p.y, p.x)
        if name == "qkv":
            for g in range(PAIRS // 2):
                for s in range(3):
                    to = lanes(p.c * half + g * 384 + s * 128, 128)
                    qkv_v[own + (slice(None), to)] = qkv_f[:, lanes(s * D + (2 * g + p.c) * 128, 128)].astype(BF16)
        elif name == "out":
            cs = lanes(p.c * (D // 2), D // 2)
            out_v[own + (slice(None), cs)] = out_f[:, cs].astype(BF16)
        elif name == "up":
            for g in range(FF // chunk):
                cs = lanes(g * chunk + p.c * (chunk // 2), chunk // 2)
                up_v[own + (slice(None), cs)] = up_f[:, cs].astype(BF16)
        else:
            down_v[own + (p.c,)] = down_f[...].astype(BF16)

    plan = iter(FORWARD_PLAN)

    def go():
        for key, stage in next(plan):
            if key in moves:
                begin(moves[key])
            else:
                items[key].advance(stage)

    begin(fetch["qkv"])
    vec_near[p.sq] = vec_m[...].astype(BF16).astype(F32)
    begin(fetch["out"] + fetch["up"] + fetch["down"])
    cast("qkv")
    go()
    begin(vec_one + move_weight + move_tokens[:2] + move_cot[:2])
    for name in ("out", "up", "down"):
        cast(name)
    finish(vec_one)
    block = vec_near[0]
    for k in range(1, p.nsq):
        block = block + vec_near[k]
    vec_far[p.dp] = block
    begin(vec_two)
    go()
    finish(vec_two)
    tiles = vec.shape[1] // (128 * p.ndp)
    for d in range(p.ndp):
        for k in range(tiles):
            vec[0:1, pl.ds((d * tiles + k) * 128, 128)] = vec_far[d, k : k + 1, :]
    for pair in range(PAIRS):
        base = pair_base(pair)
        bias[0:1, base : base + 128] = vec[0:1, pair * 128 : (pair + 1) * 128]
        bias[0:1, base + 128 : base + 256] = jnp.zeros((1, 128), F32)
        bias[0:1, base + 256 : base + 384] = vec[0:1, D + pair * 128 : D + (pair + 1) * 128]
    finish(move_weight)
    for r in range(part):
        for k in range(p.nsq):
            row = wt_all[k, pl.ds(p.sq * part + r, 1), :]
            size = row.shape[1]
            live = lax.broadcasted_iota(jnp.int32, (size, size), 0) + k * size < lengths[p.sq * part + r]
            column = jnp.broadcast_to(row, (size, size)).T
            wt[pl.ds(r * length + k * size, size), :] = jnp.where(live, column, 0.0)
    flat = x.reshape(part * length, D)
    keep = {}

    def save(name, src, dst):
        keep[name] = sems.here(src, dst)
        keep[name].start()

    for g in range(PAIRS // 2):
        go()
        if g == 0:
            finish(move_tokens)
            save("x", x, x_out)
        for pair in (2 * g, 2 * g + 1):
            project(flat, qkv_v, bias, merged, pair)
            go()
            attend(merged, lengths, p.sq * part, heads, lse, length, pair)
            go()
    save("qkv", qkv_v, qkv_w)
    save("merged", merged, merged_out)
    save("heads", heads, heads_out)
    save("lse", lse, lse_out)
    go()
    save("out", out_v, out_w)
    first_norm(flat, heads, out_v, vec, normed, inverse, low, 0, part * length // 2)
    go()
    first_norm(flat, heads, out_v, vec, normed, inverse, low, part * length // 2, part * length // 2)
    save("normed", normed, normed_out)
    save("inverse", inverse, inverse_out)
    save("low", low, low_out)
    for j in range(FF // chunk):
        go()
        feed_up(j, low, up_v, vec, act, slope, chunk)
    save("up", up_v, up_w)
    save("act", act, act_out)
    save("slope", slope, slope_out)
    for j in range(D // down_cols):
        go()
        feed_down(act, down_v, branch, pl.ds(j * down_cols, down_cols))
    save("down", down_v, down_w)
    go()
    finish(move_cot)
    keep.pop("heads").wait()
    keep.pop("normed").wait()
    second_norm(normed, vec, branch, cot.reshape(part * length, D), wt, heads, grad_branch, sums)
    save("block", heads, block_out)
    save("second", normed, second_out)
    save("branch", grad_branch, branch_out)
    save("sums", sums, sums_out)
    save("vec", vec, vec_out)
    finish(keep.values())


def forward(tokens, cotangent, weight, qkv_m, out_m, up_m, down_m, vec_m, lengths):
    ndp, nsq = lax.axis_size("dp"), lax.axis_size("seq")
    rows, length, width = tokens.shape
    part, full = rows // nsq, length * nsq
    count = part * full
    chip, low = 2 * qkv_m.shape[0], down_m.shape[0]
    grid = (ndp // 2, 2, nsq // 2)
    vec_len = 8 * D + FF
    any_space = pl.BlockSpec(memory_space=pl.ANY)
    vmem = pl.BlockSpec(memory_space=pltpu.VMEM)

    def both(shape, dtype):
        return jax.ShapeDtypeStruct(shape, dtype), pltpu.VMEM(shape, dtype)

    weights = [both(grid + (chip, m.shape[1]), BF16) for m in (qkv_m, out_m, up_m)]
    weights.append(both(grid + (2, low, width), BF16))
    x = both((part, full, width), BF16)
    vec = both((1, vec_len), F32)
    merged = both((count, 3 * width), BF16)
    heads = both((count, width), BF16)
    lse = both((part, HEADS, 1, full), F32)
    normed = both((count, width), F32)
    inverse = both((count, 1), F32)
    act = both((count, FF), BF16)
    sums = both((8, width), F32)
    outs = [x[0]] + [w[0] for w in weights] + [vec[0], merged[0], heads[0], lse[0], normed[0], inverse[0]]
    outs += [heads[0], act[0], act[0], heads[0], normed[0], heads[0], sums[0]]
    scratch = [pltpu.VMEM((chip, m.shape[1]), F32) for m in (qkv_m, out_m, up_m)] + [pltpu.VMEM(down_m.shape, F32)]
    scratch += [w[1] for w in weights]
    scratch += [x[1], x[1], pltpu.VMEM((count, length), F32), pltpu.VMEM((nsq,) + weight.shape, F32)]
    scratch += [pltpu.VMEM((nsq,) + vec_m.shape, F32), pltpu.VMEM((ndp,) + vec_m.shape, F32), vec[1]]
    scratch += [pltpu.VMEM((1, 3 * width), F32), merged[1], heads[1], lse[1], normed[1], inverse[1]]
    scratch += [heads[1], act[1], act[1], normed[1], heads[1], sums[1]]
    scratch += [pltpu.SemaphoreType.DMA((96,)), pltpu.SemaphoreType.DMA((96,)), pltpu.SemaphoreType.DMA((48,))]
    return pl.pallas_call(
        forward_kernel,
        out_shape=outs,
        in_specs=[any_space] * 7 + [vmem, pl.BlockSpec(memory_space=pltpu.SMEM)],
        out_specs=[any_space] * len(outs),
        scratch_shapes=scratch,
        compiler_params=pltpu.CompilerParams(
            collective_id=1, has_side_effects=True, vmem_limit_bytes=VMEM_LIMIT
        ),
    )(tokens, cotangent, weight, qkv_m, out_m, up_m, down_m, vec_m, lengths)


def feed_back_down(j, grad_branch, down_w, act, slope, grad_down, vec_sum, rows=512):
    n = grad_down.shape[0]
    cols = FF // n
    cs = pl.ds(j * cols, cols)
    weight = matrix(down_w, j)

    total = None
    for i in range(slope.shape[0] // rows):
        rs = pl.ds(i * rows, rows)
        grad = dot(grad_branch[rs, :], weight, NT) * slope[rs, cs].astype(F32)
        low = grad.astype(BF16)
        slope[rs, cs] = low
        part = jnp.sum(low.astype(F32), axis=0, keepdims=True)
        total = part if total is None else total + part
    vec_sum[0:1, 5 * D + j * cols : 5 * D + (j + 1) * cols] = total
    value = dot(columns(act, cs), grad_branch[...], TN)
    grad_down[j] = value.astype(BF16).reshape(grad_down.shape[1:])


def feed_back_up(j, low_t, grad_pre, up_w, grad_first, grad_up, rows=512):
    n = grad_up.shape[0]
    cols = FF // n
    cs = pl.ds(j * cols, cols)
    value = dot(low_t[...], grad_pre[:, cs])
    grad_up[:, :, :, :, cs] = value.astype(BF16).reshape(grad_up.shape[:4] + (cols,))
    weight = columns(up_w, cs)
    for i in range(grad_pre.shape[0] // rows):
        rs = pl.ds(i * rows, rows)
        grad_first[rs, :] += dot(grad_pre[rs, cs], weight, NT)


def first_norm_back(grad_first, normed, inverse, vec, grad_attn, vec_sum, rows=256):
    vec_sum[0:1, 2 * D : 5 * D] = jnp.zeros((1, 3 * D), F32)

    @pl.loop(0, normed.shape[0] // rows)
    def _(i):
        rs = pl.ds(pl.multiple_of(i * rows, rows), rows)
        grad, unit = grad_first[rs, :], normed[rs, :]
        vec_sum[0:1, 3 * D : 4 * D] += jnp.sum(grad * unit, axis=0, keepdims=True)
        vec_sum[0:1, 4 * D : 5 * D] += jnp.sum(grad, axis=0, keepdims=True)
        scaled = grad * vec[0:1, 3 * D : 4 * D]
        resid = inverse[rs, :] * (scaled - mean(scaled) - unit * mean(scaled * unit))
        grad_first[rs, :] = resid
        low = resid.astype(BF16)
        grad_attn[rs, :] = low
        vec_sum[0:1, 2 * D : 3 * D] += jnp.sum(low.astype(F32), axis=0, keepdims=True)


def attend_back(merged, grad_heads, lengths, first_row, lse, grad_merged, length, p):
    per_row = merged.shape[0] // (grad_heads.shape[0] // length)
    base = pair_base(p)
    pair = range(2)

    @pl.loop(0, grad_heads.shape[0] // length)
    def _(r):
        rs = pl.ds(pl.multiple_of(r * length, 128), length)
        zs = pl.ds(r * per_row, per_row)

        def piece(start):
            return merged[zs, :, :, :, pl.ds(base + start, 128)].reshape(length, 128)

        q2 = piece(0) * jnp.asarray(HEAD_DIM**-0.5, BF16)
        k2, v2 = piece(128), piece(256)
        out2 = grad_heads[rs, pl.ds(p * 128, 128)]
        k2t = k2.T
        bias = key_bias(lengths, first_row + r, length)
        scores = [dot(of_head(k2, h), q2, NT) for h in pair]
        grad_probs = [dot(of_head(v2, h), out2, NT) for h in pair]
        low_probs, grad_scores = [], []
        for h in pair:
            probs = jnp.exp(scores[h] + bias - lse[r, 2 * p + h])
            weighted = probs * grad_probs[h]
            delta = jnp.sum(weighted, axis=0, keepdims=True)
            grad_scores.append((weighted - probs * delta).astype(BF16))
            low_probs.append(probs.astype(BF16))
        own = [k2t[HEAD_DIM * h : HEAD_DIM * (h + 1)] for h in pair]
        grad_q = jnp.concatenate([dot(own[h], grad_scores[h]) for h in pair], axis=0) * HEAD_DIM**-0.5
        keys = [dot(grad_scores[h], q2) for h in pair]
        values = [dot(low_probs[h], out2) for h in pair]
        lane = lax.broadcasted_iota(jnp.int32, keys[0].shape, 1)
        grad_merged[rs, pl.ds(base, 128)] = grad_q.T.astype(BF16)
        grad_merged[rs, pl.ds(base + 128, 128)] = jnp.where(lane < HEAD_DIM, *keys).astype(BF16)
        grad_merged[rs, pl.ds(base + 256, 128)] = jnp.where(lane < HEAD_DIM, *values).astype(BF16)


def project_back(x_t, grad_merged, grad_qkv, vec_sum, p):
    cs = pl.ds(pair_base(p), 384)
    grad = grad_merged[:, cs]
    total = jnp.sum(grad.astype(F32), axis=0, keepdims=True)
    vec_sum[0:1, p * 128 : (p + 1) * 128] = total[:, :128]
    vec_sum[0:1, D + p * 128 : D + (p + 1) * 128] = total[:, 256:]
    value = dot(x_t[...], grad).astype(BF16)
    grad_qkv[:, :, :, :, cs] = value.reshape(grad_qkv.shape[:4] + (384,))


def backward_kernel(
    x_in, qkv_w, out_w, up_w, down_w, vec_in, merged_in, heads_in, lse_in, normed_in, inverse_in,
    low_in, act_in, slope_in, block_rows, second_in, branch_in, sums_in, lengths,
    block_out, input_grad, qkv_s, out_s, up_s, down_s, vec_s, norm,
    up_v, down_v, out_v, act, slope, grad_branch, grad_first, low, low_t, x, normed, inverse, lse, vec, sums,
    grad_down, grad_up, grad_out, vec_sum, vec_parts, vec_recv, vec_near, near_sum, far_sum, down_near, *rest,
):
    send, recv, local, free = rest[-4:]
    pool = list(rest[:-4])
    p = Place()
    greet(p.group() + p.columns())
    sems = Sems(send, recv, local)
    part, length = x_in.shape[:2]
    n = down_v.shape[0]
    chunk = FF // n
    wide = 3 * D
    load_one = [sems.here(branch_in, grad_branch)]
    load_chunk = [
        [
            sems.here(down_w.at[j], down_v.at[j]),
            sems.here(slope_in.at[:, pl.ds(j * chunk, chunk)], slope.at[:, pl.ds(j * chunk, chunk)]),
            sems.here(act_in.at[:, :, :, :, pl.ds(j * chunk, chunk)], act.at[:, :, :, :, pl.ds(j * chunk, chunk)]),
        ]
        for j in range(n)
    ]
    load_two = [sems.here(low_in, low), sems.here(up_w, up_v), sems.here(second_in, grad_first), sems.here(sums_in, sums)]
    load_three = [
        sems.here(normed_in, normed),
        sems.here(inverse_in, inverse),
        sems.here(vec_in, vec),
        sems.here(out_w, out_v),
        sems.here(lse_in, lse),
        sems.here(x_in, x),
    ]
    load_merged = [sems.here(merged_in, act.at[:, :, :, :, pl.ds(0, wide)])]
    load_heads = [sems.here(heads_in, grad_branch)]
    load_qkv = [sems.here(qkv_w, up_v.at[:, :, :, :, pl.ds(0, wide)])]
    grad_rows = grad_branch
    move_out = rows_to_tokens(p, sems, block_rows, block_out)
    moves = {"outA": [move_out[2]], "outB": [move_out[3]]}
    move_grad = rows_to_tokens(p, sems, grad_rows.reshape(x.shape), input_grad)

    rows = out_v.shape[3]
    grad_qkv = act.at[:, :, :, pl.ds(0, rows), pl.ds(0, wide)]
    down_cols = D // len([name for name, _ in SCATTER if name[0] == "down"])

    def nearby(slot, i):
        row, col = (i // 2) * rows, (i % 2) * 384
        return down_v.at[:, :, :, slot, pl.ds(row, rows), pl.ds(col, 384)]

    def qkv_span(i):
        group, first, end = QKV_PARTS[i]
        return group * 384 + first * 128, (end - first) * 128

    places = {
        "down": lambda g: lambda core: grad_down.at[:, :, :, core, :, pl.ds(g * down_cols, down_cols)],
        "up": lambda g: lambda core: grad_up.at[:, :, :, :, lanes(g * chunk + core * (chunk // 2), chunk // 2)],
        "out": lambda g: lambda core: grad_out.at[:, :, :, :, lanes(core * (D // 2), D // 2)],
        "qkv": lambda g: lambda core: act.at[
            :, :, :, pl.ds(0, rows), lanes(core * (wide // 2) + qkv_span(g)[0], qkv_span(g)[1])
        ],
    }
    nears = {
        "down": lambda g: down_near.at[:, :, :, :, pl.ds(g * down_cols, down_cols)],
        "up": lambda g: nearby(0, g),
        "out": lambda g: nearby(1, 3),
        "qkv": lambda g: nearby(1, QKV_PARTS[g][0]).at[
            :, :, :, :, pl.ds(QKV_PARTS[g][1] * 128, qkv_span(g)[1])
        ],
    }
    items = {}
    for (name, g), order in SCATTER:
        items[name, g] = Scatter(p, sems, places[name](g), nears[name](g), pool[:4], order)
        pool = pool[4:]
    last = []

    def close(key):
        (name, g), final = key, items[key].final
        if name == "down":
            copies = [sems.here(final, down_s.at[:, pl.ds(g * down_cols, down_cols)])]
        else:
            own = rows // 2
            if name == "qkv":
                group, first, end = QKV_PARTS[g]
                parts = [
                    (qkv_s, (s - first) * 128, s * D + (2 * group + p.c) * 128, 128) for s in range(first, end)
                ]
            elif name == "out":
                parts = [(out_s, 0, p.c * (D // 2), D // 2)]
            else:
                parts = [(up_s, 0, g * chunk + p.c * (chunk // 2), chunk // 2)]
            copies = []
            for shard, start, to, size in parts:
                spot = shard.at[:, lanes(to, size)]
                copies.append(sems.here(final.at[pl.ds(p.c * own, own), pl.ds(start, size)], spot))
                copies.append(
                    sems.remote(final.at[pl.ds((1 - p.c) * own, own), pl.ds(start, size)], spot, p.core)
                )
        begin(copies)
        last.extend(copies)

    plan = iter(BACKWARD_PLAN)

    def go():
        for key, stage in next(plan):
            if key in moves:
                begin(moves[key])
            else:
                items[key].advance(stage)
                if stage == 4:
                    close(key)

    begin(load_one)
    for copies in load_chunk:
        begin(copies)
    begin(load_two + load_three + move_out[:2])
    finish(load_one)
    for j in range(n):
        finish(load_chunk[j])
        feed_back_down(j, grad_branch, down_v, act, slope, grad_down, vec_sum)
    pl.semaphore_signal(free, inc=1, device_id=p.core, device_id_type=MESH)
    begin(load_merged + load_heads)
    finish(load_two)
    for j in range(n):
        go()
        if j == 0:
            low_t[...] = low[...].T
        if j == 1:
            pl.semaphore_wait(free, 1)
        feed_back_up(j, low_t, slope, up_v, grad_first, grad_up)
    begin(load_qkv)
    finish(load_three)
    go()
    grad_attn = low
    first_norm_back(grad_first, normed, inverse, vec, grad_attn, vec_sum)
    go()
    finish(load_heads)
    grad_out[...] = dot(grad_branch[...], grad_attn[...], TN).astype(BF16).reshape(grad_out.shape)
    go()
    grad_heads = grad_branch
    for i in range(grad_attn.shape[0] // 512):
        rs = pl.ds(i * 512, 512)
        grad_heads[rs, :] = dot(grad_attn[rs, :], matrix(out_v), NT).astype(BF16)
    x_t = low_t
    x_t[...] = matrix(x).T
    finish(load_merged)
    for g in range(PAIRS // 2):
        for pair in (2 * g, 2 * g + 1):
            go()
            attend_back(act, grad_heads, lengths, p.sq * part, lse, slope, length, pair)
            go()
            project_back(x_t, slope, grad_qkv, vec_sum, pair)
    go()
    vec_sum[0:1, 5 * D + FF :] = jnp.zeros((1, 3 * D), F32)
    for k in range(3):
        vec_sum[0:1, 5 * D + FF + k * D : 5 * D + FF + (k + 1) * D] = sums[k : k + 1, :]
    tiles = vec_sum.shape[1] // (128 * p.ndp)
    for d in range(p.ndp):
        for k in range(tiles):
            vec_parts[d, k : k + 1, :] = vec_sum[0:1, pl.ds((d * tiles + k) * 128, 128)]
        vec_parts[d, tiles:, :] = jnp.zeros((vec_parts.shape[1] - tiles, 128), F32)
    vec_one = [
        sems.remote(vec_parts.at[(p.dp + k) % p.ndp], vec_recv.at[p.dp], ((p.dp + k) % p.ndp, p.sq))
        for k in range(1, p.ndp)
    ]
    begin(vec_one)
    vec_recv[p.dp] = vec_parts[p.dp]
    finish(load_qkv)
    for k in (2, 3, 1, 0):
        to = (p.sq + k) % p.nsq
        for r in range(part):
            rs = pl.ds(pl.multiple_of(r * length + to * (length // p.nsq), 128), length // p.nsq)
            value = dot(slope[rs, pl.ds(0, wide)], columns(up_v, pl.ds(0, wide)), NT)
            grad_rows[rs, :] = (grad_first[rs, :] + value).astype(BF16)
        begin([move_grad[k]])
        go()
    finish(vec_one)
    value = vec_recv[0]
    for k in range(1, p.ndp):
        value = value + vec_recv[k]
    vec_near[p.sq] = value
    near = vec_near.at[p.sq]
    vec_two = [sems.remote(near, near, to) for to in p.group()]
    begin(vec_two)
    go()
    finish(vec_two)
    value = vec_near[0]
    for k in range(1, p.nsq):
        value = value + vec_near[k]
    for k in range(value.shape[0]):
        vec_s[0:1, k * 128 : (k + 1) * 128] = value[k : k + 1, :]

    def squares(value):
        return jnp.sum(jnp.sum(value * value, axis=0, keepdims=True), axis=1, keepdims=True)

    total = squares(value) * (1.0 / p.nsq)
    for item in items.values():
        total = total + squares(item.final[...])
    near_sum[p.sq] = jnp.broadcast_to(total, near_sum.shape[1:])
    near = near_sum.at[p.sq]
    spread = [sems.remote(near, near, to) for to in p.group()]
    begin(spread)
    finish(spread)
    total = near_sum[0]
    for k in range(1, p.nsq):
        total = total + near_sum[k]
    far_sum[p.dp] = total
    far = far_sum.at[p.dp]
    spread = [sems.remote(far, far, to) for to in p.columns()]
    begin(spread)
    finish(spread)
    total = far_sum[0]
    for k in range(1, p.ndp):
        total = total + far_sum[k]
    norm[...] = jnp.sqrt(total)
    finish(last + move_out + move_grad)


def backward(saved, lengths):
    (x, qkv_w, out_w, up_w, down_w, vec, merged, heads, lse, normed, inverse, low, act, slope, block, second,
     grad_branch, sums) = saved
    ndp, nsq = lax.axis_size("dp"), lax.axis_size("seq")
    nz = ndp // 2
    part, full, width = x.shape
    count = part * full
    grid = qkv_w.shape[:3]
    rows, low_rows = qkv_w.shape[3], down_w.shape[4]
    merged = merged.reshape(grid + (count // math.prod(grid), 3 * width))
    act = act.reshape(grid + (count // math.prod(grid), FF))
    block = block.reshape(x.shape)
    token_shape = (part * nsq, full // nsq, width)
    any_space = pl.BlockSpec(memory_space=pl.ANY)
    vmem = pl.BlockSpec(memory_space=pltpu.VMEM)
    vec_tile = (16, 128)
    shapes = [jax.ShapeDtypeStruct(token_shape, BF16)] * 2
    shapes += [jax.ShapeDtypeStruct((rows // 2, w.shape[4]), F32) for w in (qkv_w, out_w, up_w)]
    shapes += [jax.ShapeDtypeStruct((low_rows, width), F32), jax.ShapeDtypeStruct((1, math.prod(vec_tile)), F32)]
    shapes += [jax.ShapeDtypeStruct((8, 128), F32)]

    def like(array):
        return pltpu.VMEM(array.shape, array.dtype)

    scratch = [like(a) for a in (up_w, down_w, out_w, act, slope, grad_branch, second, low)]
    scratch += [pltpu.VMEM((width, count), BF16)]
    scratch += [like(a) for a in (x, normed, inverse, lse, vec, sums, down_w, up_w, out_w, vec)]
    scratch += [pltpu.VMEM((ndp,) + vec_tile, F32)] * 2 + [pltpu.VMEM((nsq,) + vec_tile, F32)]
    scratch += [pltpu.VMEM((nsq, 8, 128), F32), pltpu.VMEM((ndp, 8, 128), F32)]
    scratch += [pltpu.VMEM(grid + (low_rows, width), BF16)]
    down_cols = width // len([name for name, _ in SCATTER if name[0] == "down"])
    for (name, g), order in SCATTER:
        size = (QKV_PARTS[g][2] - QKV_PARTS[g][1]) * 128 if name == "qkv" else 384
        scratch += scatter_buffers((low_rows, down_cols) if name == "down" else (rows, size), nz, order)
    scratch += [pltpu.SemaphoreType.DMA((128,)), pltpu.SemaphoreType.DMA((128,)), pltpu.SemaphoreType.DMA((64,))]
    scratch += [pltpu.SemaphoreType.REGULAR]
    return pl.pallas_call(
        backward_kernel,
        out_shape=shapes,
        in_specs=[any_space] * 18 + [pl.BlockSpec(memory_space=pltpu.SMEM)],
        out_specs=[any_space] * 6 + [vmem, vmem],
        scratch_shapes=scratch,
        compiler_params=pltpu.CompilerParams(
            collective_id=2, has_side_effects=True, vmem_limit_bytes=VMEM_LIMIT
        ),
    )(
        x, qkv_w, out_w, up_w, down_w, vec, merged, heads, lse, normed, inverse, low, act, slope, block, second,
        grad_branch, sums, lengths,
    )


def adam_kernel(norm, *refs):
    ins, done, outs, given, bufs, sems = refs[:16], refs[16:18], refs[18:34], refs[34:36], refs[36:68], refs[70]
    held = refs[68:70]
    factor = CLIP_NORM / jnp.maximum(norm[0:1, 0:1], CLIP_NORM)
    loads = [pltpu.make_async_copy(ref, buf, sems.at[i]) for i, (ref, buf) in enumerate(zip(ins, bufs))]
    stores = [pltpu.make_async_copy(buf, ref, sems.at[16 + i]) for i, (ref, buf) in enumerate(zip(outs, bufs[16:]))]
    fetch = [pltpu.make_async_copy(ref, buf, sems.at[32 + i]) for i, (ref, buf) in enumerate(zip(done, held))]
    give = [pltpu.make_async_copy(buf, ref, sems.at[34 + i]) for i, (ref, buf) in enumerate(zip(given, held))]
    begin(fetch + loads)
    finish(fetch)
    begin(give)
    for k in range(4):
        finish(loads[4 * k : 4 * k + 4])
        master, first, second, shard = (buf[...] for buf in bufs[4 * k : 4 * k + 4])
        for out, value in zip(
            bufs[16 + 4 * k : 20 + 4 * k], adam_step(master, shard, first, second, factor, WEIGHT_DECAY, LEARN_RATE)
        ):
            out[...] = value
        begin(stores[4 * k : 4 * k + 4])
    finish(stores + give)


def adam_matrices(norm, done, masters, firsts, seconds, shards):
    args, shapes = [], []
    for master, first, second, shard in zip(masters, firsts, seconds, shards):
        args += [master, first, second, shard]
        shapes += [jax.ShapeDtypeStruct(master.shape, F32)] * 3 + [jax.ShapeDtypeStruct(master.shape, BF16)]
    any_space = pl.BlockSpec(memory_space=pl.ANY)
    given = [jax.ShapeDtypeStruct(a.shape, a.dtype) for a in done]
    *outs, first, second = pl.pallas_call(
        adam_kernel,
        out_shape=shapes + given,
        in_specs=[pl.BlockSpec(memory_space=pltpu.VMEM)] + [any_space] * 18,
        out_specs=[any_space] * 18,
        scratch_shapes=[pltpu.VMEM(a.shape, a.dtype) for a in args + shapes + given]
        + [pltpu.SemaphoreType.DMA((36,))],
        compiler_params=pltpu.CompilerParams(vmem_limit_bytes=VMEM_LIMIT),
    )(norm, *args, *done)
    return [first, second] + outs


def unpack(vector):
    return (
        vector[:D],
        vector[D : 2 * D],
        vector[2 * D : 3 * D],
        vector[3 * D : 4 * D],
        vector[4 * D : 5 * D],
        vector[5 * D : 5 * D + FF],
        vector[5 * D + FF : 6 * D + FF],
        vector[6 * D + FF : 7 * D + FF],
        vector[7 * D + FF : 8 * D + FF],
    )


def normalize(hidden, gain_vec, shift_vec):
    centre = hidden - jnp.mean(hidden, axis=-1, keepdims=True)
    inverse = lax.rsqrt(jnp.mean(centre * centre, axis=-1, keepdims=True) + NORM_EPS)
    normed = centre * inverse
    return (normed * gain_vec + shift_vec, normed, inverse)


def normalize_back(grad_out, normed, inverse, gain_vec):
    scaled = grad_out * gain_vec
    centred = scaled - jnp.mean(scaled, axis=-1, keepdims=True)
    return inverse * (centred - normed * jnp.mean(scaled * normed, axis=-1, keepdims=True))


def gelu_exact(values):
    return jax.nn.gelu(values, approximate=False)


def split_parts(packed_rows):
    full_len = packed_rows.shape[0]
    group_count = packed_rows.shape[-1] // (3 * HEAD_DIM)
    parts = packed_rows.reshape(full_len, 3, group_count, HEAD_DIM)
    return (parts[:, 0], parts[:, 1], parts[:, 2])


def row_probs(queries, key_rows, key_mask):
    scale = 1.0 / math.sqrt(HEAD_DIM)
    scores = jnp.einsum("qhd,khd->hqk", queries, key_rows, preferred_element_type=F32) * scale
    scores = jnp.where(key_mask[None, None, :], scores, MASK_FILL)
    row_peak = jnp.max(scores, axis=-1, keepdims=True)
    row_exp = jnp.exp(scores - row_peak)
    return row_exp / jnp.sum(row_exp, axis=-1, keepdims=True)


def whole_row(packed):
    packed_rows, key_mask = packed
    queries, key_rows, value_rows = split_parts(packed_rows)
    attn_probs = row_probs(queries, key_rows, key_mask)
    mixed_rows = jnp.einsum("hqk,khd->qhd", attn_probs.astype(BF16), value_rows, preferred_element_type=F32)
    return mixed_rows.astype(BF16).reshape(packed_rows.shape[0], D)


def whole_back(packed):
    packed_rows, grad_rows, key_mask = packed
    full_len = packed_rows.shape[0]
    queries, key_rows, value_rows = split_parts(packed_rows)
    grad_mixed = grad_rows.reshape(full_len, HEADS, HEAD_DIM)
    attn_probs = row_probs(queries, key_rows, key_mask)
    grad_probs = jnp.einsum("qhd,khd->hqk", grad_mixed, value_rows, preferred_element_type=F32)
    row_delta = jnp.sum(attn_probs * grad_probs, axis=-1, keepdims=True)
    grad_scores = (attn_probs * (grad_probs - row_delta)).astype(BF16)
    scale = 1.0 / math.sqrt(HEAD_DIM)
    grad_query = jnp.einsum("hqk,khd->qhd", grad_scores, key_rows, preferred_element_type=F32) * scale
    grad_key = jnp.einsum("hqk,qhd->khd", grad_scores, queries, preferred_element_type=F32) * scale
    grad_value = jnp.einsum("hqk,qhd->khd", attn_probs.astype(BF16), grad_mixed, preferred_element_type=F32)
    stacked = jnp.stack([grad_query, grad_key, grad_value], axis=1).astype(BF16)
    return stacked.reshape(full_len, 3 * D)


def adam_step(master, gradient, moment_one, second, factor, decay_rate, step_rate):
    clipped = gradient * factor
    first_new = BETA_ONE * moment_one + (1.0 - BETA_ONE) * clipped
    second_new = BETA_TWO * second + (1.0 - BETA_TWO) * clipped * clipped
    first_hat = first_new / (1.0 - BETA_ONE**STEP_COUNT)
    second_hat = second_new / (1.0 - BETA_TWO**STEP_COUNT)
    updated = master - step_rate * (first_hat / (jnp.sqrt(second_hat) + ADAM_EPS) + decay_rate * master)
    return (updated, first_new, second_new, updated.astype(BF16))


def layer(rows_in, cot_in, token_weight, lengths, qkv_w, out_w, up_w, down_w, vec_w):
    row_count, full_len, width_d = rows_in.shape
    token_count = row_count * full_len
    bias_q, bias_v, bias_o, gain_one, shift_one, bias_up, bias_down, gain_two, shift_two = unpack(vec_w)
    key_mask = jnp.arange(full_len, dtype=jnp.int32)[None, :] < lengths[:, None]
    flat = rows_in.reshape(token_count, width_d)
    merged = jnp.dot(flat, qkv_w, preferred_element_type=F32)
    merged = (merged + jnp.concatenate([bias_q, jnp.zeros_like(bias_q), bias_v])).astype(BF16)
    merged_rows = merged.reshape(row_count, full_len, 3 * width_d)
    mixed = lax.map(whole_row, (merged_rows, key_mask)).reshape(token_count, width_d)
    attn_out = jnp.dot(mixed, out_w, preferred_element_type=F32) + bias_o
    first_out, normed_one, inverse_one = normalize(flat.astype(F32) + attn_out, gain_one, shift_one)
    first_low = first_out.astype(BF16)
    pre_act = jnp.dot(first_low, up_w, preferred_element_type=F32) + bias_up
    activated, gelu_pull = jax.vjp(gelu_exact, pre_act)
    act_low = activated.astype(BF16)
    branch = jnp.dot(act_low, down_w, preferred_element_type=F32) + bias_down
    result, normed_two, inverse_two = normalize(first_out + branch, gain_two, shift_two)
    block_out = result.astype(BF16).reshape(row_count, full_len, width_d)
    grad_result = cot_in.astype(F32) * (token_weight * key_mask.astype(F32))[:, :, None]
    grad_result = grad_result.reshape(token_count, width_d)
    grad_gain_two = jnp.sum(grad_result * normed_two, axis=0)
    grad_shift_two = jnp.sum(grad_result, axis=0)
    grad_second = normalize_back(grad_result, normed_two, inverse_two, gain_two)
    grad_branch = grad_second.astype(BF16)
    grad_bias_down = jnp.sum(grad_branch, axis=0, dtype=F32)
    grad_down = jnp.einsum("tf,td->fd", act_low, grad_branch, preferred_element_type=F32)
    grad_act = jnp.einsum("td,fd->tf", grad_branch, down_w, preferred_element_type=F32)
    grad_pre = gelu_pull(grad_act)[0].astype(BF16)
    grad_bias_up = jnp.sum(grad_pre, axis=0, dtype=F32)
    grad_up = jnp.einsum("td,tf->df", first_low, grad_pre, preferred_element_type=F32)
    grad_first = grad_second + jnp.einsum("tf,df->td", grad_pre, up_w, preferred_element_type=F32)
    grad_gain_one = jnp.sum(grad_first * normed_one, axis=0)
    grad_shift_one = jnp.sum(grad_first, axis=0)
    grad_resid = normalize_back(grad_first, normed_one, inverse_one, gain_one)
    grad_attn = grad_resid.astype(BF16)
    grad_bias_o = jnp.sum(grad_attn, axis=0, dtype=F32)
    grad_out = jnp.einsum("td,te->de", mixed, grad_attn, preferred_element_type=F32)
    grad_mixed = jnp.einsum("te,de->td", grad_attn, out_w, preferred_element_type=F32).astype(BF16)
    grad_merged = lax.map(
        whole_back, (merged_rows, grad_mixed.reshape(row_count, full_len, width_d), key_mask)
    ).reshape(token_count, 3 * width_d)
    grad_qkv = jnp.einsum("td,te->de", flat, grad_merged, preferred_element_type=F32)
    column_sums = jnp.sum(grad_merged, axis=0, dtype=F32)
    input_grad = grad_resid + jnp.einsum("te,de->td", grad_merged, qkv_w, preferred_element_type=F32)
    input_grad = input_grad.astype(BF16).reshape(row_count, full_len, width_d)
    grad_vec = jnp.concatenate(
        [
            column_sums[:width_d],
            column_sums[2 * width_d :],
            grad_bias_o,
            grad_gain_one,
            grad_shift_one,
            grad_bias_up,
            grad_bias_down,
            grad_gain_two,
            grad_shift_two,
        ]
    )
    low = [g.astype(BF16) for g in (grad_qkv, grad_out, grad_up, grad_down)]
    return block_out, input_grad, *low, grad_vec


def body(
    tokens, cotangent, token_weight, lengths,
    qkv_master, out_master, up_master, down_master, vec_master,
    qkv_first, out_first, up_first, down_first, vec_first,
    qkv_second, out_second, up_second, down_second, vec_second,
):
    ndp, nsq = lax.axis_size("dp"), lax.axis_size("seq")
    devices = ndp * nsq
    row_count, local_len, width_d = tokens.shape
    full_len, part = local_len * nsq, row_count // nsq
    vec_size = vec_master.shape[0]
    sq = lax.axis_index("seq")
    my_lengths = lax.dynamic_slice_in_dim(lengths, sq * part, part)
    both = ("dp", "seq")
    chip = 2 * qkv_master.shape[0]
    own_kernels = (
        qkv_master.shape[0] % 8 == 0
        and down_master.shape[0] % 16 == 0
        and nsq == 4
        and ndp % 2 == 0
        and vec_size * nsq % 128 == 0
        and part * full_len // (ndp * nsq // 2) >= chip
        and local_len == 128
    )
    if own_kernels:
        spread = jnp.zeros((16 * 128,), F32)
        spread = lax.dynamic_update_slice(spread, vec_master, (sq * vec_size,)).reshape(16, 128)
        saved = forward(
            tokens, cotangent, token_weight, qkv_master, out_master, up_master, down_master, spread, lengths
        )
        block_out, input_grad, *shards, vec_s, norm = backward(saved, lengths)
        shards.append(lax.dynamic_slice(vec_s.reshape(-1), (sq * vec_size,), (vec_size,)))
        norm_value = norm[0, 0]
        block_out, input_grad, *matrices = adam_matrices(
            norm,
            (block_out, input_grad),
            (qkv_master, out_master, up_master, down_master),
            (qkv_first, out_first, up_first, down_first),
            (qkv_second, out_second, up_second, down_second),
            shards[:4],
        )
    else:
        rows_in, cot_in = (
            lax.all_to_all(a, "seq", split_axis=0, concat_axis=1, tiled=True) for a in (tokens, cotangent)
        )
        weights = lax.all_gather(token_weight, "seq", axis=0)
        qkv_w, out_w, up_w, down_w, vec_w = (
            lax.all_gather(m.astype(BF16), both, axis=0, tiled=True)
            for m in (qkv_master, out_master, up_master, down_master, vec_master)
        )
        my_weight = lax.dynamic_slice_in_dim(weights, sq * part, part, axis=1)
        my_weight = my_weight.transpose(1, 0, 2).reshape(part, full_len)
        block_rows, grad_rows, *grads, grad_vec = layer(
            rows_in, cot_in, my_weight, my_lengths, qkv_w, out_w, up_w, down_w, vec_w.astype(F32)
        )
        block_out, input_grad = (
            lax.all_to_all(a, "seq", split_axis=1, concat_axis=0, tiled=True) for a in (block_rows, grad_rows)
        )
        shards = [lax.psum_scatter(g.astype(F32), both, scatter_dimension=0, tiled=True) for g in grads]
        shards.append(lax.psum_scatter(grad_vec, both, scatter_dimension=0, tiled=True))
        norm_value = jnp.sqrt(lax.psum(sum(jnp.sum(s * s) for s in shards), both))
    factor = CLIP_NORM / jnp.maximum(norm_value, CLIP_NORM)
    outs = [block_out, input_grad, norm_value]
    if own_kernels:
        outs += matrices
    else:
        for master, shard, first, second in (
            (qkv_master, shards[0], qkv_first, qkv_second),
            (out_master, shards[1], out_first, out_second),
            (up_master, shards[2], up_first, up_second),
            (down_master, shards[3], down_first, down_second),
        ):
            outs += adam_step(master, shard, first, second, factor, WEIGHT_DECAY, LEARN_RATE)
    outs += adam_step(vec_master, shards[4], vec_first, vec_second, factor, 0.0, VEC_RATE)
    return tuple(outs)


def solution(mesh):
    tokens, both, flat = P("dp", "seq", None), P(("dp", "seq"), None), P(("dp", "seq"))
    weights = (both, both, both, both, flat)
    in_specs = (tokens, tokens, P("dp", "seq"), P("dp")) + 3 * weights
    out_specs = (tokens, tokens, P()) + 4 * (both,) * 4 + (flat,) * 4
    return jax.shard_map(body, mesh=mesh, in_specs=in_specs, out_specs=out_specs, check_vma=False)
```

```python
import functools
import math

import jax
import jax.numpy as jnp
from jax import lax
from jax.experimental import pallas as pl
from jax.experimental.pallas import tpu as pltpu
from jax.sharding import PartitionSpec as P

D = 768
HEADS = 12
HEAD_DIM = 64
FF = 3072
STEP_COUNT = 10
CLIP_NORM = 1.0
BETA_ONE = 0.9
BETA_TWO = 0.999
LEARN_RATE = 0.05
VEC_RATE = 0.3
WEIGHT_DECAY = 0.01
ADAM_EPS = 1e-08
NORM_EPS = 1e-05
MASK_FILL = -1e30
MESH = pl.DeviceIdType.MESH
F32 = jnp.float32
BF16 = jnp.bfloat16
VMEM_LIMIT = 62 << 20


class Place:
    def __init__(self):
        self.ndp, self.nsq = lax.axis_size("dp"), lax.axis_size("seq")
        self.dp, self.sq = lax.axis_index("dp"), lax.axis_index("seq")
        self.z, self.y = self.dp // 2, self.dp % 2
        self.x, self.c = self.sq // 2, self.sq % 2
        self.nz = self.ndp // 2
        self.core = (self.dp, self.x * 2 + 1 - self.c)
        self.across_x = (self.dp, (1 - self.x) * 2 + self.c)
        self.across_y = (self.z * 2 + 1 - self.y, self.sq)

    def along_z(self, k):
        return (self.z + k) % self.nz

    def at_z(self, z):
        return (z * 2 + self.y, self.sq)

    def group(self):
        return [(self.dp, (self.sq + k) % self.nsq) for k in range(1, self.nsq)]

    def columns(self):
        return [((self.dp + k) % self.ndp, self.sq) for k in range(1, self.ndp)]


def greet(targets):
    barrier = pltpu.get_barrier_semaphore()
    for target in targets:
        pl.semaphore_signal(barrier, inc=1, device_id=target, device_id_type=MESH)
    pl.semaphore_wait(barrier, len(targets))


class Sems:
    def __init__(self, send, recv, local):
        self.send, self.recv, self.local = send, recv, local
        self.n = self.m = 0

    def remote(self, src, dst, target):
        i = self.n
        self.n += 1
        return pltpu.make_async_remote_copy(
            src_ref=src,
            dst_ref=dst,
            send_sem=self.send.at[i],
            recv_sem=self.recv.at[i],
            device_id=target,
            device_id_type=MESH,
        )

    def here(self, src, dst):
        i = self.m
        self.m += 1
        return pltpu.make_async_copy(src, dst, self.local.at[i])


def begin(copies):
    for copy in copies:
        copy.start()


def finish(copies):
    for copy in copies:
        copy.wait()


GATHER = (
    (('qkv', 0), 'zxy'),
    (('qkv', 1), 'xzy'),
    (('up', 0), 'yzx'),
    (('out', 0), 'zyx'),
    (('qkv', 2), 'xzy'),
    (('up', 2), 'zyx'),
    (('down', 0), 'zyx'),
    (('up', 1), 'xzy'),
    (('up', 3), 'zxy'),
    (('down', 2), 'xzy'),
    (('down', 1), 'xyz'),
)
SCATTER = (
    (('up', 2), 'yxz'),
    (('qkv', 2), 'yzx'),
    (('down', 0), 'yxz'),
    (('up', 3), 'xyz'),
    (('qkv', 1), 'yxz'),
    (('qkv', 0), 'yxz'),
    (('up', 0), 'yxz'),
    (('up', 1), 'xzy'),
    (('down', 1), 'zyx'),
    (('out', 0), 'xyz'),
)
FORWARD_PLAN = (
    ((('qkv', 0), 0), (('qkv', 1), 0), (('qkv', 2), 0)),
    ((('up', 0), 0), (('out', 0), 0), (('up', 2), 0), (('up', 1), 0)),
    (('tokA', 0), ('tokB', 0), (('down', 2), 0), (('qkv', 1), 1), (('qkv', 0), 1), (('up', 0), 1), (('out', 0), 1), (('qkv', 2), 1), (('up', 2), 1), (('qkv', 0), 2), (('out', 0), 2), (('qkv', 1), 2), (('down', 0), 0), (('up', 2), 2), (('down', 1), 0), (('up', 1), 1), (('up', 3), 0), (('qkv', 0), 3), (('qkv', 2), 2), (('up', 0), 2), (('down', 2), 1), (('qkv', 0), 4)),
    ((('out', 0), 3),),
    ((('qkv', 1), 3), (('down', 0), 1)),
    (),
    ((('out', 0), 4),),
    ((('up', 3), 1), (('qkv', 1), 4)),
    ((('qkv', 2), 3), (('down', 1), 1)),
    ((('up', 2), 3),),
    (),
    ((('qkv', 2), 4), (('down', 0), 2), (('up', 1), 2)),
    (),
    ((('up', 0), 3), (('up', 2), 4), (('down', 1), 2)),
    ((('up', 3), 2),),
    (),
    (('cotA', 0), ('cotB', 0), (('up', 0), 4)),
    (),
    (),
    (),
    ((('up', 1), 3), (('down', 2), 2), (('down', 0), 3), (('up', 1), 4)),
    ((('up', 3), 3),),
    ((('down', 0), 4), (('down', 1), 3), (('up', 3), 4)),
    ((('down', 2), 3),),
    ((('down', 1), 4),),
    ((('down', 2), 4),),
    (),
)
BACKWARD_PLAN = (
    (('outA', 0), (('down', 0), 0), (('down', 1), 0)),
    (),
    ((('up', 0), 0), (('up', 1), 0)),
    (),
    (('outB', 0), (('up', 2), 0), (('down', 0), 1), (('up', 3), 0), (('down', 1), 1), (('up', 0), 1), (('up', 1), 1)),
    ((('up', 2), 1), (('up', 3), 1)),
    ((('out', 0), 0),),
    (),
    (),
    (),
    (),
    ((('qkv', 0), 0),),
    ((('up', 0), 2), (('up', 1), 2), (('out', 0), 1), (('up', 3), 2)),
    ((('up', 2), 2), (('qkv', 0), 1)),
    (),
    ((('qkv', 1), 0),),
    ((('down', 0), 2), (('up', 3), 3), (('qkv', 1), 1), (('up', 0), 3), (('down', 1), 2), (('up', 2), 3)),
    (),
    ((('qkv', 0), 2), (('up', 1), 3)),
    ((('qkv', 2), 0),),
    ((('down', 0), 3), (('up', 3), 4), (('down', 1), 3), (('out', 0), 2), (('up', 2), 4), (('qkv', 2), 1), (('up', 0), 4), (('up', 1), 4), (('qkv', 0), 3)),
    (),
    (),
    ((('qkv', 1), 2), (('down', 1), 4)),
    ((('out', 0), 3), (('qkv', 0), 4), (('down', 0), 4), (('qkv', 2), 2), (('out', 0), 4), (('qkv', 1), 3), (('qkv', 2), 3), (('qkv', 1), 4), (('qkv', 2), 4)),
)
PAIRS = HEADS // 2
QKV_PARTS = ((0, 0, 3), (1, 0, 3), (2, 0, 3))
NT = (((1,), (1,)), ((), ()))
TN = (((0,), (0,)), ((), ()))
NN = (((1,), (0,)), ((), ()))
def dot(a, b, dims=NN):
    return lax.dot_general(a, b, dims, preferred_element_type=F32)


def lanes(start, size):
    return pl.ds(pl.multiple_of(start, 128), size)


def mean(values):
    return jnp.sum(values, axis=-1, keepdims=True) * (1.0 / D)


def matrix(ref, *index):
    value = ref[index] if index else ref[...]
    return value.reshape(-1, value.shape[-1])


def columns(ref, cols):
    value = ref[:, :, :, :, cols]
    return value.reshape(-1, value.shape[-1])


class Gather:
    def __init__(self, place, sems, at, order):
        p = place
        spot = {"z": p.z, "y": p.y, "x": p.x}
        self.stages = []
        for axis in order:
            here = at(**spot)
            if axis == "z":
                targets = [p.at_z(p.along_z(k)) for k in range(1, p.nz)]
            else:
                targets = [p.across_x if axis == "x" else p.across_y]
            self.stages.append([sems.remote(here, here, target) for target in targets])
            spot[axis] = slice(None)
        here = at(**spot)
        self.stages.append([sems.remote(here, here, p.core)])

    def advance(self, stage):
        if stage:
            finish(self.stages[stage - 1])
        if stage < len(self.stages):
            begin(self.stages[stage])


class Scatter:
    def __init__(self, place, sems, at, near, bufs, order):
        p = place
        *bufs, final = bufs
        total = at(p.c)
        self.final = final
        self.stages = [[sems.remote(at(1 - p.c), near, p.core)]]
        sizes = {"z": p.nz, "y": 2, "x": 2}
        own = {"z": p.z, "y": p.y, "x": p.x}
        spot = {axis: slice(None) for axis in "zyx"}
        left = [axis for axis in "zyx"]

        def index(spot):
            return (spot["z"], spot["y"], spot["x"])

        self.after = [functools.partial(add_into, total, [near], [sizes[axis] for axis in left])]
        for buf, axis in zip(bufs, order):
            if axis == "z":
                targets = [(p.along_z(k), p.at_z(p.along_z(k)), buf.at[k - 1]) for k in range(1, p.nz)]
            elif axis == "y":
                targets = [(1 - p.y, p.across_y, buf)]
            else:
                targets = [(1 - p.x, p.across_x, buf)]
            self.stages.append(
                [sems.remote(total.at[index({**spot, axis: to})], into, device) for to, device, into in targets]
            )
            spot[axis] = own[axis]
            left.remove(axis)
            extra = [into for _, _, into in targets]
            kept = total.at[index(spot)]
            if left:
                self.after.append(functools.partial(add_into, kept, extra, [sizes[axis] for axis in left]))
            else:
                self.after.append(functools.partial(add_last, final, kept, extra))

    def advance(self, stage):
        if stage:
            finish(self.stages[stage - 1])
            self.after[stage - 1]()
        if stage < len(self.stages):
            begin(self.stages[stage])


def add_into(total, extra, lead):
    def one(i, carry):
        spot = []
        for size in reversed(lead):
            spot.insert(0, i % size)
            i = i // size
        spot = tuple(spot)
        if len(extra) == 1:
            total[spot] = total[spot] + extra[0][spot]
            return carry
        value = total[spot].astype(F32)
        for part in extra:
            value = value + part[spot].astype(F32)
        total[spot] = value.astype(total.dtype)
        return carry

    lax.fori_loop(0, math.prod(lead), one, 0)


def add_last(final, total, extra):
    value = total[...].astype(F32)
    for part in extra:
        value = value + part[...].astype(F32)
    final[...] = value


def scatter_buffers(block, nz, order):
    sizes = {"z": nz, "y": 2, "x": 2}
    left, bufs = list("zyx"), []
    for axis in order:
        left.remove(axis)
        lead = tuple(sizes[a] for a in left)
        if axis == "z":
            lead = (nz - 1,) + lead
        bufs.append(pltpu.VMEM(lead + block, BF16))
    return bufs + [pltpu.VMEM(block, F32)]


def tokens_to_rows(place, sems, src, dst):
    p = place
    part, length = dst.shape[0], src.shape[1]
    spot = dst.at[:, pl.ds(p.sq * length, length)]
    copies = [sems.here(src.at[pl.ds(p.sq * part, part)], spot)]
    for k in range(1, p.nsq):
        to = (p.sq + k) % p.nsq
        copies.append(sems.remote(src.at[pl.ds(to * part, part)], spot, (p.dp, to)))
    return copies


def rows_to_tokens(place, sems, src, dst):
    p = place
    part, length = src.shape[0], dst.shape[1]
    spot = dst.at[pl.ds(p.sq * part, part)]
    copies = [sems.here(src.at[:, pl.ds(p.sq * length, length)], spot)]
    for k in range(1, p.nsq):
        to = (p.sq + k) % p.nsq
        copies.append(sems.remote(src.at[:, pl.ds(to * length, length)], spot, (p.dp, to)))
    return copies


def of_head(values, h):
    lane = lax.broadcasted_iota(jnp.int32, values.shape, 1)
    own = lane < HEAD_DIM if h == 0 else lane >= HEAD_DIM
    return jnp.where(own, values, jnp.zeros_like(values))


def pair_base(p):
    return (p % 2) * (3 * D // 2) + (p // 2) * (3 * 128)


def project(x, w, bias, merged, p, rows=512):
    cs = pl.ds(pair_base(p), 384)
    part = columns(w, cs)
    for i in range(x.shape[0] // rows):
        rs = pl.ds(i * rows, rows)
        merged[rs, cs] = (dot(x[rs, :], part) + bias[0:1, cs]).astype(BF16)


def key_bias(lengths, row, count):
    key = lax.broadcasted_iota(jnp.int32, (count, 1), 0)
    return jnp.where(key < lengths[row], 0.0, MASK_FILL).astype(F32)


def attend(merged, lengths, first_row, heads_out, lse, length, p):
    base = pair_base(p)
    pair = range(2)
    for r in range(heads_out.shape[0] // length):
        rs = pl.ds(r * length, length)
        q2 = merged[rs, pl.ds(base, 128)] * jnp.asarray(HEAD_DIM**-0.5, BF16)
        k2 = merged[rs, pl.ds(base + 128, 128)]
        v2t = merged[rs, pl.ds(base + 256, 128)].T
        bias = key_bias(lengths, first_row + r, length)
        scores = [dot(of_head(k2, h), q2, NT) for h in pair]
        weights, totals = [], []
        for h in pair:
            biased = scores[h] + bias
            peak = jnp.max(biased, axis=0, keepdims=True)
            value = jnp.exp(biased - peak)
            total = jnp.sum(value, axis=0, keepdims=True)
            lse[r, 2 * p + h] = peak + jnp.log(total)
            weights.append(value.astype(BF16))
            totals.append(total)
        own = [v2t[HEAD_DIM * h : HEAD_DIM * (h + 1)] for h in pair]
        mixed = jnp.concatenate([dot(own[h], weights[h]) * (1.0 / totals[h]) for h in pair], axis=0)
        heads_out[rs, pl.ds(p * 128, 128)] = mixed.T.astype(BF16)


def first_norm(x, heads_out, w, vec, normed, inverse, low, start, count, rows=512):
    @pl.loop(0, count // rows)
    def _(i):
        rs = pl.ds(pl.multiple_of(start + i * rows, rows), rows)
        hidden = x[rs, :].astype(F32) + (dot(heads_out[rs, :], matrix(w)) + vec[0:1, 2 * D : 3 * D])
        centre = hidden - mean(hidden)
        scale = lax.rsqrt(mean(centre * centre) + NORM_EPS)
        unit = centre * scale
        normed[rs, :] = unit
        inverse[rs, :] = scale
        low[rs, :] = (unit * vec[0:1, 3 * D : 4 * D] + vec[0:1, 4 * D : 5 * D]).astype(BF16)


def feed_up(j, low, up_w, vec, act, slope, chunk, rows=256):
    cs = pl.ds(j * chunk, chunk)
    bias = vec[0:1, 5 * D + j * chunk : 5 * D + (j + 1) * chunk]

    @pl.loop(0, low.shape[0] // (2 * rows))
    def _(i):
        weight = columns(up_w, cs)
        for k in range(2):
            rs = pl.ds(pl.multiple_of((2 * i + k) * rows, rows), rows)
            value = dot(low[rs, :], weight) + bias
            cdf = 0.5 + 0.5 * lax.erf(value * 0.5**0.5)
            bell = jnp.exp(-0.5 * (value * value)) * (2 * math.pi) ** -0.5
            act[rs, cs] = (value * cdf).astype(BF16)
            slope[rs, cs] = (cdf + value * bell).astype(slope.dtype)


def feed_down(act, down_w, branch, cs, rows=512):
    weight = down_w[:, :, :, :, :, cs]
    weight = weight.reshape(-1, weight.shape[-1])
    for i in range(act.shape[0] // rows):
        rs = pl.ds(i * rows, rows)
        branch[rs, cs] = dot(act[rs, :], weight)


def second_norm(normed, vec, branch, cot, weight, block_out, grad_branch, sums, rows=256):
    sums[...] = jnp.zeros_like(sums)
    at = 5 * D + FF
    gain_one, shift_one, bias_down = (vec[0:1, s : s + D] for s in (3 * D, 4 * D, at))
    gain_two, shift_two = (vec[0:1, s : s + D] for s in (at + D, at + 2 * D))

    @pl.loop(0, normed.shape[0] // rows)
    def _(i):
        rs = pl.ds(pl.multiple_of(i * rows, rows), rows)
        hidden = normed[rs, :] * gain_one + shift_one + (branch[rs, :] + bias_down)
        centre = hidden - mean(hidden)
        scale = lax.rsqrt(mean(centre * centre) + NORM_EPS)
        unit = centre * scale
        block_out[rs, :] = (unit * gain_two + shift_two).astype(BF16)
        grad = cot[rs, :].astype(F32) * weight[rs, 0:1]
        sums[1:2, :] += jnp.sum(grad * unit, axis=0, keepdims=True)
        sums[2:3, :] += jnp.sum(grad, axis=0, keepdims=True)
        scaled = grad * gain_two
        second = scale * (scaled - mean(scaled) - unit * mean(scaled * unit))
        normed[rs, :] = second
        low = second.astype(BF16)
        grad_branch[rs, :] = low
        sums[0:1, :] += jnp.sum(low.astype(F32), axis=0, keepdims=True)


def forward_kernel(
    tokens, cotangent, weight, qkv_m, out_m, up_m, down_m, vec_m, lengths,
    x_out, qkv_w, out_w, up_w, down_w, vec_out, merged_out, heads_out, lse_out, normed_out, inverse_out,
    low_out, act_out, slope_out, block_out, second_out, branch_out, sums_out,
    qkv_f, out_f, up_f, down_f,
    qkv_v, out_v, up_v, down_v, x, cot, wt, wt_all, vec_near, vec_far, vec, bias, merged, heads, lse, normed, inverse,
    low, act, slope, branch, grad_branch, sums, send, recv, local,
):
    p = Place()
    greet(p.group() + p.columns())
    sems = Sems(send, recv, local)
    part, length = x.shape[0], x.shape[1]
    moves = {}
    move_tokens = tokens_to_rows(p, sems, tokens, x)
    move_cot = tokens_to_rows(p, sems, cotangent, cot)
    for name, copies in (("tok", move_tokens), ("cot", move_cot)):
        moves[name + "A"], moves[name + "B"] = [copies[2]], [copies[3]]
    spot = wt_all.at[p.sq]
    move_weight = [sems.here(weight, spot)] + [sems.remote(weight, spot, to) for to in p.group()]
    masters = {"qkv": (qkv_m, qkv_f), "out": (out_m, out_f), "up": (up_m, up_f)}
    rows = qkv_m.shape[0]
    mine = pl.ds(p.c * rows, rows)
    fetch = {
        name: [sems.here(master, wide.at[mine]), sems.remote(master, wide.at[mine], p.core)]
        for name, (master, wide) in masters.items()
    }
    fetch["down"] = [sems.here(down_m, down_f)]
    chunk = FF // len([name for name, _ in GATHER if name[0] == "up"])
    down_cols = D // len([name for name, _ in GATHER if name[0] == "down"])
    half = 3 * D // 2
    places = {
        "qkv": lambda g: lambda z, y, x: qkv_v.at[z, y, x, :, lanes(p.c * half + g * 384, 384)],
        "out": lambda g: lambda z, y, x: out_v.at[z, y, x, :, lanes(p.c * (D // 2), D // 2)],
        "up": lambda g: lambda z, y, x: up_v.at[z, y, x, :, lanes(g * chunk + p.c * (chunk // 2), chunk // 2)],
        "down": lambda g: lambda z, y, x: down_v.at[z, y, x, p.c, :, pl.ds(g * down_cols, down_cols)],
    }
    items = {key: Gather(p, sems, places[key[0]](key[1]), order) for key, order in GATHER}
    near = vec_near.at[p.sq]
    vec_one = [sems.remote(near, near, to) for to in p.group()]
    far = vec_far.at[p.dp]
    vec_two = [sems.remote(far, far, to) for to in p.columns()]

    def cast(name):
        finish(fetch[name])
        own = (p.z, p.y, p.x)
        if name == "qkv":
            for g in range(PAIRS // 2):
                for s in range(3):
                    to = lanes(p.c * half + g * 384 + s * 128, 128)
                    qkv_v[own + (slice(None), to)] = qkv_f[:, lanes(s * D + (2 * g + p.c) * 128, 128)].astype(BF16)
        elif name == "out":
            cs = lanes(p.c * (D // 2), D // 2)
            out_v[own + (slice(None), cs)] = out_f[:, cs].astype(BF16)
        elif name == "up":
            for g in range(FF // chunk):
                cs = lanes(g * chunk + p.c * (chunk // 2), chunk // 2)
                up_v[own + (slice(None), cs)] = up_f[:, cs].astype(BF16)
        else:
            down_v[own + (p.c,)] = down_f[...].astype(BF16)

    plan = iter(FORWARD_PLAN)

    def go():
        for key, stage in next(plan):
            if key in moves:
                begin(moves[key])
            else:
                items[key].advance(stage)

    begin(fetch["qkv"])
    vec_near[p.sq] = vec_m[...].astype(BF16).astype(F32)
    begin(fetch["out"] + fetch["up"] + fetch["down"])
    cast("qkv")
    go()
    begin(vec_one + move_weight + move_tokens[:2] + move_cot[:2])
    for name in ("out", "up", "down"):
        cast(name)
    finish(vec_one)
    block = vec_near[0]
    for k in range(1, p.nsq):
        block = block + vec_near[k]
    vec_far[p.dp] = block
    begin(vec_two)
    go()
    finish(vec_two)
    tiles = vec.shape[1] // (128 * p.ndp)
    for d in range(p.ndp):
        for k in range(tiles):
            vec[0:1, pl.ds((d * tiles + k) * 128, 128)] = vec_far[d, k : k + 1, :]
    for pair in range(PAIRS):
        base = pair_base(pair)
        bias[0:1, base : base + 128] = vec[0:1, pair * 128 : (pair + 1) * 128]
        bias[0:1, base + 128 : base + 256] = jnp.zeros((1, 128), F32)
        bias[0:1, base + 256 : base + 384] = vec[0:1, D + pair * 128 : D + (pair + 1) * 128]
    finish(move_weight)
    for r in range(part):
        for k in range(p.nsq):
            row = wt_all[k, pl.ds(p.sq * part + r, 1), :]
            size = row.shape[1]
            live = lax.broadcasted_iota(jnp.int32, (size, size), 0) + k * size < lengths[p.sq * part + r]
            column = jnp.broadcast_to(row, (size, size)).T
            wt[pl.ds(r * length + k * size, size), :] = jnp.where(live, column, 0.0)
    flat = x.reshape(part * length, D)
    keep = {}

    def save(name, src, dst):
        keep[name] = sems.here(src, dst)
        keep[name].start()

    for g in range(PAIRS // 2):
        go()
        if g == 0:
            finish(move_tokens)
            save("x", x, x_out)
        for pair in (2 * g, 2 * g + 1):
            project(flat, qkv_v, bias, merged, pair)
            go()
            attend(merged, lengths, p.sq * part, heads, lse, length, pair)
            go()
    save("qkv", qkv_v, qkv_w)
    save("merged", merged, merged_out)
    save("heads", heads, heads_out)
    save("lse", lse, lse_out)
    go()
    save("out", out_v, out_w)
    first_norm(flat, heads, out_v, vec, normed, inverse, low, 0, part * length // 2)
    go()
    first_norm(flat, heads, out_v, vec, normed, inverse, low, part * length // 2, part * length // 2)
    save("normed", normed, normed_out)
    save("inverse", inverse, inverse_out)
    save("low", low, low_out)
    for j in range(FF // chunk):
        go()
        feed_up(j, low, up_v, vec, act, slope, chunk)
    save("up", up_v, up_w)
    save("act", act, act_out)
    save("slope", slope, slope_out)
    for j in range(D // down_cols):
        go()
        feed_down(act, down_v, branch, pl.ds(j * down_cols, down_cols))
    save("down", down_v, down_w)
    go()
    finish(move_cot)
    keep.pop("heads").wait()
    keep.pop("normed").wait()
    second_norm(normed, vec, branch, cot.reshape(part * length, D), wt, heads, grad_branch, sums)
    save("block", heads, block_out)
    save("second", normed, second_out)
    save("branch", grad_branch, branch_out)
    save("sums", sums, sums_out)
    save("vec", vec, vec_out)
    finish(keep.values())


def forward(tokens, cotangent, weight, qkv_m, out_m, up_m, down_m, vec_m, lengths):
    ndp, nsq = lax.axis_size("dp"), lax.axis_size("seq")
    rows, length, width = tokens.shape
    part, full = rows // nsq, length * nsq
    count = part * full
    chip, low = 2 * qkv_m.shape[0], down_m.shape[0]
    grid = (ndp // 2, 2, nsq // 2)
    vec_len = 8 * D + FF
    any_space = pl.BlockSpec(memory_space=pl.ANY)
    vmem = pl.BlockSpec(memory_space=pltpu.VMEM)

    def both(shape, dtype):
        return jax.ShapeDtypeStruct(shape, dtype), pltpu.VMEM(shape, dtype)

    weights = [both(grid + (chip, m.shape[1]), BF16) for m in (qkv_m, out_m, up_m)]
    weights.append(both(grid + (2, low, width), BF16))
    x = both((part, full, width), BF16)
    vec = both((1, vec_len), F32)
    merged = both((count, 3 * width), BF16)
    heads = both((count, width), BF16)
    lse = both((part, HEADS, 1, full), F32)
    normed = both((count, width), F32)
    inverse = both((count, 1), F32)
    act = both((count, FF), BF16)
    sums = both((8, width), F32)
    outs = [x[0]] + [w[0] for w in weights] + [vec[0], merged[0], heads[0], lse[0], normed[0], inverse[0]]
    outs += [heads[0], act[0], act[0], heads[0], normed[0], heads[0], sums[0]]
    scratch = [pltpu.VMEM((chip, m.shape[1]), F32) for m in (qkv_m, out_m, up_m)] + [pltpu.VMEM(down_m.shape, F32)]
    scratch += [w[1] for w in weights]
    scratch += [x[1], x[1], pltpu.VMEM((count, length), F32), pltpu.VMEM((nsq,) + weight.shape, F32)]
    scratch += [pltpu.VMEM((nsq,) + vec_m.shape, F32), pltpu.VMEM((ndp,) + vec_m.shape, F32), vec[1]]
    scratch += [pltpu.VMEM((1, 3 * width), F32), merged[1], heads[1], lse[1], normed[1], inverse[1]]
    scratch += [heads[1], act[1], act[1], normed[1], heads[1], sums[1]]
    scratch += [pltpu.SemaphoreType.DMA((96,)), pltpu.SemaphoreType.DMA((96,)), pltpu.SemaphoreType.DMA((48,))]
    return pl.pallas_call(
        forward_kernel,
        out_shape=outs,
        in_specs=[any_space] * 7 + [vmem, pl.BlockSpec(memory_space=pltpu.SMEM)],
        out_specs=[any_space] * len(outs),
        scratch_shapes=scratch,
        compiler_params=pltpu.CompilerParams(
            collective_id=1, has_side_effects=True, vmem_limit_bytes=VMEM_LIMIT
        ),
    )(tokens, cotangent, weight, qkv_m, out_m, up_m, down_m, vec_m, lengths)


def feed_back_down(j, grad_branch, down_w, act, slope, grad_down, vec_sum, rows=512):
    n = grad_down.shape[0]
    cols = FF // n
    cs = pl.ds(j * cols, cols)
    weight = matrix(down_w, j)

    total = None
    for i in range(slope.shape[0] // rows):
        rs = pl.ds(i * rows, rows)
        grad = dot(grad_branch[rs, :], weight, NT) * slope[rs, cs].astype(F32)
        low = grad.astype(BF16)
        slope[rs, cs] = low
        part = jnp.sum(low.astype(F32), axis=0, keepdims=True)
        total = part if total is None else total + part
    vec_sum[0:1, 5 * D + j * cols : 5 * D + (j + 1) * cols] = total
    value = dot(columns(act, cs), grad_branch[...], TN)
    grad_down[j] = value.astype(BF16).reshape(grad_down.shape[1:])


def feed_back_up(j, low_t, grad_pre, up_w, grad_first, grad_up, rows=512):
    n = grad_up.shape[0]
    cols = FF // n
    cs = pl.ds(j * cols, cols)
    value = dot(low_t[...], grad_pre[:, cs])
    grad_up[:, :, :, :, cs] = value.astype(BF16).reshape(grad_up.shape[:4] + (cols,))
    weight = columns(up_w, cs)
    for i in range(grad_pre.shape[0] // rows):
        rs = pl.ds(i * rows, rows)
        grad_first[rs, :] += dot(grad_pre[rs, cs], weight, NT)


def first_norm_back(grad_first, normed, inverse, vec, grad_attn, vec_sum, rows=256):
    vec_sum[0:1, 2 * D : 5 * D] = jnp.zeros((1, 3 * D), F32)

    @pl.loop(0, normed.shape[0] // rows)
    def _(i):
        rs = pl.ds(pl.multiple_of(i * rows, rows), rows)
        grad, unit = grad_first[rs, :], normed[rs, :]
        vec_sum[0:1, 3 * D : 4 * D] += jnp.sum(grad * unit, axis=0, keepdims=True)
        vec_sum[0:1, 4 * D : 5 * D] += jnp.sum(grad, axis=0, keepdims=True)
        scaled = grad * vec[0:1, 3 * D : 4 * D]
        resid = inverse[rs, :] * (scaled - mean(scaled) - unit * mean(scaled * unit))
        grad_first[rs, :] = resid
        low = resid.astype(BF16)
        grad_attn[rs, :] = low
        vec_sum[0:1, 2 * D : 3 * D] += jnp.sum(low.astype(F32), axis=0, keepdims=True)


def attend_back(merged, grad_heads, lengths, first_row, lse, grad_merged, length, p):
    per_row = merged.shape[0] // (grad_heads.shape[0] // length)
    base = pair_base(p)
    pair = range(2)

    for r in range(grad_heads.shape[0] // length):
        rs = pl.ds(r * length, length)
        zs = pl.ds(r * per_row, per_row)

        def piece(start):
            return merged[zs, :, :, :, pl.ds(base + start, 128)].reshape(length, 128)

        q2 = piece(0) * jnp.asarray(HEAD_DIM**-0.5, BF16)
        k2, v2 = piece(128), piece(256)
        out2 = grad_heads[rs, pl.ds(p * 128, 128)]
        k2t = k2.T
        bias = key_bias(lengths, first_row + r, length)
        scores = [dot(of_head(k2, h), q2, NT) for h in pair]
        grad_probs = [dot(of_head(v2, h), out2, NT) for h in pair]
        low_probs, grad_scores = [], []
        for h in pair:
            probs = jnp.exp(scores[h] + bias - lse[r, 2 * p + h])
            weighted = probs * grad_probs[h]
            delta = jnp.sum(weighted, axis=0, keepdims=True)
            grad_scores.append((weighted - probs * delta).astype(BF16))
            low_probs.append(probs.astype(BF16))
        own = [k2t[HEAD_DIM * h : HEAD_DIM * (h + 1)] for h in pair]
        grad_q = jnp.concatenate([dot(own[h], grad_scores[h]) for h in pair], axis=0) * HEAD_DIM**-0.5
        keys = [dot(grad_scores[h], q2) for h in pair]
        values = [dot(low_probs[h], out2) for h in pair]
        lane = lax.broadcasted_iota(jnp.int32, keys[0].shape, 1)
        grad_merged[rs, pl.ds(base, 128)] = grad_q.T.astype(BF16)
        grad_merged[rs, pl.ds(base + 128, 128)] = jnp.where(lane < HEAD_DIM, *keys).astype(BF16)
        grad_merged[rs, pl.ds(base + 256, 128)] = jnp.where(lane < HEAD_DIM, *values).astype(BF16)


def project_back(x_t, grad_merged, grad_qkv, vec_sum, p):
    cs = pl.ds(pair_base(p), 384)
    grad = grad_merged[:, cs]
    total = jnp.sum(grad.astype(F32), axis=0, keepdims=True)
    vec_sum[0:1, p * 128 : (p + 1) * 128] = total[:, :128]
    vec_sum[0:1, D + p * 128 : D + (p + 1) * 128] = total[:, 256:]
    value = dot(x_t[...], grad).astype(BF16)
    grad_qkv[:, :, :, :, cs] = value.reshape(grad_qkv.shape[:4] + (384,))


def backward_kernel(
    x_in, qkv_w, out_w, up_w, down_w, vec_in, merged_in, heads_in, lse_in, normed_in, inverse_in,
    low_in, act_in, slope_in, block_rows, second_in, branch_in, sums_in, lengths,
    block_out, input_grad, qkv_s, out_s, up_s, down_s, vec_s, norm,
    up_v, down_v, out_v, act, slope, grad_branch, grad_first, low, low_t, x, normed, inverse, lse, vec, sums,
    grad_down, grad_up, grad_out, vec_sum, vec_parts, vec_recv, vec_near, near_sum, far_sum, down_near, *rest,
):
    send, recv, local, free = rest[-4:]
    pool = list(rest[:-4])
    p = Place()
    greet(p.group() + p.columns())
    sems = Sems(send, recv, local)
    part, length = x_in.shape[:2]
    n = down_v.shape[0]
    chunk = FF // n
    wide = 3 * D
    load_one = [sems.here(branch_in, grad_branch)]
    load_chunk = [
        [
            sems.here(down_w.at[j], down_v.at[j]),
            sems.here(slope_in.at[:, pl.ds(j * chunk, chunk)], slope.at[:, pl.ds(j * chunk, chunk)]),
            sems.here(act_in.at[:, :, :, :, pl.ds(j * chunk, chunk)], act.at[:, :, :, :, pl.ds(j * chunk, chunk)]),
        ]
        for j in range(n)
    ]
    load_two = [sems.here(low_in, low), sems.here(up_w, up_v), sems.here(second_in, grad_first), sems.here(sums_in, sums)]
    load_three = [
        sems.here(normed_in, normed),
        sems.here(inverse_in, inverse),
        sems.here(vec_in, vec),
        sems.here(out_w, out_v),
        sems.here(lse_in, lse),
        sems.here(x_in, x),
    ]
    load_merged = [sems.here(merged_in, act.at[:, :, :, :, pl.ds(0, wide)])]
    load_heads = [sems.here(heads_in, grad_branch)]
    load_qkv = [sems.here(qkv_w, up_v.at[:, :, :, :, pl.ds(0, wide)])]
    grad_rows = grad_branch
    move_out = rows_to_tokens(p, sems, block_rows, block_out)
    moves = {"outA": [move_out[2]], "outB": [move_out[3]]}
    move_grad = rows_to_tokens(p, sems, grad_rows.reshape(x.shape), input_grad)

    rows = out_v.shape[3]
    grad_qkv = act.at[:, :, :, pl.ds(0, rows), pl.ds(0, wide)]
    down_cols = D // len([name for name, _ in SCATTER if name[0] == "down"])

    def nearby(slot, i):
        row, col = (i // 2) * rows, (i % 2) * 384
        return down_v.at[:, :, :, slot, pl.ds(row, rows), pl.ds(col, 384)]

    def qkv_span(i):
        group, first, end = QKV_PARTS[i]
        return group * 384 + first * 128, (end - first) * 128

    places = {
        "down": lambda g: lambda core: grad_down.at[:, :, :, core, :, pl.ds(g * down_cols, down_cols)],
        "up": lambda g: lambda core: grad_up.at[:, :, :, :, lanes(g * chunk + core * (chunk // 2), chunk // 2)],
        "out": lambda g: lambda core: grad_out.at[:, :, :, :, lanes(core * (D // 2), D // 2)],
        "qkv": lambda g: lambda core: act.at[
            :, :, :, pl.ds(0, rows), lanes(core * (wide // 2) + qkv_span(g)[0], qkv_span(g)[1])
        ],
    }
    nears = {
        "down": lambda g: down_near.at[:, :, :, :, pl.ds(g * down_cols, down_cols)],
        "up": lambda g: nearby(0, g),
        "out": lambda g: nearby(1, 3),
        "qkv": lambda g: nearby(1, QKV_PARTS[g][0]).at[
            :, :, :, :, pl.ds(QKV_PARTS[g][1] * 128, qkv_span(g)[1])
        ],
    }
    items = {}
    for (name, g), order in SCATTER:
        items[name, g] = Scatter(p, sems, places[name](g), nears[name](g), pool[:4], order)
        pool = pool[4:]
    last = []

    def close(key):
        (name, g), final = key, items[key].final
        if name == "down":
            copies = [sems.here(final, down_s.at[:, pl.ds(g * down_cols, down_cols)])]
        else:
            own = rows // 2
            if name == "qkv":
                group, first, end = QKV_PARTS[g]
                parts = [
                    (qkv_s, (s - first) * 128, s * D + (2 * group + p.c) * 128, 128) for s in range(first, end)
                ]
            elif name == "out":
                parts = [(out_s, 0, p.c * (D // 2), D // 2)]
            else:
                parts = [(up_s, 0, g * chunk + p.c * (chunk // 2), chunk // 2)]
            copies = []
            for shard, start, to, size in parts:
                spot = shard.at[:, lanes(to, size)]
                copies.append(sems.here(final.at[pl.ds(p.c * own, own), pl.ds(start, size)], spot))
                copies.append(
                    sems.remote(final.at[pl.ds((1 - p.c) * own, own), pl.ds(start, size)], spot, p.core)
                )
        begin(copies)
        last.extend(copies)

    plan = iter(BACKWARD_PLAN)

    def go():
        for key, stage in next(plan):
            if key in moves:
                begin(moves[key])
            else:
                items[key].advance(stage)
                if stage == 4:
                    close(key)

    begin(load_one)
    for copies in load_chunk:
        begin(copies)
    begin(load_two + load_three + move_out[:2])
    finish(load_one)
    for j in range(n):
        finish(load_chunk[j])
        feed_back_down(j, grad_branch, down_v, act, slope, grad_down, vec_sum)
    pl.semaphore_signal(free, inc=1, device_id=p.core, device_id_type=MESH)
    begin(load_merged + load_heads)
    finish(load_two)
    for j in range(n):
        go()
        if j == 0:
            low_t[...] = low[...].T
        if j == 1:
            pl.semaphore_wait(free, 1)
        feed_back_up(j, low_t, slope, up_v, grad_first, grad_up)
    begin(load_qkv)
    finish(load_three)
    go()
    grad_attn = low
    first_norm_back(grad_first, normed, inverse, vec, grad_attn, vec_sum)
    go()
    finish(load_heads)
    grad_out[...] = dot(grad_branch[...], grad_attn[...], TN).astype(BF16).reshape(grad_out.shape)
    go()
    grad_heads = grad_branch
    for i in range(grad_attn.shape[0] // 512):
        rs = pl.ds(i * 512, 512)
        grad_heads[rs, :] = dot(grad_attn[rs, :], matrix(out_v), NT).astype(BF16)
    x_t = low_t
    x_t[...] = matrix(x).T
    finish(load_merged)
    for g in range(PAIRS // 2):
        for pair in (2 * g, 2 * g + 1):
            go()
            attend_back(act, grad_heads, lengths, p.sq * part, lse, slope, length, pair)
            go()
            project_back(x_t, slope, grad_qkv, vec_sum, pair)
    go()
    vec_sum[0:1, 5 * D + FF :] = jnp.zeros((1, 3 * D), F32)
    for k in range(3):
        vec_sum[0:1, 5 * D + FF + k * D : 5 * D + FF + (k + 1) * D] = sums[k : k + 1, :]
    tiles = vec_sum.shape[1] // (128 * p.ndp)
    for d in range(p.ndp):
        for k in range(tiles):
            vec_parts[d, k : k + 1, :] = vec_sum[0:1, pl.ds((d * tiles + k) * 128, 128)]
        vec_parts[d, tiles:, :] = jnp.zeros((vec_parts.shape[1] - tiles, 128), F32)
    vec_one = [
        sems.remote(vec_parts.at[(p.dp + k) % p.ndp], vec_recv.at[p.dp], ((p.dp + k) % p.ndp, p.sq))
        for k in range(1, p.ndp)
    ]
    begin(vec_one)
    vec_recv[p.dp] = vec_parts[p.dp]
    finish(load_qkv)
    for k in (2, 3, 1, 0):
        to = (p.sq + k) % p.nsq
        for r in range(part):
            rs = pl.ds(pl.multiple_of(r * length + to * (length // p.nsq), 128), length // p.nsq)
            value = dot(slope[rs, pl.ds(0, wide)], columns(up_v, pl.ds(0, wide)), NT)
            grad_rows[rs, :] = (grad_first[rs, :] + value).astype(BF16)
        begin([move_grad[k]])
        go()
    finish(vec_one)
    value = vec_recv[0]
    for k in range(1, p.ndp):
        value = value + vec_recv[k]
    vec_near[p.sq] = value
    near = vec_near.at[p.sq]
    vec_two = [sems.remote(near, near, to) for to in p.group()]
    begin(vec_two)
    go()
    finish(vec_two)
    value = vec_near[0]
    for k in range(1, p.nsq):
        value = value + vec_near[k]
    for k in range(value.shape[0]):
        vec_s[0:1, k * 128 : (k + 1) * 128] = value[k : k + 1, :]

    def squares(value):
        return jnp.sum(jnp.sum(value * value, axis=0, keepdims=True), axis=1, keepdims=True)

    total = squares(value) * (1.0 / p.nsq)
    for item in items.values():
        total = total + squares(item.final[...])
    near_sum[p.sq] = jnp.broadcast_to(total, near_sum.shape[1:])
    near = near_sum.at[p.sq]
    spread = [sems.remote(near, near, to) for to in p.group()]
    begin(spread)
    finish(spread)
    total = near_sum[0]
    for k in range(1, p.nsq):
        total = total + near_sum[k]
    far_sum[p.dp] = total
    far = far_sum.at[p.dp]
    spread = [sems.remote(far, far, to) for to in p.columns()]
    begin(spread)
    finish(spread)
    total = far_sum[0]
    for k in range(1, p.ndp):
        total = total + far_sum[k]
    norm[...] = jnp.sqrt(total)
    finish(last + move_out + move_grad)


def backward(saved, lengths):
    (x, qkv_w, out_w, up_w, down_w, vec, merged, heads, lse, normed, inverse, low, act, slope, block, second,
     grad_branch, sums) = saved
    ndp, nsq = lax.axis_size("dp"), lax.axis_size("seq")
    nz = ndp // 2
    part, full, width = x.shape
    count = part * full
    grid = qkv_w.shape[:3]
    rows, low_rows = qkv_w.shape[3], down_w.shape[4]
    merged = merged.reshape(grid + (count // math.prod(grid), 3 * width))
    act = act.reshape(grid + (count // math.prod(grid), FF))
    block = block.reshape(x.shape)
    token_shape = (part * nsq, full // nsq, width)
    any_space = pl.BlockSpec(memory_space=pl.ANY)
    vmem = pl.BlockSpec(memory_space=pltpu.VMEM)
    vec_tile = (16, 128)
    shapes = [jax.ShapeDtypeStruct(token_shape, BF16)] * 2
    shapes += [jax.ShapeDtypeStruct((rows // 2, w.shape[4]), F32) for w in (qkv_w, out_w, up_w)]
    shapes += [jax.ShapeDtypeStruct((low_rows, width), F32), jax.ShapeDtypeStruct((1, math.prod(vec_tile)), F32)]
    shapes += [jax.ShapeDtypeStruct((8, 128), F32)]

    def like(array):
        return pltpu.VMEM(array.shape, array.dtype)

    scratch = [like(a) for a in (up_w, down_w, out_w, act, slope, grad_branch, second, low)]
    scratch += [pltpu.VMEM((width, count), BF16)]
    scratch += [like(a) for a in (x, normed, inverse, lse, vec, sums, down_w, up_w, out_w, vec)]
    scratch += [pltpu.VMEM((ndp,) + vec_tile, F32)] * 2 + [pltpu.VMEM((nsq,) + vec_tile, F32)]
    scratch += [pltpu.VMEM((nsq, 8, 128), F32), pltpu.VMEM((ndp, 8, 128), F32)]
    scratch += [pltpu.VMEM(grid + (low_rows, width), BF16)]
    down_cols = width // len([name for name, _ in SCATTER if name[0] == "down"])
    for (name, g), order in SCATTER:
        size = (QKV_PARTS[g][2] - QKV_PARTS[g][1]) * 128 if name == "qkv" else 384
        scratch += scatter_buffers((low_rows, down_cols) if name == "down" else (rows, size), nz, order)
    scratch += [pltpu.SemaphoreType.DMA((128,)), pltpu.SemaphoreType.DMA((128,)), pltpu.SemaphoreType.DMA((64,))]
    scratch += [pltpu.SemaphoreType.REGULAR]
    return pl.pallas_call(
        backward_kernel,
        out_shape=shapes,
        in_specs=[any_space] * 18 + [pl.BlockSpec(memory_space=pltpu.SMEM)],
        out_specs=[any_space] * 6 + [vmem, vmem],
        scratch_shapes=scratch,
        compiler_params=pltpu.CompilerParams(
            collective_id=2, has_side_effects=True, vmem_limit_bytes=VMEM_LIMIT
        ),
    )(
        x, qkv_w, out_w, up_w, down_w, vec, merged, heads, lse, normed, inverse, low, act, slope, block, second,
        grad_branch, sums, lengths,
    )


def adam_kernel(norm, *refs):
    ins, done, outs, given, bufs, sems = refs[:16], refs[16:18], refs[18:34], refs[34:36], refs[36:68], refs[70]
    held = refs[68:70]
    factor = CLIP_NORM / jnp.maximum(norm[0:1, 0:1], CLIP_NORM)
    loads = [pltpu.make_async_copy(ref, buf, sems.at[i]) for i, (ref, buf) in enumerate(zip(ins, bufs))]
    stores = [pltpu.make_async_copy(buf, ref, sems.at[16 + i]) for i, (ref, buf) in enumerate(zip(outs, bufs[16:]))]
    fetch = [pltpu.make_async_copy(ref, buf, sems.at[32 + i]) for i, (ref, buf) in enumerate(zip(done, held))]
    give = [pltpu.make_async_copy(buf, ref, sems.at[34 + i]) for i, (ref, buf) in enumerate(zip(given, held))]
    begin(fetch + loads)
    finish(fetch)
    begin(give)
    for k in range(4):
        finish(loads[4 * k : 4 * k + 4])
        master, first, second, shard = (buf[...] for buf in bufs[4 * k : 4 * k + 4])
        for out, value in zip(
            bufs[16 + 4 * k : 20 + 4 * k], adam_step(master, shard, first, second, factor, WEIGHT_DECAY, LEARN_RATE)
        ):
            out[...] = value
        begin(stores[4 * k : 4 * k + 4])
    finish(stores + give)


def adam_matrices(norm, done, masters, firsts, seconds, shards):
    args, shapes = [], []
    for master, first, second, shard in zip(masters, firsts, seconds, shards):
        args += [master, first, second, shard]
        shapes += [jax.ShapeDtypeStruct(master.shape, F32)] * 3 + [jax.ShapeDtypeStruct(master.shape, BF16)]
    any_space = pl.BlockSpec(memory_space=pl.ANY)
    given = [jax.ShapeDtypeStruct(a.shape, a.dtype) for a in done]
    *outs, first, second = pl.pallas_call(
        adam_kernel,
        out_shape=shapes + given,
        in_specs=[pl.BlockSpec(memory_space=pltpu.VMEM)] + [any_space] * 18,
        out_specs=[any_space] * 18,
        scratch_shapes=[pltpu.VMEM(a.shape, a.dtype) for a in args + shapes + given]
        + [pltpu.SemaphoreType.DMA((36,))],
        compiler_params=pltpu.CompilerParams(vmem_limit_bytes=VMEM_LIMIT),
    )(norm, *args, *done)
    return [first, second] + outs


def unpack(vector):
    return (
        vector[:D],
        vector[D : 2 * D],
        vector[2 * D : 3 * D],
        vector[3 * D : 4 * D],
        vector[4 * D : 5 * D],
        vector[5 * D : 5 * D + FF],
        vector[5 * D + FF : 6 * D + FF],
        vector[6 * D + FF : 7 * D + FF],
        vector[7 * D + FF : 8 * D + FF],
    )


def normalize(hidden, gain_vec, shift_vec):
    centre = hidden - jnp.mean(hidden, axis=-1, keepdims=True)
    inverse = lax.rsqrt(jnp.mean(centre * centre, axis=-1, keepdims=True) + NORM_EPS)
    normed = centre * inverse
    return (normed * gain_vec + shift_vec, normed, inverse)


def normalize_back(grad_out, normed, inverse, gain_vec):
    scaled = grad_out * gain_vec
    centred = scaled - jnp.mean(scaled, axis=-1, keepdims=True)
    return inverse * (centred - normed * jnp.mean(scaled * normed, axis=-1, keepdims=True))


def gelu_exact(values):
    return jax.nn.gelu(values, approximate=False)


def split_parts(packed_rows):
    full_len = packed_rows.shape[0]
    group_count = packed_rows.shape[-1] // (3 * HEAD_DIM)
    parts = packed_rows.reshape(full_len, 3, group_count, HEAD_DIM)
    return (parts[:, 0], parts[:, 1], parts[:, 2])


def row_probs(queries, key_rows, key_mask):
    scale = 1.0 / math.sqrt(HEAD_DIM)
    scores = jnp.einsum("qhd,khd->hqk", queries, key_rows, preferred_element_type=F32) * scale
    scores = jnp.where(key_mask[None, None, :], scores, MASK_FILL)
    row_peak = jnp.max(scores, axis=-1, keepdims=True)
    row_exp = jnp.exp(scores - row_peak)
    return row_exp / jnp.sum(row_exp, axis=-1, keepdims=True)


def whole_row(packed):
    packed_rows, key_mask = packed
    queries, key_rows, value_rows = split_parts(packed_rows)
    attn_probs = row_probs(queries, key_rows, key_mask)
    mixed_rows = jnp.einsum("hqk,khd->qhd", attn_probs.astype(BF16), value_rows, preferred_element_type=F32)
    return mixed_rows.astype(BF16).reshape(packed_rows.shape[0], D)


def whole_back(packed):
    packed_rows, grad_rows, key_mask = packed
    full_len = packed_rows.shape[0]
    queries, key_rows, value_rows = split_parts(packed_rows)
    grad_mixed = grad_rows.reshape(full_len, HEADS, HEAD_DIM)
    attn_probs = row_probs(queries, key_rows, key_mask)
    grad_probs = jnp.einsum("qhd,khd->hqk", grad_mixed, value_rows, preferred_element_type=F32)
    row_delta = jnp.sum(attn_probs * grad_probs, axis=-1, keepdims=True)
    grad_scores = (attn_probs * (grad_probs - row_delta)).astype(BF16)
    scale = 1.0 / math.sqrt(HEAD_DIM)
    grad_query = jnp.einsum("hqk,khd->qhd", grad_scores, key_rows, preferred_element_type=F32) * scale
    grad_key = jnp.einsum("hqk,qhd->khd", grad_scores, queries, preferred_element_type=F32) * scale
    grad_value = jnp.einsum("hqk,qhd->khd", attn_probs.astype(BF16), grad_mixed, preferred_element_type=F32)
    stacked = jnp.stack([grad_query, grad_key, grad_value], axis=1).astype(BF16)
    return stacked.reshape(full_len, 3 * D)


def adam_step(master, gradient, moment_one, second, factor, decay_rate, step_rate):
    clipped = gradient * factor
    first_new = BETA_ONE * moment_one + (1.0 - BETA_ONE) * clipped
    second_new = BETA_TWO * second + (1.0 - BETA_TWO) * clipped * clipped
    first_hat = first_new / (1.0 - BETA_ONE**STEP_COUNT)
    second_hat = second_new / (1.0 - BETA_TWO**STEP_COUNT)
    updated = master - step_rate * (first_hat / (jnp.sqrt(second_hat) + ADAM_EPS) + decay_rate * master)
    return (updated, first_new, second_new, updated.astype(BF16))


def layer(rows_in, cot_in, token_weight, lengths, qkv_w, out_w, up_w, down_w, vec_w):
    row_count, full_len, width_d = rows_in.shape
    token_count = row_count * full_len
    bias_q, bias_v, bias_o, gain_one, shift_one, bias_up, bias_down, gain_two, shift_two = unpack(vec_w)
    key_mask = jnp.arange(full_len, dtype=jnp.int32)[None, :] < lengths[:, None]
    flat = rows_in.reshape(token_count, width_d)
    merged = jnp.dot(flat, qkv_w, preferred_element_type=F32)
    merged = (merged + jnp.concatenate([bias_q, jnp.zeros_like(bias_q), bias_v])).astype(BF16)
    merged_rows = merged.reshape(row_count, full_len, 3 * width_d)
    mixed = lax.map(whole_row, (merged_rows, key_mask)).reshape(token_count, width_d)
    attn_out = jnp.dot(mixed, out_w, preferred_element_type=F32) + bias_o
    first_out, normed_one, inverse_one = normalize(flat.astype(F32) + attn_out, gain_one, shift_one)
    first_low = first_out.astype(BF16)
    pre_act = jnp.dot(first_low, up_w, preferred_element_type=F32) + bias_up
    activated, gelu_pull = jax.vjp(gelu_exact, pre_act)
    act_low = activated.astype(BF16)
    branch = jnp.dot(act_low, down_w, preferred_element_type=F32) + bias_down
    result, normed_two, inverse_two = normalize(first_out + branch, gain_two, shift_two)
    block_out = result.astype(BF16).reshape(row_count, full_len, width_d)
    grad_result = cot_in.astype(F32) * (token_weight * key_mask.astype(F32))[:, :, None]
    grad_result = grad_result.reshape(token_count, width_d)
    grad_gain_two = jnp.sum(grad_result * normed_two, axis=0)
    grad_shift_two = jnp.sum(grad_result, axis=0)
    grad_second = normalize_back(grad_result, normed_two, inverse_two, gain_two)
    grad_branch = grad_second.astype(BF16)
    grad_bias_down = jnp.sum(grad_branch, axis=0, dtype=F32)
    grad_down = jnp.einsum("tf,td->fd", act_low, grad_branch, preferred_element_type=F32)
    grad_act = jnp.einsum("td,fd->tf", grad_branch, down_w, preferred_element_type=F32)
    grad_pre = gelu_pull(grad_act)[0].astype(BF16)
    grad_bias_up = jnp.sum(grad_pre, axis=0, dtype=F32)
    grad_up = jnp.einsum("td,tf->df", first_low, grad_pre, preferred_element_type=F32)
    grad_first = grad_second + jnp.einsum("tf,df->td", grad_pre, up_w, preferred_element_type=F32)
    grad_gain_one = jnp.sum(grad_first * normed_one, axis=0)
    grad_shift_one = jnp.sum(grad_first, axis=0)
    grad_resid = normalize_back(grad_first, normed_one, inverse_one, gain_one)
    grad_attn = grad_resid.astype(BF16)
    grad_bias_o = jnp.sum(grad_attn, axis=0, dtype=F32)
    grad_out = jnp.einsum("td,te->de", mixed, grad_attn, preferred_element_type=F32)
    grad_mixed = jnp.einsum("te,de->td", grad_attn, out_w, preferred_element_type=F32).astype(BF16)
    grad_merged = lax.map(
        whole_back, (merged_rows, grad_mixed.reshape(row_count, full_len, width_d), key_mask)
    ).reshape(token_count, 3 * width_d)
    grad_qkv = jnp.einsum("td,te->de", flat, grad_merged, preferred_element_type=F32)
    column_sums = jnp.sum(grad_merged, axis=0, dtype=F32)
    input_grad = grad_resid + jnp.einsum("te,de->td", grad_merged, qkv_w, preferred_element_type=F32)
    input_grad = input_grad.astype(BF16).reshape(row_count, full_len, width_d)
    grad_vec = jnp.concatenate(
        [
            column_sums[:width_d],
            column_sums[2 * width_d :],
            grad_bias_o,
            grad_gain_one,
            grad_shift_one,
            grad_bias_up,
            grad_bias_down,
            grad_gain_two,
            grad_shift_two,
        ]
    )
    low = [g.astype(BF16) for g in (grad_qkv, grad_out, grad_up, grad_down)]
    return block_out, input_grad, *low, grad_vec


def body(
    tokens, cotangent, token_weight, lengths,
    qkv_master, out_master, up_master, down_master, vec_master,
    qkv_first, out_first, up_first, down_first, vec_first,
    qkv_second, out_second, up_second, down_second, vec_second,
):
    ndp, nsq = lax.axis_size("dp"), lax.axis_size("seq")
    devices = ndp * nsq
    row_count, local_len, width_d = tokens.shape
    full_len, part = local_len * nsq, row_count // nsq
    vec_size = vec_master.shape[0]
    sq = lax.axis_index("seq")
    my_lengths = lax.dynamic_slice_in_dim(lengths, sq * part, part)
    both = ("dp", "seq")
    chip = 2 * qkv_master.shape[0]
    own_kernels = (
        qkv_master.shape[0] % 8 == 0
        and down_master.shape[0] % 16 == 0
        and nsq == 4
        and ndp % 2 == 0
        and vec_size * nsq % 128 == 0
        and part * full_len // (ndp * nsq // 2) >= chip
        and local_len == 128
    )
    if own_kernels:
        spread = jnp.zeros((16 * 128,), F32)
        spread = lax.dynamic_update_slice(spread, vec_master, (sq * vec_size,)).reshape(16, 128)
        saved = forward(
            tokens, cotangent, token_weight, qkv_master, out_master, up_master, down_master, spread, lengths
        )
        block_out, input_grad, *shards, vec_s, norm = backward(saved, lengths)
        shards.append(lax.dynamic_slice(vec_s.reshape(-1), (sq * vec_size,), (vec_size,)))
        norm_value = norm[0, 0]
        block_out, input_grad, *matrices = adam_matrices(
            norm,
            (block_out, input_grad),
            (qkv_master, out_master, up_master, down_master),
            (qkv_first, out_first, up_first, down_first),
            (qkv_second, out_second, up_second, down_second),
            shards[:4],
        )
    else:
        rows_in, cot_in = (
            lax.all_to_all(a, "seq", split_axis=0, concat_axis=1, tiled=True) for a in (tokens, cotangent)
        )
        weights = lax.all_gather(token_weight, "seq", axis=0)
        qkv_w, out_w, up_w, down_w, vec_w = (
            lax.all_gather(m.astype(BF16), both, axis=0, tiled=True)
            for m in (qkv_master, out_master, up_master, down_master, vec_master)
        )
        my_weight = lax.dynamic_slice_in_dim(weights, sq * part, part, axis=1)
        my_weight = my_weight.transpose(1, 0, 2).reshape(part, full_len)
        block_rows, grad_rows, *grads, grad_vec = layer(
            rows_in, cot_in, my_weight, my_lengths, qkv_w, out_w, up_w, down_w, vec_w.astype(F32)
        )
        block_out, input_grad = (
            lax.all_to_all(a, "seq", split_axis=1, concat_axis=0, tiled=True) for a in (block_rows, grad_rows)
        )
        shards = [lax.psum_scatter(g.astype(F32), both, scatter_dimension=0, tiled=True) for g in grads]
        shards.append(lax.psum_scatter(grad_vec, both, scatter_dimension=0, tiled=True))
        norm_value = jnp.sqrt(lax.psum(sum(jnp.sum(s * s) for s in shards), both))
    factor = CLIP_NORM / jnp.maximum(norm_value, CLIP_NORM)
    outs = [block_out, input_grad, norm_value]
    if own_kernels:
        outs += matrices
    else:
        for master, shard, first, second in (
            (qkv_master, shards[0], qkv_first, qkv_second),
            (out_master, shards[1], out_first, out_second),
            (up_master, shards[2], up_first, up_second),
            (down_master, shards[3], down_first, down_second),
        ):
            outs += adam_step(master, shard, first, second, factor, WEIGHT_DECAY, LEARN_RATE)
    outs += adam_step(vec_master, shards[4], vec_first, vec_second, factor, 0.0, VEC_RATE)
    return tuple(outs)


def solution(mesh):
    tokens, both, flat = P("dp", "seq", None), P(("dp", "seq"), None), P(("dp", "seq"))
    weights = (both, both, both, both, flat)
    in_specs = (tokens, tokens, P("dp", "seq"), P("dp")) + 3 * weights
    out_specs = (tokens, tokens, P()) + 4 * (both,) * 4 + (flat,) * 4
    return jax.shard_map(body, mesh=mesh, in_specs=in_specs, out_specs=out_specs, check_vma=False)
```
